32 devices in a mesh: series: 1, tm: 16 (over z, y, x), tile: 2 (over core).
Axes of the slice: x: 2, y: 2, z: 4, core: 2. Of those that a mesh axis runs over, the one named last changes fastest.
Arguments:
- frames: bfloat16 [128, 2304, 128], P('tm', ('series', 'tile')), may hold values from 0.001 to 6000, as said below
- block_cycle: int32 [2304], P('series'), may hold values from 0 to 31, as said below
- block_valid: int32 [2304], P('series'), may hold values from 1 to 128, as said below
- cycle_owner: int32 [32], replicated, may hold values from 0 to 31, each once
Outputs:
- two_time: float32 [4096, 128], P(('series', 'tm', 'tile'))
The draws below stay inside these ranges and needn't reach their ends.
Inputs may be any that keep to these rules, and one draw needn't show every extreme that they name: `block_cycle`: each cycle is named by at least one block; in each aligned run of 1152 blocks no cycle is named by more than 71 blocks, and one cycle is named by exactly 71. The first block_valid[b] pixels of block b are valid. `frames`: positive intensities.
All inputs are finite; a program needn't handle non-finite values.
Results may differ from the reference program's by a relative error of at most 0.0003.
Values may be sent and summed in bfloat16 or wider, within the bound.
No kernel may reach another device: no remote copies, remote signals or barrier semaphores. Data moves between devices by JAX's collectives and lax.ppermute only.
A program may use at most 64 MiB of HBM per device.

```python
import math
import jax
import jax.numpy as jnp
from jax import lax

LANES = 128
CYCLE_TOTAL = 32
FRAMES = 128
BLK_DEV = 72
BLOCKS = 2304
HALF = 1152


def cycle_layout(key):
    key_cycle = jax.random.fold_in(key, 11)
    key_perm, key_mix = jax.random.split(key_cycle, 2)
    cycle_rank = jnp.arange(CYCLE_TOTAL + 1, dtype=jnp.int32)
    bounds = HALF - (CYCLE_TOTAL - cycle_rank) ** 2 * HALF // (CYCLE_TOTAL * CYCLE_TOTAL)
    position = jnp.arange(HALF, dtype=jnp.int32)
    rank = jnp.sum((position[:, None] >= bounds[None, 1:CYCLE_TOTAL]).astype(jnp.int32), axis=1)
    cycle_perm = jax.random.permutation(key_perm, CYCLE_TOTAL).astype(jnp.int32)
    pieces = []
    for segment in range(BLOCKS // HALF):
        random_reorder = jax.random.permutation(jax.random.fold_in(key_mix, segment), HALF)
        seg_rank = rank[random_reorder]
        if segment % 2 == 1:
            seg_rank = CYCLE_TOTAL - 1 - seg_rank
        pieces.append(cycle_perm[seg_rank])
    return jnp.concatenate(pieces).astype(jnp.int32)


def valid_layout(key):
    key_valid = jax.random.fold_in(key, 12)
    counts = jax.random.randint(key_valid, (BLOCKS,), 1, LANES + 1).astype(jnp.int32)
    return counts.at[CYCLE_TOTAL].set(LANES).at[CYCLE_TOTAL + 1].set(1)


def draw_block_cycle(key, part):
    return cycle_layout(key)


def draw_block_valid(key, part):
    return valid_layout(key)


def draw_frames(key, part):
    cycle_ids = cycle_layout(key)
    valid_count = valid_layout(key)
    key = jax.random.fold_in(key, 3)
    key_pixel, key_frame, key_signal, key_amp, key_speckle = jax.random.split(key, 5)
    pixel_scale = jnp.exp(jax.random.uniform(key_pixel, (1, BLOCKS, LANES), jnp.float32, 0.0, math.log(20.0)))
    frame_scale = jnp.exp(jax.random.uniform(key_frame, (FRAMES, 1, 1), jnp.float32, math.log(0.5), math.log(2.0)))
    cycle_signal = jnp.clip(jax.random.normal(key_signal, (FRAMES, CYCLE_TOTAL), jnp.float32), -3.0, 3.0)
    block_signal = cycle_signal[:, cycle_ids]
    amplitude = jax.random.uniform(key_amp, (1, BLOCKS, LANES), jnp.float32, -1.0, 1.0)
    speckle = jnp.clip(jax.random.normal(key_speckle, (FRAMES, BLOCKS, LANES), jnp.float32), -4.0, 4.0)
    lane_index = jnp.arange(LANES, dtype=jnp.int32)
    valid_mask = (lane_index[None, :] < valid_count[:, None])[None]
    exponent = jnp.where(valid_mask, amplitude * block_signal[:, :, None] + 0.4 * speckle, 1.2 * speckle)
    return (pixel_scale * frame_scale * jnp.exp(exponent)).astype(jnp.bfloat16)


def setup_inputs(seed: int = 0, part: int = 0) -> dict:
    splits = jax.random.split(jax.random.key(seed), 5)
    own_keys = jax.random.split(jax.random.fold_in(splits[4], part), 5)
    return {
        "frames": draw_frames(jax.random.fold_in(jax.random.fold_in(splits[4], part), 71), part),
        "block_cycle": draw_block_cycle(jax.random.fold_in(jax.random.fold_in(splits[4], part), 71), part),
        "block_valid": draw_block_valid(jax.random.fold_in(jax.random.fold_in(splits[4], part), 71), part),
        "cycle_owner": jax.random.permutation(splits[3], CYCLE_TOTAL).astype(jnp.int32),
    }


def reference(frames, block_cycle, block_valid, cycle_owner):
    member = (block_cycle[None, :] == cycle_owner[:, None]).astype(jnp.float32)
    pixel_total = jnp.dot(member, block_valid.astype(jnp.float32), precision=lax.Precision.HIGHEST)
    lane_index = jnp.arange(LANES, dtype=jnp.int32)
    group_count = BLOCKS // BLK_DEV

    def step(carry, group):
        gram_total, frame_total = carry
        offset = (group * BLK_DEV).astype(jnp.int32)
        block_data = lax.dynamic_slice_in_dim(frames, offset, BLK_DEV, 1).astype(jnp.float32)
        block_count = lax.dynamic_slice_in_dim(block_valid, offset, BLK_DEV, 0)
        members = lax.dynamic_slice_in_dim(member, offset, BLK_DEV, 1)
        pixel_mean = jnp.sum(block_data, axis=0) / FRAMES
        valid_mask = lane_index[None, :] < block_count[:, None]
        normalized_frames = jnp.where(valid_mask[None], block_data / pixel_mean[None], jnp.float32(0.0))
        gram_matrices = jnp.einsum("rnk,jnk->nrj", normalized_frames, normalized_frames, precision=lax.Precision.HIGHEST)
        gram_total = gram_total + jnp.dot(members, gram_matrices.reshape(BLK_DEV, FRAMES * FRAMES), precision=lax.Precision.HIGHEST)
        frame_total = frame_total + jnp.dot(members, jnp.sum(normalized_frames, axis=2).T, precision=lax.Precision.HIGHEST)
        return (gram_total, frame_total), None

    start_carry = (jnp.zeros((CYCLE_TOTAL, FRAMES * FRAMES), jnp.float32), jnp.zeros((CYCLE_TOTAL, FRAMES), jnp.float32))
    (gram_total, frame_total), _ = lax.scan(step, start_carry, jnp.arange(group_count, dtype=jnp.int32))
    gram_total = gram_total.reshape(CYCLE_TOTAL, FRAMES, FRAMES)
    two_time = (pixel_total[:, None, None] * gram_total) / (frame_total[:, :, None] * frame_total[:, None, :])
    return two_time.reshape(CYCLE_TOTAL * FRAMES, FRAMES)
```

```python
import functools

import jax
import jax.numpy as jnp
from jax import lax
from jax.experimental import pallas as pl
from jax.experimental.pallas import tpu as pltpu
from jax.sharding import PartitionSpec as P

LANE = 128
UNROLL = 8
VMEM_LIMIT = 48 * 1024 * 1024
LADDER = (16, 24, 32, 36, 40, 42, 44, 46, 48, 52, 56, 64, 80, 104, 144)
NT = (((1,), (1,)), ((), ()))


def plan_kernel(where_ref, cycle_ref, valid_ref, owner_ref, block_ref, start_ref, scalar_ref):
    tm_index, tile_index = where_ref[0], where_ref[1]
    block_count = cycle_ref.shape[1]
    chunks = block_count // LANE
    slots = owner_ref.shape[0]
    list_rows = block_ref.shape[0]
    owner = owner_ref[...]
    slot = lax.broadcasted_iota(jnp.int32, (slots, LANE), 0)
    mine = (slot % 2 == tile_index).astype(jnp.float32)

    member, weighted = [], []
    for k in range(chunks):
        cut = slice(k * LANE, (k + 1) * LANE)
        hit = (cycle_ref[:, cut] == owner).astype(jnp.float32)
        member.append(hit)
        weighted.append(hit * valid_ref[:, cut].astype(jnp.float32))
    stacked = jnp.concatenate(member + weighted, axis=0).astype(jnp.bfloat16)
    before = lax.broadcasted_iota(jnp.int32, (LANE, 2 * LANE), 0)
    column = lax.broadcasted_iota(jnp.int32, (LANE, 2 * LANE), 1)
    prefix = ((before < column) | (column >= LANE)).astype(jnp.float32).astype(jnp.bfloat16)
    sums = jnp.dot(stacked, prefix, preferred_element_type=jnp.float32)

    count = jnp.zeros((slots, LANE), jnp.float32)
    pixels = jnp.zeros((slots, LANE), jnp.float32)
    rank, start = [], []
    for k in range(chunks):
        low = slice(k * slots, (k + 1) * slots)
        high = slice((chunks + k) * slots, (chunks + k + 1) * slots)
        rank.append(count + sums[low, :LANE])
        start.append(jnp.sum(member[k] * (pixels + sums[high, :LANE]), axis=0, keepdims=True))
        count = count + sums[low, LANE:]
        pixels = pixels + sums[high, LANE:]

    row = lax.broadcasted_iota(jnp.int32, (slots, slots), 0)
    col = lax.broadcasted_iota(jnp.int32, (slots, slots), 1)
    earlier = ((col < row) & (col % 2 == tile_index)).astype(jnp.float32)
    base = jnp.dot(
        earlier, count, precision=lax.Precision.HIGHEST, preferred_element_type=jnp.float32
    )

    list_row = lax.broadcasted_iota(jnp.int32, (list_rows, LANE), 0)
    list_col = lax.broadcasted_iota(jnp.int32, (LANE, LANE), 0)
    lane = lax.broadcasted_iota(jnp.int32, (1, LANE), 1)
    half_slot = (slot // 2).astype(jnp.float32)
    lists = jnp.zeros((4 * list_rows, LANE), jnp.float32)
    for k in range(chunks):
        own = member[k] * mine
        place = jnp.sum(own * (rank[k] + base), axis=0, keepdims=True).astype(jnp.int32)
        target = jnp.sum(own * half_slot, axis=0, keepdims=True).astype(jnp.int32)
        used = jnp.sum(own, axis=0, keepdims=True) > 0
        begin = start[k].astype(jnp.int32)
        block = k * LANE + lane
        at_row = list_row == jnp.where(used, place // LANE, -1)
        at_col = (list_col == place % LANE).astype(jnp.float32).astype(jnp.bfloat16)
        parts = (block % 256, block // 256 + 16 * target, begin % 256, begin // 256)
        spread = jnp.concatenate(
            [jnp.where(at_row, part.astype(jnp.float32), 0.0) for part in parts], axis=0
        ).astype(jnp.bfloat16)
        lists = lists + lax.dot_general(spread, at_col, NT, preferred_element_type=jnp.float32)
    lists = lists.astype(jnp.int32)
    block_ref[...] = lists[:list_rows] + 256 * lists[list_rows : 2 * list_rows]
    start_ref[...] = lists[2 * list_rows : 3 * list_rows] + 256 * lists[3 * list_rows :]

    most = jnp.max(pixels).astype(jnp.int32)
    rows = (most + LANE - 1) // LANE
    rung = jnp.int32(0)
    for size in LADDER[:-1]:
        rung = rung + (rows > size).astype(jnp.int32)
    own_slot = 2 * tm_index + tile_index
    scalar_ref[0] = rung
    scalar_ref[1] = jnp.sum(count[:, :1] * mine[:, :1]).astype(jnp.int32)
    scalar_ref[2] = jnp.sum(jnp.where(slot == own_slot, pixels, 0.0)[:, :1]).astype(jnp.int32)
    scalar_ref[3] = tile_index


def pack_kernel(size, block_ref, start_ref, scalar_ref, near_ref, far_ref, out_ref, pool, stage):
    frames, half, _ = near_ref.shape
    near_at = scalar_ref[3] * half
    far_at = half - near_at
    step = 64
    for source, at in ((near_ref, near_at), (far_ref, far_at)):
        for f in range(frames):

            def widen(i, _, source=source, at=at, f=f):
                begin = pl.multiple_of(i * step, step)
                to = pl.multiple_of(f * 2 * half + at + begin, 8)
                pool[pl.ds(to, step), :] = source[f, pl.ds(begin, step), :].astype(jnp.float32)
                return 0

            lax.fori_loop(0, half // step, widen, 0)

    lane = lax.broadcasted_iota(jnp.int32, (frames, LANE), 1)

    def place(i, carry):
        held, spill, last = carry
        word = block_ref[i]
        begin = start_ref[i]
        block = word & 4095
        row = (word >> 12) * size + (begin >> 7)
        shift = begin & (LANE - 1)
        x = pool[pl.ds(block, frames, stride=2 * half), :]
        turned = pltpu.roll(x, shift, 1)
        held = jnp.where(lane >= shift, turned, jnp.where(row == last, held, spill))
        at = pl.multiple_of(row * frames, frames)
        stage[pl.ds(at, frames), :] = held
        stage[pl.ds(at + frames, frames), :] = turned
        return held, turned, row

    def group(j, carry):
        for i in range(UNROLL):
            carry = place(j * UNROLL + i, carry)
        return carry

    total = scalar_ref[1]
    zero = jnp.zeros((frames, LANE), jnp.float32)
    carry = lax.fori_loop(0, total // UNROLL, group, (zero, zero, jnp.int32(-1)))
    lax.fori_loop(total // UNROLL * UNROLL, total, place, carry)

    depth = size * frames
    for d in range(out_ref.shape[0]):
        out_ref[d] = stage[d * depth : (d + 1) * depth, :].astype(jnp.bfloat16)


def gram_kernel(scalar_ref, x_ref, out_ref):
    sources = x_ref.shape[0]
    frames = out_ref.shape[0]
    local = frames // sources
    pixels = scalar_ref[2]
    lane = lax.broadcasted_iota(jnp.int32, (1, LANE), 1)

    def pair(j, carry):
        gram, total = carry
        both = x_ref[:, pl.ds(pl.multiple_of(j * 2 * local, 2 * local), 2 * local), :]
        both = both.astype(jnp.float32).reshape(sources, 2, local, LANE)
        exact, high, low = [], [], []
        for i in range(2):
            used = lane + (2 * j + i) * LANE < pixels
            x = jnp.where(used, both[:, i].reshape(frames, LANE), 0.0)
            mean = jnp.where(used, jnp.sum(x, axis=0, keepdims=True) / frames, 1.0)
            scale = 1.0 / mean
            total = total + x * scale
            y = x * (scale * scale)
            top = y.astype(jnp.bfloat16)
            exact.append(x.astype(jnp.bfloat16))
            high.append(top)
            low.append((y - top.astype(jnp.float32)).astype(jnp.bfloat16))
        left = jnp.concatenate(exact, axis=1)
        right = jnp.concatenate(
            [jnp.concatenate(high, axis=1), jnp.concatenate(low, axis=1)], axis=0
        )
        gram = gram + lax.dot_general(left, right, NT, preferred_element_type=jnp.float32)
        return gram, total

    start = (jnp.zeros((frames, 2 * frames), jnp.float32), jnp.zeros((frames, LANE), jnp.float32))
    gram, total = lax.fori_loop(0, (pixels + 2 * LANE - 1) // (2 * LANE), pair, start)
    gram = gram[:, :frames] + gram[:, frames:]
    first = jnp.sum(total, axis=1, keepdims=True)
    second = jnp.sum(total.T, axis=0, keepdims=True)
    out_ref[...] = pixels.astype(jnp.float32) * gram / (first * second)


def on_device_routed(frames, block_cycle, block_valid, cycle_owner):
    tm_count = lax.axis_size("tm")
    local_frames, half, _ = frames.shape
    block_count = block_cycle.shape[0]
    slots = cycle_owner.shape[0]
    list_rows = -(-block_count // (8 * LANE)) * 8
    vmem = pl.BlockSpec(memory_space=pltpu.VMEM)
    smem = pl.BlockSpec(memory_space=pltpu.SMEM)
    params = pltpu.CompilerParams(vmem_limit_bytes=VMEM_LIMIT)

    far = lax.ppermute(frames, "tile", [(0, 1), (1, 0)])
    where = jnp.stack([lax.axis_index("tm"), lax.axis_index("tile")]).astype(jnp.int32)
    block_list, start_list, scalars = pl.pallas_call(
        plan_kernel,
        out_shape=(
            jax.ShapeDtypeStruct((list_rows, LANE), jnp.int32),
            jax.ShapeDtypeStruct((list_rows, LANE), jnp.int32),
            jax.ShapeDtypeStruct((4,), jnp.int32),
        ),
        in_specs=[smem, vmem, vmem, vmem],
        out_specs=(vmem, vmem, smem),
        compiler_params=params,
        name="plan",
    )(where, block_cycle[None, :], block_valid[None, :], cycle_owner[:, None])
    block_list = block_list.reshape(-1)
    start_list = start_list.reshape(-1)

    def branch(size):
        def run(block_list, start_list, scalars, near, far):
            send = pl.pallas_call(
                functools.partial(pack_kernel, size),
                out_shape=jax.ShapeDtypeStruct(
                    (tm_count, size * local_frames, LANE), jnp.bfloat16
                ),
                in_specs=[smem, smem, smem, vmem, vmem],
                out_specs=vmem,
                scratch_shapes=[
                    pltpu.VMEM((local_frames * 2 * half, LANE), jnp.float32),
                    pltpu.VMEM(((tm_count * size + 1) * local_frames, LANE), jnp.float32),
                ],
                compiler_params=params,
                name="pack",
            )(block_list, start_list, scalars, near, far)
            got = lax.all_to_all(send, "tm", split_axis=0, concat_axis=0, tiled=True)
            return pl.pallas_call(
                gram_kernel,
                out_shape=jax.ShapeDtypeStruct(
                    (tm_count * local_frames, tm_count * local_frames), jnp.float32
                ),
                in_specs=[smem, vmem],
                out_specs=vmem,
                compiler_params=params,
                name="gram",
            )(scalars, got)

        return run

    return lax.switch(
        scalars[0], [branch(size) for size in LADDER], block_list, start_list, scalars, frames, far
    )


def normalize(pixel_intensity, valid_count, lanes):
    lane_index = jnp.arange(lanes, dtype=jnp.int32)
    valid_mask = lane_index[None, :] < valid_count[:, None]
    pixel_mean = jnp.sum(pixel_intensity, axis=0) / pixel_intensity.shape[0]
    guarded_average = jnp.where(valid_mask, pixel_mean, jnp.float32(1.0))
    return jnp.where(valid_mask[None], pixel_intensity / guarded_average[None], jnp.float32(0.0))


def on_device_summed(frames, block_cycle, block_valid, cycle_owner):
    tm_count = lax.axis_size("tm")
    tile_count = lax.axis_size("tile")
    tm_index = lax.axis_index("tm")
    tile_index = lax.axis_index("tile")
    local_frames = frames.shape[0]
    half = frames.shape[1]
    lanes = frames.shape[2]
    cycle_count = cycle_owner.shape[0]
    frame_count = local_frames * tm_count
    cycle_range = jnp.arange(cycle_count, dtype=jnp.int32)
    member_all = (block_cycle[None, :] == cycle_owner[:, None]).astype(jnp.float32)
    pixel_total = jnp.dot(
        member_all, block_valid.astype(jnp.float32), precision=lax.Precision.HIGHEST
    )
    row_count = cycle_count * frame_count // (tm_count * tile_count)
    block_local = half // tm_count
    reshaped = frames.reshape(local_frames, tm_count, block_local, lanes)
    arrived = lax.all_to_all(reshaped, "tm", split_axis=1, concat_axis=0, tiled=True)
    pixel_intensity = arrived.reshape(frame_count, block_local, lanes).astype(jnp.float32)
    offset = (tile_index * tm_count + tm_index) * block_local
    cycle_ids = lax.dynamic_slice_in_dim(block_cycle, offset, block_local, 0)
    valid_count = lax.dynamic_slice_in_dim(block_valid, offset, block_local, 0)
    members = (cycle_ids[None, :] == cycle_owner[:, None]).astype(jnp.float32)
    normalized_frames = normalize(pixel_intensity, valid_count, lanes)
    gram_matrices = jnp.einsum(
        "rnk,jnk->nrj", normalized_frames, normalized_frames, precision=lax.Precision.HIGHEST
    )
    partial_value = jnp.dot(
        members,
        gram_matrices.reshape(block_local, frame_count * frame_count),
        precision=lax.Precision.HIGHEST,
    )
    partial_value = partial_value.reshape(cycle_count * frame_count, frame_count)
    frame_sums = jnp.dot(
        members, jnp.sum(normalized_frames, axis=2).T, precision=lax.Precision.HIGHEST
    )
    owned = lax.psum_scatter(partial_value, ("tm", "tile"), scatter_dimension=0, tiled=True)
    frame_total = lax.psum(frame_sums, ("tm", "tile"))
    row_start = (tm_index * tile_count + tile_index) * row_count
    row_global = row_start + jnp.arange(row_count, dtype=jnp.int32)
    slot_index = row_global // frame_count
    frame_time_index = row_global % frame_count
    select = (slot_index[:, None] == cycle_range[None, :]).astype(jnp.float32)
    row_sums = jnp.dot(select, frame_total, precision=lax.Precision.HIGHEST)
    row_pixels = jnp.dot(select, pixel_total, precision=lax.Precision.HIGHEST)
    time_pick = (
        jnp.arange(frame_count, dtype=jnp.int32)[None, :] == frame_time_index[:, None]
    ).astype(jnp.float32)
    first_sums = jnp.sum(row_sums * time_pick, axis=1)
    return row_pixels[:, None] * owned / (first_sums[:, None] * row_sums)


def solution(mesh):
    in_specs = (P("tm", ("series", "tile"), None), P("series"), P("series"), P())
    out_specs = P(("series", "tm", "tile"), None)

    def on_device(frames, block_cycle, block_valid, cycle_owner):
        routed = (
            mesh.shape["tile"] == 2
            and mesh.shape["tm"] * 2 == cycle_owner.shape[0]
            and frames.shape[0] == 8
            and mesh.shape["tm"] * 8 == LANE
            and block_cycle.shape[0] <= 4096
        )
        body = on_device_routed if routed else on_device_summed
        return body(frames, block_cycle, block_valid, cycle_owner)

    return jax.shard_map(
        on_device, mesh=mesh, in_specs=in_specs, out_specs=out_specs, check_vma=False
    )
```

```python
import functools

import jax
import jax.numpy as jnp
from jax import lax
from jax.experimental import pallas as pl
from jax.experimental.pallas import tpu as pltpu
from jax.sharding import PartitionSpec as P

LANE = 128
UNROLL = 8
STEP = 192
VMEM_LIMIT = 48 * 1024 * 1024
LADDER = (16, 24, 32, 36, 40, 42, 44, 46, 48, 52, 56, 64, 80, 104, 144)
NT = (((1,), (1,)), ((), ()))


def plan_kernel(where_ref, owner_ref, cycle_ref, valid_ref, word_ref, scalar_ref):
    tm_index, tile_index = where_ref[0], where_ref[1]
    chunks = cycle_ref.shape[0] // LANE
    slots = owner_ref.shape[0]
    list_rows = word_ref.shape[0]
    slot = lax.broadcasted_iota(jnp.int32, (slots, LANE), 0)
    mine = (slot % 2 == tile_index).astype(jnp.float32)
    owner = jnp.zeros((slots, LANE), jnp.int32)
    for s in range(slots):
        owner = jnp.where(slot == s, owner_ref[s], owner)

    member, weighted = [], []
    for k in range(chunks):
        cut = slice(k * LANE, (k + 1) * LANE)
        hit = (cycle_ref[cut].reshape(1, LANE) == owner).astype(jnp.float32)
        member.append(hit)
        weighted.append(hit * valid_ref[cut].reshape(1, LANE).astype(jnp.float32))
    stacked = jnp.concatenate(member + weighted, axis=0).astype(jnp.bfloat16)
    before = lax.broadcasted_iota(jnp.int32, (LANE, 2 * LANE), 0)
    column = lax.broadcasted_iota(jnp.int32, (LANE, 2 * LANE), 1)
    prefix = ((before < column) | (column >= LANE)).astype(jnp.float32).astype(jnp.bfloat16)
    sums = jnp.dot(stacked, prefix, preferred_element_type=jnp.float32)

    count = jnp.zeros((slots, LANE), jnp.float32)
    pixels = jnp.zeros((slots, LANE), jnp.float32)
    rank, start = [], []
    for k in range(chunks):
        low = slice(k * slots, (k + 1) * slots)
        high = slice((chunks + k) * slots, (chunks + k + 1) * slots)
        rank.append(count + sums[low, :LANE])
        start.append(pixels + sums[high, :LANE])
        count = count + sums[low, LANE:]
        pixels = pixels + sums[high, LANE:]

    rows = (jnp.max(pixels).astype(jnp.int32) + LANE - 1) // LANE
    rung = jnp.int32(0)
    size = jnp.int32(LADDER[0])
    for smaller, larger in zip(LADDER[:-1], LADDER[1:]):
        rung = rung + (rows > smaller).astype(jnp.int32)
        size = jnp.where(rows > smaller, larger, size)

    last = slots // 2 - 1
    order = (slot // 2) ^ tm_index ^ last
    row = lax.broadcasted_iota(jnp.int32, (slots, slots), 0) // 2
    col = lax.broadcasted_iota(jnp.int32, (slots, slots), 1)
    earlier = ((col // 2) ^ tm_index ^ last) < (row ^ tm_index ^ last)
    earlier = (earlier & (col % 2 == tile_index)).astype(jnp.float32)
    base = jnp.dot(
        earlier, count, precision=lax.Precision.HIGHEST, preferred_element_type=jnp.float32
    )
    begin = (order * size * LANE).astype(jnp.float32)

    list_row = lax.broadcasted_iota(jnp.int32, (list_rows, LANE), 0)
    list_col = lax.broadcasted_iota(jnp.int32, (LANE, LANE), 0)
    lane = lax.broadcasted_iota(jnp.int32, (1, LANE), 1)
    lists = jnp.zeros((4 * list_rows, LANE), jnp.float32)
    for k in range(chunks):
        own = member[k] * mine
        place = jnp.sum(own * (rank[k] + base), axis=0, keepdims=True).astype(jnp.int32)
        at = jnp.sum(own * (start[k] + begin), axis=0, keepdims=True).astype(jnp.int32)
        used = jnp.sum(own, axis=0, keepdims=True) > 0
        word = at * 4096 + (k * LANE + lane)
        at_row = list_row == jnp.where(used, place // LANE, -1)
        at_col = (list_col == place % LANE).astype(jnp.float32).astype(jnp.bfloat16)
        spread = jnp.concatenate(
            [
                jnp.where(at_row, ((word >> (8 * part)) & 255).astype(jnp.float32), 0.0)
                for part in range(4)
            ],
            axis=0,
        ).astype(jnp.bfloat16)
        lists = lists + lax.dot_general(spread, at_col, NT, preferred_element_type=jnp.float32)
    lists = lists.astype(jnp.int32)
    words = jnp.zeros((list_rows, LANE), jnp.int32)
    for part in range(4):
        words = words + (lists[part * list_rows : (part + 1) * list_rows] << (8 * part))
    word_ref[...] = words

    own_slot = 2 * tm_index + tile_index
    scalar_ref[0] = rung
    scalar_ref[1] = jnp.sum(count[:, :1] * mine[:, :1]).astype(jnp.int32)
    scalar_ref[2] = jnp.sum(jnp.where(slot == own_slot, pixels, 0.0)[:, :1]).astype(jnp.int32)
    scalar_ref[3] = tile_index
    scalar_ref[4] = tm_index


def pack_kernel(word_ref, scalar_ref, near_ref, far_ref, *rest):
    out_refs, (pool, stage) = rest[:-2], rest[-2:]
    frames, half, _ = near_ref.shape
    stride = 2 * half + 1
    near_at = scalar_ref[3] * half
    far_at = half - near_at
    for source, at in ((near_ref, near_at), (far_ref, far_at)):
        for f in range(frames):

            def widen(i, _, source=source, at=at, f=f):
                begin = pl.multiple_of(i * STEP, STEP)
                to = f * stride + pl.multiple_of(at + begin, 8)
                pool[pl.ds(to, STEP), :] = source[f, pl.ds(begin, STEP), :].astype(jnp.float32)
                return 0

            lax.fori_loop(0, half // STEP, widen, 0)

    lane = lax.broadcasted_iota(jnp.int32, (frames, LANE), 1)

    def place(i, carry):
        held, spill, last = carry
        word = word_ref[i]
        block = word & 4095
        row = word >> 19
        shift = (word >> 12) & (LANE - 1)
        x = pool[pl.ds(block, frames, stride=stride), :]
        turned = pltpu.roll(x, shift, 1)
        held = jnp.where(lane >= shift, turned, jnp.where(row == last, held, spill))
        at = pl.multiple_of(row * frames, frames)
        stage[pl.ds(at, frames), :] = held
        stage[pl.ds(at + frames, frames), :] = turned
        return held, turned, row

    def group(j, carry):
        for i in range(UNROLL):
            carry = place(j * UNROLL + i, carry)
        return carry

    total = scalar_ref[1]
    zero = jnp.zeros((frames, LANE), jnp.float32)
    carry = lax.fori_loop(0, total // UNROLL, group, (zero, zero, jnp.int32(-1)))
    lax.fori_loop(total // UNROLL * UNROLL, total, place, carry)

    depth = out_refs[0].shape[0]
    for d, out_ref in enumerate(out_refs):
        out_ref[...] = stage[d * depth : (d + 1) * depth, :].astype(jnp.bfloat16)


def gram_kernel(scalar_ref, *refs):
    x_refs, (out_ref, turn) = refs[:-2], refs[-2:]
    sources = len(x_refs)
    frames = out_ref.shape[0]
    local = frames // sources
    pixels = scalar_ref[2]
    tm_index = scalar_ref[4]
    lane = lax.broadcasted_iota(jnp.int32, (1, LANE), 1)

    def pair(j, carry):
        gram, total = carry
        rows = pl.ds(pl.multiple_of(j * 2 * local, 2 * local), 2 * local)
        both = [ref[rows, :].astype(jnp.float32) for ref in x_refs]
        exact, high, low = [], [], []
        for i in range(2):
            used = lane + (2 * j + i) * LANE < pixels
            x = jnp.concatenate([part[i * local : (i + 1) * local] for part in both], axis=0)
            x = jnp.where(used, x, 0.0)
            mean = jnp.where(used, jnp.sum(x, axis=0, keepdims=True) / frames, 1.0)
            scale = 1.0 / mean
            total = total + x * scale
            y = x * (scale * scale)
            top = y.astype(jnp.bfloat16)
            exact.append(x.astype(jnp.bfloat16))
            high.append(top)
            low.append((y - top.astype(jnp.float32)).astype(jnp.bfloat16))
        left = jnp.concatenate(exact, axis=1)
        right = jnp.concatenate(
            [jnp.concatenate(high, axis=1), jnp.concatenate(low, axis=1)], axis=0
        )
        gram = gram + lax.dot_general(left, right, NT, preferred_element_type=jnp.float32)
        return gram, total

    def two_pairs(j, carry):
        return pair(2 * j + 1, pair(2 * j, carry))

    def in_order(value):
        for j in range(sources):
            at = pl.multiple_of((tm_index ^ (sources - 1 - j)) * local, local)
            turn[pl.ds(at, local), :] = value[j * local : (j + 1) * local]
        return turn[...]

    carry = (jnp.zeros((frames, 2 * frames), jnp.float32), jnp.zeros((frames, LANE), jnp.float32))
    pairs = (pixels + 2 * LANE - 1) // (2 * LANE)
    carry = lax.fori_loop(0, pairs // 2, two_pairs, carry)
    gram, total = lax.fori_loop(pairs // 2 * 2, pairs, pair, carry)
    gram = in_order(gram[:, :frames] + gram[:, frames:])
    gram = in_order(gram.T)
    total = in_order(total)
    first = jnp.sum(total, axis=1, keepdims=True)
    second = jnp.sum(total.T, axis=0, keepdims=True)
    out_ref[...] = pixels.astype(jnp.float32) * gram / (first * second)


def on_device_routed(frames, block_cycle, block_valid, cycle_owner):
    tm_count = lax.axis_size("tm")
    local_frames, half, _ = frames.shape
    list_rows = -(-block_cycle.shape[0] // (8 * LANE)) * 8
    vmem = pl.BlockSpec(memory_space=pltpu.VMEM)
    smem = pl.BlockSpec(memory_space=pltpu.SMEM)
    params = pltpu.CompilerParams(vmem_limit_bytes=VMEM_LIMIT)

    far = lax.ppermute(frames, "tile", [(0, 1), (1, 0)])
    where = jnp.stack([lax.axis_index("tm"), lax.axis_index("tile")]).astype(jnp.int32)
    words, scalars = pl.pallas_call(
        plan_kernel,
        out_shape=(
            jax.ShapeDtypeStruct((list_rows, LANE), jnp.int32),
            jax.ShapeDtypeStruct((5,), jnp.int32),
        ),
        in_specs=[smem, smem, vmem, vmem],
        out_specs=(vmem, smem),
        compiler_params=params,
        name="plan",
    )(where, cycle_owner, block_cycle, block_valid)
    words = words.reshape(-1)

    def branch(size):
        depth = size * local_frames

        def run(words, scalars, near, far):
            send = pl.pallas_call(
                pack_kernel,
                out_shape=(jax.ShapeDtypeStruct((depth, LANE), jnp.bfloat16),) * tm_count,
                in_specs=[smem, smem, vmem, vmem],
                out_specs=(vmem,) * tm_count,
                scratch_shapes=[
                    pltpu.VMEM((local_frames * (2 * half + 1) + 8, LANE), jnp.float32),
                    pltpu.VMEM((tm_count * depth + local_frames, LANE), jnp.float32),
                ],
                compiler_params=params,
                name="pack",
            )(words, scalars, near, far)
            got = []
            for j in range(tm_count):
                apart = tm_count - 1 - j
                pairs = [(i, i ^ apart) for i in range(tm_count)]
                got.append(lax.ppermute(send[j], "tm", pairs) if apart else send[j])
            return pl.pallas_call(
                gram_kernel,
                out_shape=jax.ShapeDtypeStruct(
                    (tm_count * local_frames, tm_count * local_frames), jnp.float32
                ),
                in_specs=[smem] + [vmem] * tm_count,
                out_specs=vmem,
                scratch_shapes=[pltpu.VMEM((tm_count * local_frames, LANE), jnp.float32)],
                compiler_params=params,
                name="gram",
            )(scalars, *got)

        return run

    return lax.switch(
        scalars[0], [branch(size) for size in LADDER], words, scalars, frames, far
    )


def normalize(pixel_intensity, valid_count, lanes):
    lane_index = jnp.arange(lanes, dtype=jnp.int32)
    valid_mask = lane_index[None, :] < valid_count[:, None]
    pixel_mean = jnp.sum(pixel_intensity, axis=0) / pixel_intensity.shape[0]
    guarded_average = jnp.where(valid_mask, pixel_mean, jnp.float32(1.0))
    return jnp.where(valid_mask[None], pixel_intensity / guarded_average[None], jnp.float32(0.0))


def on_device_summed(frames, block_cycle, block_valid, cycle_owner):
    tm_count = lax.axis_size("tm")
    tile_count = lax.axis_size("tile")
    tm_index = lax.axis_index("tm")
    tile_index = lax.axis_index("tile")
    local_frames = frames.shape[0]
    half = frames.shape[1]
    lanes = frames.shape[2]
    cycle_count = cycle_owner.shape[0]
    frame_count = local_frames * tm_count
    cycle_range = jnp.arange(cycle_count, dtype=jnp.int32)
    member_all = (block_cycle[None, :] == cycle_owner[:, None]).astype(jnp.float32)
    pixel_total = jnp.dot(
        member_all, block_valid.astype(jnp.float32), precision=lax.Precision.HIGHEST
    )
    row_count = cycle_count * frame_count // (tm_count * tile_count)
    block_local = half // tm_count
    reshaped = frames.reshape(local_frames, tm_count, block_local, lanes)
    arrived = lax.all_to_all(reshaped, "tm", split_axis=1, concat_axis=0, tiled=True)
    pixel_intensity = arrived.reshape(frame_count, block_local, lanes).astype(jnp.float32)
    offset = (tile_index * tm_count + tm_index) * block_local
    cycle_ids = lax.dynamic_slice_in_dim(block_cycle, offset, block_local, 0)
    valid_count = lax.dynamic_slice_in_dim(block_valid, offset, block_local, 0)
    members = (cycle_ids[None, :] == cycle_owner[:, None]).astype(jnp.float32)
    normalized_frames = normalize(pixel_intensity, valid_count, lanes)
    gram_matrices = jnp.einsum(
        "rnk,jnk->nrj", normalized_frames, normalized_frames, precision=lax.Precision.HIGHEST
    )
    partial_value = jnp.dot(
        members,
        gram_matrices.reshape(block_local, frame_count * frame_count),
        precision=lax.Precision.HIGHEST,
    )
    partial_value = partial_value.reshape(cycle_count * frame_count, frame_count)
    frame_sums = jnp.dot(
        members, jnp.sum(normalized_frames, axis=2).T, precision=lax.Precision.HIGHEST
    )
    owned = lax.psum_scatter(partial_value, ("tm", "tile"), scatter_dimension=0, tiled=True)
    frame_total = lax.psum(frame_sums, ("tm", "tile"))
    row_start = (tm_index * tile_count + tile_index) * row_count
    row_global = row_start + jnp.arange(row_count, dtype=jnp.int32)
    slot_index = row_global // frame_count
    frame_time_index = row_global % frame_count
    select = (slot_index[:, None] == cycle_range[None, :]).astype(jnp.float32)
    row_sums = jnp.dot(select, frame_total, precision=lax.Precision.HIGHEST)
    row_pixels = jnp.dot(select, pixel_total, precision=lax.Precision.HIGHEST)
    time_pick = (
        jnp.arange(frame_count, dtype=jnp.int32)[None, :] == frame_time_index[:, None]
    ).astype(jnp.float32)
    first_sums = jnp.sum(row_sums * time_pick, axis=1)
    return row_pixels[:, None] * owned / (first_sums[:, None] * row_sums)


def solution(mesh):
    in_specs = (P("tm", ("series", "tile"), None), P("series"), P("series"), P())
    out_specs = P(("series", "tm", "tile"), None)

    def on_device(frames, block_cycle, block_valid, cycle_owner):
        routed = (
            mesh.shape["tile"] == 2
            and mesh.shape["tm"] * 2 == cycle_owner.shape[0]
            and frames.shape[0] == 8
            and mesh.shape["tm"] * 8 == LANE
            and block_cycle.shape[0] <= 4096
        )
        body = on_device_routed if routed else on_device_summed
        return body(frames, block_cycle, block_valid, cycle_owner)

    return jax.shard_map(
        on_device, mesh=mesh, in_specs=in_specs, out_specs=out_specs, check_vma=False
    )
```

```python
import functools

import jax
import jax.numpy as jnp
from jax import lax
from jax.experimental import pallas as pl
from jax.experimental.pallas import tpu as pltpu
from jax.sharding import PartitionSpec as P

LANE = 128
UNROLL = 16
STEP = 384
VMEM_LIMIT = 48 * 1024 * 1024
LADDER = (16, 24, 32, 36, 40, 42, 44, 46, 48, 52, 56, 64, 80, 104, 144)
NT = (((1,), (1,)), ((), ()))


def plan_kernel(
    owner_in, cycle_in, valid_in, word_ref, scalar_ref, owner_ref, cycle_ref, valid_ref, arrived
):
    tm_index, tile_index = lax.axis_index("tm"), lax.axis_index("tile")
    fetches = [
        pltpu.make_async_copy(source, target, arrived.at[i])
        for i, (source, target) in enumerate(
            ((owner_in, owner_ref), (cycle_in, cycle_ref), (valid_in, valid_ref))
        )
    ]
    for fetch in fetches:
        fetch.start()
    for fetch in fetches:
        fetch.wait()
    chunks = cycle_ref.shape[0] // LANE
    slots = owner_ref.shape[0]
    list_rows = word_ref.shape[0]
    slot = lax.broadcasted_iota(jnp.int32, (slots, LANE), 0)
    mine = (slot % 2 == tile_index).astype(jnp.float32)
    owner = jnp.zeros((slots, LANE), jnp.int32)
    for s in range(slots):
        owner = jnp.where(slot == s, owner_ref[s], owner)

    member, weighted = [], []
    for k in range(chunks):
        cut = slice(k * LANE, (k + 1) * LANE)
        hit = (cycle_ref[cut].reshape(1, LANE) == owner).astype(jnp.float32)
        member.append(hit)
        weighted.append(hit * valid_ref[cut].reshape(1, LANE).astype(jnp.float32))
    stacked = jnp.concatenate(member + weighted, axis=0).astype(jnp.bfloat16)
    before = lax.broadcasted_iota(jnp.int32, (LANE, 2 * LANE), 0)
    column = lax.broadcasted_iota(jnp.int32, (LANE, 2 * LANE), 1)
    prefix = ((before < column) | (column >= LANE)).astype(jnp.float32).astype(jnp.bfloat16)
    sums = jnp.dot(stacked, prefix, preferred_element_type=jnp.float32)

    count = jnp.zeros((slots, LANE), jnp.float32)
    pixels = jnp.zeros((slots, LANE), jnp.float32)
    rank, start = [], []
    for k in range(chunks):
        low = slice(k * slots, (k + 1) * slots)
        high = slice((chunks + k) * slots, (chunks + k + 1) * slots)
        rank.append(count + sums[low, :LANE])
        start.append(pixels + sums[high, :LANE])
        count = count + sums[low, LANE:]
        pixels = pixels + sums[high, LANE:]

    rows = (jnp.max(pixels).astype(jnp.int32) + LANE - 1) // LANE
    rung = jnp.int32(0)
    size = jnp.int32(LADDER[0])
    for smaller, larger in zip(LADDER[:-1], LADDER[1:]):
        rung = rung + (rows > smaller).astype(jnp.int32)
        size = jnp.where(rows > smaller, larger, size)

    row = lax.broadcasted_iota(jnp.int32, (slots, slots), 0)
    col = lax.broadcasted_iota(jnp.int32, (slots, slots), 1)
    earlier = ((col < row) & (col % 2 == tile_index)).astype(jnp.float32)
    base = jnp.dot(
        earlier, count, precision=lax.Precision.HIGHEST, preferred_element_type=jnp.float32
    )
    begin = (slot // 2 * size * LANE).astype(jnp.float32)

    list_row = lax.broadcasted_iota(jnp.int32, (list_rows, LANE), 0)
    list_col = lax.broadcasted_iota(jnp.int32, (LANE, LANE), 0)
    lane = lax.broadcasted_iota(jnp.int32, (1, LANE), 1)
    lists = jnp.zeros((4 * list_rows, LANE), jnp.float32)
    for k in range(chunks):
        own = member[k] * mine
        place = jnp.sum(own * (rank[k] + base), axis=0, keepdims=True).astype(jnp.int32)
        at = jnp.sum(own * (start[k] + begin), axis=0, keepdims=True).astype(jnp.int32)
        used = jnp.sum(own, axis=0, keepdims=True) > 0
        word = at * 4096 + (k * LANE + lane)
        at_row = list_row == jnp.where(used, place // LANE, -1)
        at_col = (list_col == place % LANE).astype(jnp.float32).astype(jnp.bfloat16)
        spread = jnp.concatenate(
            [
                jnp.where(at_row, ((word >> (8 * part)) & 255).astype(jnp.float32), 0.0)
                for part in range(4)
            ],
            axis=0,
        ).astype(jnp.bfloat16)
        lists = lists + lax.dot_general(spread, at_col, NT, preferred_element_type=jnp.float32)
    lists = lists.astype(jnp.int32)
    words = jnp.zeros((list_rows, LANE), jnp.int32)
    for part in range(4):
        words = words + (lists[part * list_rows : (part + 1) * list_rows] << (8 * part))
    word_ref[...] = words

    own_slot = 2 * tm_index + tile_index
    scalar_ref[0] = rung
    scalar_ref[1] = jnp.sum(count[:, :1] * mine[:, :1]).astype(jnp.int32)
    scalar_ref[2] = jnp.sum(jnp.where(slot == own_slot, pixels, 0.0)[:, :1]).astype(jnp.int32)
    scalar_ref[3] = tile_index


def pack_kernel(word_ref, scalar_ref, near_ref, far_ref, out_ref, pool, stage):
    frames, half, _ = near_ref.shape
    stride = 2 * half + 1
    near_at = scalar_ref[3] * half
    far_at = half - near_at
    for source, at in ((near_ref, near_at), (far_ref, far_at)):
        for f in range(frames):

            def widen(i, _, source=source, at=at, f=f):
                begin = pl.multiple_of(i * STEP, STEP)
                to = f * stride + pl.multiple_of(at + begin, 8)
                pool[pl.ds(to, STEP), :] = source[f, pl.ds(begin, STEP), :].astype(jnp.float32)
                return 0

            lax.fori_loop(0, half // STEP, widen, 0)

    lane = lax.broadcasted_iota(jnp.int32, (frames, LANE), 1)

    def place(i, count, carry):
        held, spill, last = carry
        turned, row, shift = [], [], []
        for j in range(count):
            word = word_ref[i + j]
            x = pool[pl.ds(word & 4095, frames, stride=stride), :]
            row.append(word >> 19)
            shift.append((word >> 12) & (LANE - 1))
            turned.append(pltpu.roll(x, shift[j], 1))
        for j in range(count):
            held = jnp.where(
                lane >= shift[j], turned[j], jnp.where(row[j] == last, held, spill)
            )
            spill, last = turned[j], row[j]
            at = pl.multiple_of(last * frames, frames)
            stage[pl.ds(at, frames), :] = held
            stage[pl.ds(at + frames, frames), :] = spill
        return held, spill, last

    total = scalar_ref[1]
    zero = jnp.zeros((frames, LANE), jnp.float32)
    carry = (zero, zero, jnp.int32(-1))
    groups = total // UNROLL
    carry = lax.fori_loop(0, groups, lambda i, c: place(i * UNROLL, UNROLL, c), carry)
    lax.fori_loop(groups * UNROLL, total, lambda i, c: place(i, 1, c), carry)

    depth = out_ref.shape[1]
    for d in range(out_ref.shape[0]):
        out_ref[d] = stage[d * depth : (d + 1) * depth, :].astype(jnp.bfloat16)


def gram_kernel(scalar_ref, x_ref, out_ref):
    sources = x_ref.shape[0]
    frames = out_ref.shape[0]
    local = frames // sources
    pixels = scalar_ref[2]
    lane = lax.broadcasted_iota(jnp.int32, (1, LANE), 1)

    def pair(j, carry):
        gram, total = carry
        rows = pl.ds(pl.multiple_of(j * 2 * local, 2 * local), 2 * local)
        both = [x_ref[source, rows, :].astype(jnp.float32) for source in range(sources)]
        exact, high, low = [], [], []
        for i in range(2):
            used = lane + (2 * j + i) * LANE < pixels
            x = jnp.concatenate([part[i * local : (i + 1) * local] for part in both], axis=0)
            x = jnp.where(used, x, 0.0)
            mean = jnp.where(used, jnp.sum(x, axis=0, keepdims=True) / frames, 1.0)
            scale = 1.0 / mean
            total = total + x * scale
            y = x * (scale * scale)
            top = y.astype(jnp.bfloat16)
            exact.append(x.astype(jnp.bfloat16))
            high.append(top)
            low.append((y - top.astype(jnp.float32)).astype(jnp.bfloat16))
        left = jnp.concatenate(exact, axis=1)
        right = jnp.concatenate(
            [jnp.concatenate(high, axis=1), jnp.concatenate(low, axis=1)], axis=0
        )
        gram = gram + lax.dot_general(left, right, NT, preferred_element_type=jnp.float32)
        return gram, total

    def two_pairs(j, carry):
        return pair(2 * j + 1, pair(2 * j, carry))

    carry = (jnp.zeros((frames, 2 * frames), jnp.float32), jnp.zeros((frames, LANE), jnp.float32))
    pairs = (pixels + 2 * LANE - 1) // (2 * LANE)
    carry = lax.fori_loop(0, pairs // 2, two_pairs, carry)
    gram, total = lax.fori_loop(pairs // 2 * 2, pairs, pair, carry)
    gram = gram[:, :frames] + gram[:, frames:]
    first = jnp.sum(total, axis=1, keepdims=True)
    second = jnp.sum(total.T, axis=0, keepdims=True)
    out_ref[...] = pixels.astype(jnp.float32) * gram / (first * second)


def on_device_routed(frames, block_cycle, block_valid, cycle_owner):
    tm_count = lax.axis_size("tm")
    local_frames, half, _ = frames.shape
    list_rows = -(-block_cycle.shape[0] // (8 * LANE)) * 8
    vmem = pl.BlockSpec(memory_space=pltpu.VMEM)
    smem = pl.BlockSpec(memory_space=pltpu.SMEM)
    params = pltpu.CompilerParams(vmem_limit_bytes=VMEM_LIMIT)

    far = lax.ppermute(frames, "tile", [(0, 1), (1, 0)])
    words, scalars = pl.pallas_call(
        plan_kernel,
        out_shape=(
            jax.ShapeDtypeStruct((list_rows, LANE), jnp.int32),
            jax.ShapeDtypeStruct((4,), jnp.int32),
        ),
        in_specs=[pl.BlockSpec(memory_space=pl.ANY)] * 3,
        out_specs=(vmem, smem),
        scratch_shapes=[
            pltpu.SMEM(cycle_owner.shape, jnp.int32),
            pltpu.VMEM(block_cycle.shape, jnp.int32),
            pltpu.VMEM(block_valid.shape, jnp.int32),
            pltpu.SemaphoreType.DMA((3,)),
        ],
        compiler_params=params,
        name="plan",
    )(cycle_owner, block_cycle, block_valid)
    words = words.reshape(-1)

    def branch(size):
        depth = size * local_frames

        def run(words, scalars, near, far):
            send = pl.pallas_call(
                pack_kernel,
                out_shape=jax.ShapeDtypeStruct((tm_count, depth, LANE), jnp.bfloat16),
                in_specs=[smem, smem, vmem, vmem],
                out_specs=vmem,
                scratch_shapes=[
                    pltpu.VMEM((local_frames * (2 * half + 1) + 8, LANE), jnp.float32),
                    pltpu.VMEM((tm_count * depth + local_frames, LANE), jnp.float32),
                ],
                compiler_params=params,
                name="pack",
            )(words, scalars, near, far)
            got = lax.all_to_all(send, "tm", split_axis=0, concat_axis=0, tiled=True)
            return pl.pallas_call(
                gram_kernel,
                out_shape=jax.ShapeDtypeStruct(
                    (tm_count * local_frames, tm_count * local_frames), jnp.float32
                ),
                in_specs=[smem, vmem],
                out_specs=vmem,
                compiler_params=params,
                name="gram",
            )(scalars, got)

        return run

    return lax.switch(
        scalars[0], [branch(size) for size in LADDER], words, scalars, frames, far
    )


def normalize(pixel_intensity, valid_count, lanes):
    lane_index = jnp.arange(lanes, dtype=jnp.int32)
    valid_mask = lane_index[None, :] < valid_count[:, None]
    pixel_mean = jnp.sum(pixel_intensity, axis=0) / pixel_intensity.shape[0]
    guarded_average = jnp.where(valid_mask, pixel_mean, jnp.float32(1.0))
    return jnp.where(valid_mask[None], pixel_intensity / guarded_average[None], jnp.float32(0.0))


def on_device_summed(frames, block_cycle, block_valid, cycle_owner):
    tm_count = lax.axis_size("tm")
    tile_count = lax.axis_size("tile")
    tm_index = lax.axis_index("tm")
    tile_index = lax.axis_index("tile")
    local_frames = frames.shape[0]
    half = frames.shape[1]
    lanes = frames.shape[2]
    cycle_count = cycle_owner.shape[0]
    frame_count = local_frames * tm_count
    cycle_range = jnp.arange(cycle_count, dtype=jnp.int32)
    member_all = (block_cycle[None, :] == cycle_owner[:, None]).astype(jnp.float32)
    pixel_total = jnp.dot(
        member_all, block_valid.astype(jnp.float32), precision=lax.Precision.HIGHEST
    )
    row_count = cycle_count * frame_count // (tm_count * tile_count)
    block_local = half // tm_count
    reshaped = frames.reshape(local_frames, tm_count, block_local, lanes)
    arrived = lax.all_to_all(reshaped, "tm", split_axis=1, concat_axis=0, tiled=True)
    pixel_intensity = arrived.reshape(frame_count, block_local, lanes).astype(jnp.float32)
    offset = (tile_index * tm_count + tm_index) * block_local
    cycle_ids = lax.dynamic_slice_in_dim(block_cycle, offset, block_local, 0)
    valid_count = lax.dynamic_slice_in_dim(block_valid, offset, block_local, 0)
    members = (cycle_ids[None, :] == cycle_owner[:, None]).astype(jnp.float32)
    normalized_frames = normalize(pixel_intensity, valid_count, lanes)
    gram_matrices = jnp.einsum(
        "rnk,jnk->nrj", normalized_frames, normalized_frames, precision=lax.Precision.HIGHEST
    )
    partial_value = jnp.dot(
        members,
        gram_matrices.reshape(block_local, frame_count * frame_count),
        precision=lax.Precision.HIGHEST,
    )
    partial_value = partial_value.reshape(cycle_count * frame_count, frame_count)
    frame_sums = jnp.dot(
        members, jnp.sum(normalized_frames, axis=2).T, precision=lax.Precision.HIGHEST
    )
    owned = lax.psum_scatter(partial_value, ("tm", "tile"), scatter_dimension=0, tiled=True)
    frame_total = lax.psum(frame_sums, ("tm", "tile"))
    row_start = (tm_index * tile_count + tile_index) * row_count
    row_global = row_start + jnp.arange(row_count, dtype=jnp.int32)
    slot_index = row_global // frame_count
    frame_time_index = row_global % frame_count
    select = (slot_index[:, None] == cycle_range[None, :]).astype(jnp.float32)
    row_sums = jnp.dot(select, frame_total, precision=lax.Precision.HIGHEST)
    row_pixels = jnp.dot(select, pixel_total, precision=lax.Precision.HIGHEST)
    time_pick = (
        jnp.arange(frame_count, dtype=jnp.int32)[None, :] == frame_time_index[:, None]
    ).astype(jnp.float32)
    first_sums = jnp.sum(row_sums * time_pick, axis=1)
    return row_pixels[:, None] * owned / (first_sums[:, None] * row_sums)


def solution(mesh):
    in_specs = (P("tm", ("series", "tile"), None), P("series"), P("series"), P())
    out_specs = P(("series", "tm", "tile"), None)

    def on_device(frames, block_cycle, block_valid, cycle_owner):
        routed = (
            mesh.shape["tile"] == 2
            and mesh.shape["tm"] * 2 == cycle_owner.shape[0]
            and frames.shape[0] == 8
            and mesh.shape["tm"] * 8 == LANE
            and block_cycle.shape[0] <= 4096
        )
        body = on_device_routed if routed else on_device_summed
        return body(frames, block_cycle, block_valid, cycle_owner)

    return jax.shard_map(
        on_device, mesh=mesh, in_specs=in_specs, out_specs=out_specs, check_vma=False
    )
```

```python
import functools

import jax
import jax.numpy as jnp
from jax import lax
from jax.experimental import pallas as pl
from jax.experimental.pallas import tpu as pltpu
from jax.sharding import PartitionSpec as P

LANE = 128
UNROLL = 16
STEP = 384
VMEM_LIMIT = 48 * 1024 * 1024
LADDER = (16, 24, 32, 36, 40, 42, 44, 46, 48, 52, 56, 64, 80, 104, 144)
NT = (((1,), (1,)), ((), ()))


def plan_kernel(
    owner_in, cycle_in, valid_in, word_ref, scalar_ref, owner_ref, cycle_ref, valid_ref, arrived
):
    tm_index, tile_index = lax.axis_index("tm"), lax.axis_index("tile")
    fetches = [
        pltpu.make_async_copy(source, target, arrived.at[i])
        for i, (source, target) in enumerate(
            ((owner_in, owner_ref), (cycle_in, cycle_ref), (valid_in, valid_ref))
        )
    ]
    for fetch in fetches:
        fetch.start()
    for fetch in fetches:
        fetch.wait()
    chunks = cycle_ref.shape[0] // LANE
    slots = owner_ref.shape[0]
    list_rows = word_ref.shape[0]
    slot = lax.broadcasted_iota(jnp.int32, (slots, LANE), 0)
    mine = (slot % 2 == tile_index).astype(jnp.float32)
    owner = jnp.zeros((slots, LANE), jnp.int32)
    for s in range(slots):
        owner = jnp.where(slot == s, owner_ref[s], owner)

    member, weighted = [], []
    for k in range(chunks):
        cut = slice(k * LANE, (k + 1) * LANE)
        hit = (cycle_ref[cut].reshape(1, LANE) == owner).astype(jnp.float32)
        member.append(hit)
        weighted.append(hit * valid_ref[cut].reshape(1, LANE).astype(jnp.float32))
    stacked = jnp.concatenate(member + weighted, axis=0).astype(jnp.bfloat16)
    before = lax.broadcasted_iota(jnp.int32, (LANE, 2 * LANE), 0)
    column = lax.broadcasted_iota(jnp.int32, (LANE, 2 * LANE), 1)
    prefix = ((before < column) | (column >= LANE)).astype(jnp.float32).astype(jnp.bfloat16)
    sums = jnp.dot(stacked, prefix, preferred_element_type=jnp.float32)

    count = jnp.zeros((slots, LANE), jnp.float32)
    pixels = jnp.zeros((slots, LANE), jnp.float32)
    rank, start = [], []
    for k in range(chunks):
        low = slice(k * slots, (k + 1) * slots)
        high = slice((chunks + k) * slots, (chunks + k + 1) * slots)
        rank.append(count + sums[low, :LANE])
        start.append(pixels + sums[high, :LANE])
        count = count + sums[low, LANE:]
        pixels = pixels + sums[high, LANE:]

    rows = (jnp.max(pixels).astype(jnp.int32) + LANE - 1) // LANE
    rung = jnp.int32(0)
    size = jnp.int32(LADDER[0])
    for smaller, larger in zip(LADDER[:-1], LADDER[1:]):
        rung = rung + (rows > smaller).astype(jnp.int32)
        size = jnp.where(rows > smaller, larger, size)

    row = lax.broadcasted_iota(jnp.int32, (slots, slots), 0)
    col = lax.broadcasted_iota(jnp.int32, (slots, slots), 1)
    earlier = ((col < row) & (col % 2 == tile_index)).astype(jnp.float32)
    base = jnp.dot(
        earlier, count, precision=lax.Precision.HIGHEST, preferred_element_type=jnp.float32
    )
    begin = (slot // 2 * size * LANE).astype(jnp.float32)

    list_row = lax.broadcasted_iota(jnp.int32, (list_rows, LANE), 0)
    list_col = lax.broadcasted_iota(jnp.int32, (LANE, LANE), 0)
    lane = lax.broadcasted_iota(jnp.int32, (1, LANE), 1)
    lists = jnp.zeros((4 * list_rows, LANE), jnp.float32)
    for k in range(chunks):
        own = member[k] * mine
        place = jnp.sum(own * (rank[k] + base), axis=0, keepdims=True).astype(jnp.int32)
        at = jnp.sum(own * (start[k] + begin), axis=0, keepdims=True).astype(jnp.int32)
        used = jnp.sum(own, axis=0, keepdims=True) > 0
        word = at * 4096 + (k * LANE + lane)
        at_row = list_row == jnp.where(used, place // LANE, -1)
        at_col = (list_col == place % LANE).astype(jnp.float32).astype(jnp.bfloat16)
        spread = jnp.concatenate(
            [
                jnp.where(at_row, ((word >> (8 * part)) & 255).astype(jnp.float32), 0.0)
                for part in range(4)
            ],
            axis=0,
        ).astype(jnp.bfloat16)
        lists = lists + lax.dot_general(spread, at_col, NT, preferred_element_type=jnp.float32)
    lists = lists.astype(jnp.int32)
    words = jnp.zeros((list_rows, LANE), jnp.int32)
    for part in range(4):
        words = words + (lists[part * list_rows : (part + 1) * list_rows] << (8 * part))
    word_ref[...] = words

    scalar_ref[0] = rung
    scalar_ref[1] = jnp.sum(count[:, :1] * mine[:, :1]).astype(jnp.int32)
    scalar_ref[2] = tile_index


def pack_kernel(word_ref, scalar_ref, near_ref, far_ref, out_ref, pool, stage):
    frames, half, _ = near_ref.shape
    stride = 2 * half + 1
    near_at = scalar_ref[2] * half
    far_at = half - near_at
    for source, at in ((near_ref, near_at), (far_ref, far_at)):
        for f in range(frames):

            def widen(i, _, source=source, at=at, f=f):
                begin = pl.multiple_of(i * STEP, STEP)
                to = f * stride + pl.multiple_of(at + begin, 8)
                pool[pl.ds(to, STEP), :] = source[f, pl.ds(begin, STEP), :].astype(jnp.float32)
                return 0

            lax.fori_loop(0, half // STEP, widen, 0)

    lane = lax.broadcasted_iota(jnp.int32, (frames, LANE), 1)

    def place(i, count, carry):
        held, spill, last = carry
        turned, row, shift = [], [], []
        for j in range(count):
            word = word_ref[i + j]
            x = pool[pl.ds(word & 4095, frames, stride=stride), :]
            row.append(word >> 19)
            shift.append((word >> 12) & (LANE - 1))
            turned.append(pltpu.roll(x, shift[j], 1))
        for j in range(count):
            held = jnp.where(
                lane >= shift[j], turned[j], jnp.where(row[j] == last, held, spill)
            )
            spill, last = turned[j], row[j]
            at = pl.multiple_of(last * frames, frames)
            stage[pl.ds(at, frames), :] = held
            stage[pl.ds(at + frames, frames), :] = spill
        return held, spill, last

    total = scalar_ref[1]
    zero = jnp.zeros((frames, LANE), jnp.float32)
    carry = (zero, zero, jnp.int32(-1))
    groups = total // UNROLL
    carry = lax.fori_loop(0, groups, lambda i, c: place(i * UNROLL, UNROLL, c), carry)
    lax.fori_loop(groups * UNROLL, total, lambda i, c: place(i, 1, c), carry)

    depth = out_ref.shape[1]
    for d in range(out_ref.shape[0]):
        out_ref[d] = stage[d * depth : (d + 1) * depth, :].astype(jnp.bfloat16)


def gram_kernel(pixel_ref, x_ref, out_ref):
    sources = x_ref.shape[0]
    frames = out_ref.shape[0]
    local = frames // sources
    pixels = pixel_ref[0]
    lane = lax.broadcasted_iota(jnp.int32, (1, LANE), 1)

    def pair(j, carry):
        gram, total = carry
        rows = pl.ds(pl.multiple_of(j * 2 * local, 2 * local), 2 * local)
        both = [x_ref[source, rows, :].astype(jnp.float32) for source in range(sources)]
        exact, high, low = [], [], []
        for i in range(2):
            used = lane + (2 * j + i) * LANE < pixels
            x = jnp.concatenate([part[i * local : (i + 1) * local] for part in both], axis=0)
            x = jnp.where(used, x, 0.0)
            mean = jnp.where(used, jnp.sum(x, axis=0, keepdims=True) / frames, 1.0)
            scale = 1.0 / mean
            total = total + x * scale
            y = x * (scale * scale)
            top = y.astype(jnp.bfloat16)
            exact.append(x.astype(jnp.bfloat16))
            high.append(top)
            low.append((y - top.astype(jnp.float32)).astype(jnp.bfloat16))
        left = jnp.concatenate(exact, axis=1)
        right = jnp.concatenate(
            [jnp.concatenate(high, axis=1), jnp.concatenate(low, axis=1)], axis=0
        )
        gram = gram + lax.dot_general(left, right, NT, preferred_element_type=jnp.float32)
        return gram, total

    def two_pairs(j, carry):
        return pair(2 * j + 1, pair(2 * j, carry))

    carry = (jnp.zeros((frames, 2 * frames), jnp.float32), jnp.zeros((frames, LANE), jnp.float32))
    pairs = (pixels + 2 * LANE - 1) // (2 * LANE)
    carry = lax.fori_loop(0, pairs // 2, two_pairs, carry)
    gram, total = lax.fori_loop(pairs // 2 * 2, pairs, pair, carry)
    gram = gram[:, :frames] + gram[:, frames:]
    first = jnp.sum(total, axis=1, keepdims=True)
    second = jnp.sum(total.T, axis=0, keepdims=True)
    out_ref[...] = pixels.astype(jnp.float32) * gram / (first * second)


def on_device_routed(frames, block_cycle, block_valid, cycle_owner):
    tm_count = lax.axis_size("tm")
    local_frames, half, _ = frames.shape
    list_rows = -(-block_cycle.shape[0] // (8 * LANE)) * 8
    vmem = pl.BlockSpec(memory_space=pltpu.VMEM)
    smem = pl.BlockSpec(memory_space=pltpu.SMEM)
    params = pltpu.CompilerParams(vmem_limit_bytes=VMEM_LIMIT)

    far = lax.ppermute(frames, "tile", [(0, 1), (1, 0)])
    words, scalars = pl.pallas_call(
        plan_kernel,
        out_shape=(
            jax.ShapeDtypeStruct((list_rows, LANE), jnp.int32),
            jax.ShapeDtypeStruct((3,), jnp.int32),
        ),
        in_specs=[pl.BlockSpec(memory_space=pltpu.HBM)] * 3,
        out_specs=(vmem, smem),
        scratch_shapes=[
            pltpu.SMEM(cycle_owner.shape, jnp.int32),
            pltpu.VMEM(block_cycle.shape, jnp.int32),
            pltpu.VMEM(block_valid.shape, jnp.int32),
            pltpu.SemaphoreType.DMA((3,)),
        ],
        compiler_params=params,
        name="plan",
    )(cycle_owner, block_cycle, block_valid)
    words = words.reshape(-1)

    def branch(size):
        depth = size * local_frames

        def run(words, scalars, near, far, block_cycle, block_valid, cycle_owner):
            send = pl.pallas_call(
                pack_kernel,
                out_shape=jax.ShapeDtypeStruct((tm_count, depth, LANE), jnp.bfloat16),
                in_specs=[smem, smem, vmem, vmem],
                out_specs=vmem,
                scratch_shapes=[
                    pltpu.VMEM((local_frames * (2 * half + 1) + 8, LANE), jnp.float32),
                    pltpu.VMEM((tm_count * depth + local_frames, LANE), jnp.float32),
                ],
                compiler_params=params,
                name="pack",
            )(words, scalars, near, far)
            own = cycle_owner[2 * lax.axis_index("tm") + lax.axis_index("tile")]
            pixels = jnp.sum(jnp.where(block_cycle == own, block_valid, 0), keepdims=True)
            got = lax.all_to_all(send, "tm", split_axis=0, concat_axis=0, tiled=True)
            return pl.pallas_call(
                gram_kernel,
                out_shape=jax.ShapeDtypeStruct(
                    (tm_count * local_frames, tm_count * local_frames), jnp.float32
                ),
                in_specs=[smem, vmem],
                out_specs=vmem,
                compiler_params=params,
                name="gram",
            )(pixels, got)

        return run

    return lax.switch(
        scalars[0],
        [branch(size) for size in LADDER],
        words,
        scalars,
        frames,
        far,
        block_cycle,
        block_valid,
        cycle_owner,
    )


def normalize(pixel_intensity, valid_count, lanes):
    lane_index = jnp.arange(lanes, dtype=jnp.int32)
    valid_mask = lane_index[None, :] < valid_count[:, None]
    pixel_mean = jnp.sum(pixel_intensity, axis=0) / pixel_intensity.shape[0]
    guarded_average = jnp.where(valid_mask, pixel_mean, jnp.float32(1.0))
    return jnp.where(valid_mask[None], pixel_intensity / guarded_average[None], jnp.float32(0.0))


def on_device_summed(frames, block_cycle, block_valid, cycle_owner):
    tm_count = lax.axis_size("tm")
    tile_count = lax.axis_size("tile")
    tm_index = lax.axis_index("tm")
    tile_index = lax.axis_index("tile")
    local_frames = frames.shape[0]
    half = frames.shape[1]
    lanes = frames.shape[2]
    cycle_count = cycle_owner.shape[0]
    frame_count = local_frames * tm_count
    cycle_range = jnp.arange(cycle_count, dtype=jnp.int32)
    member_all = (block_cycle[None, :] == cycle_owner[:, None]).astype(jnp.float32)
    pixel_total = jnp.dot(
        member_all, block_valid.astype(jnp.float32), precision=lax.Precision.HIGHEST
    )
    row_count = cycle_count * frame_count // (tm_count * tile_count)
    block_local = half // tm_count
    reshaped = frames.reshape(local_frames, tm_count, block_local, lanes)
    arrived = lax.all_to_all(reshaped, "tm", split_axis=1, concat_axis=0, tiled=True)
    pixel_intensity = arrived.reshape(frame_count, block_local, lanes).astype(jnp.float32)
    offset = (tile_index * tm_count + tm_index) * block_local
    cycle_ids = lax.dynamic_slice_in_dim(block_cycle, offset, block_local, 0)
    valid_count = lax.dynamic_slice_in_dim(block_valid, offset, block_local, 0)
    members = (cycle_ids[None, :] == cycle_owner[:, None]).astype(jnp.float32)
    normalized_frames = normalize(pixel_intensity, valid_count, lanes)
    gram_matrices = jnp.einsum(
        "rnk,jnk->nrj", normalized_frames, normalized_frames, precision=lax.Precision.HIGHEST
    )
    partial_value = jnp.dot(
        members,
        gram_matrices.reshape(block_local, frame_count * frame_count),
        precision=lax.Precision.HIGHEST,
    )
    partial_value = partial_value.reshape(cycle_count * frame_count, frame_count)
    frame_sums = jnp.dot(
        members, jnp.sum(normalized_frames, axis=2).T, precision=lax.Precision.HIGHEST
    )
    owned = lax.psum_scatter(partial_value, ("tm", "tile"), scatter_dimension=0, tiled=True)
    frame_total = lax.psum(frame_sums, ("tm", "tile"))
    row_start = (tm_index * tile_count + tile_index) * row_count
    row_global = row_start + jnp.arange(row_count, dtype=jnp.int32)
    slot_index = row_global // frame_count
    frame_time_index = row_global % frame_count
    select = (slot_index[:, None] == cycle_range[None, :]).astype(jnp.float32)
    row_sums = jnp.dot(select, frame_total, precision=lax.Precision.HIGHEST)
    row_pixels = jnp.dot(select, pixel_total, precision=lax.Precision.HIGHEST)
    time_pick = (
        jnp.arange(frame_count, dtype=jnp.int32)[None, :] == frame_time_index[:, None]
    ).astype(jnp.float32)
    first_sums = jnp.sum(row_sums * time_pick, axis=1)
    return row_pixels[:, None] * owned / (first_sums[:, None] * row_sums)


def solution(mesh):
    in_specs = (P("tm", ("series", "tile"), None), P("series"), P("series"), P())
    out_specs = P(("series", "tm", "tile"), None)

    def on_device(frames, block_cycle, block_valid, cycle_owner):
        routed = (
            mesh.shape["tile"] == 2
            and mesh.shape["tm"] * 2 == cycle_owner.shape[0]
            and frames.shape[0] == 8
            and mesh.shape["tm"] * 8 == LANE
            and block_cycle.shape[0] <= 4096
        )
        body = on_device_routed if routed else on_device_summed
        return body(frames, block_cycle, block_valid, cycle_owner)

    return jax.shard_map(
        on_device, mesh=mesh, in_specs=in_specs, out_specs=out_specs, check_vma=False
    )
```

```python
import functools

import jax
import jax.numpy as jnp
from jax import lax
from jax.experimental import pallas as pl
from jax.experimental.pallas import tpu as pltpu
from jax.sharding import PartitionSpec as P

LANE = 128
UNROLL = 16
GROUPS = 2
STEP = 384
VMEM_LIMIT = 24 * 1024 * 1024
LADDER = (16, 24, 32, 36, 40, 42, 44, 46, 48, 52, 56, 64, 80, 104, 144)
NT = (((1,), (1,)), ((), ()))


def apart_of(turn, count):
    side = count // 2
    return (side if turn % 2 == 0 else 0) + side - 1 - turn // 2


def plan_kernel(
    owner_in, cycle_in, valid_in, word_ref, scalar_ref, owner_ref, cycle_ref, valid_ref, arrived
):
    tm_index, tile_index = lax.axis_index("tm"), lax.axis_index("tile")
    fetches = [
        pltpu.make_async_copy(source, target, arrived.at[i])
        for i, (source, target) in enumerate(
            ((owner_in, owner_ref), (cycle_in, cycle_ref), (valid_in, valid_ref))
        )
    ]
    for fetch in fetches:
        fetch.start()
    for fetch in fetches:
        fetch.wait()
    chunks = cycle_ref.shape[0] // LANE
    slots = owner_ref.shape[0]
    half = cycle_ref.shape[0] // 2
    list_rows = word_ref.shape[0]
    slot = lax.broadcasted_iota(jnp.int32, (slots, LANE), 0)
    mine = (slot % 2 == tile_index).astype(jnp.float32)
    owner = jnp.zeros((slots, LANE), jnp.int32)
    for s in range(slots):
        owner = jnp.where(slot == s, owner_ref[s], owner)

    member, weighted = [], []
    for k in range(chunks):
        cut = slice(k * LANE, (k + 1) * LANE)
        hit = (cycle_ref[cut].reshape(1, LANE) == owner).astype(jnp.float32)
        member.append(hit)
        weighted.append(hit * valid_ref[cut].reshape(1, LANE).astype(jnp.float32))
    stacked = jnp.concatenate(member + weighted, axis=0).astype(jnp.bfloat16)
    before = lax.broadcasted_iota(jnp.int32, (LANE, 2 * LANE), 0)
    column = lax.broadcasted_iota(jnp.int32, (LANE, 2 * LANE), 1)
    prefix = ((before < column) | (column >= LANE)).astype(jnp.float32).astype(jnp.bfloat16)
    sums = jnp.dot(stacked, prefix, preferred_element_type=jnp.float32)

    count = jnp.zeros((slots, LANE), jnp.float32)
    pixels = jnp.zeros((slots, LANE), jnp.float32)
    rank, start = [], []
    for k in range(chunks):
        low = slice(k * slots, (k + 1) * slots)
        high = slice((chunks + k) * slots, (chunks + k + 1) * slots)
        rank.append(count + sums[low, :LANE])
        start.append(pixels + sums[high, :LANE])
        count = count + sums[low, LANE:]
        pixels = pixels + sums[high, LANE:]

    rows = (jnp.max(pixels).astype(jnp.int32) + LANE - 1) // LANE
    rung = jnp.int32(0)
    size = jnp.int32(LADDER[0])
    for smaller, larger in zip(LADDER[:-1], LADDER[1:]):
        rung = rung + (rows > smaller).astype(jnp.int32)
        size = jnp.where(rows > smaller, larger, size)

    def turn_of(index):
        apart = (index // 2) ^ tm_index
        side = slots // 4
        return 2 * (side - 1 - apart % side) + (apart < side).astype(jnp.int32)

    row = turn_of(lax.broadcasted_iota(jnp.int32, (slots, slots), 0))
    index = lax.broadcasted_iota(jnp.int32, (slots, slots), 1)
    earlier = ((turn_of(index) < row) & (index % 2 == tile_index)).astype(jnp.float32)
    turn = turn_of(slot)
    base = jnp.dot(
        earlier, count, precision=lax.Precision.HIGHEST, preferred_element_type=jnp.float32
    )
    begin = (turn * size * LANE).astype(jnp.float32)

    list_row = lax.broadcasted_iota(jnp.int32, (list_rows, LANE), 0)
    list_col = lax.broadcasted_iota(jnp.int32, (LANE, LANE), 0)
    lane = lax.broadcasted_iota(jnp.int32, (1, LANE), 1)
    lists = jnp.zeros((4 * list_rows, LANE), jnp.float32)
    for k in range(chunks):
        own = member[k] * mine
        place = jnp.sum(own * (rank[k] + base), axis=0, keepdims=True).astype(jnp.int32)
        at = jnp.sum(own * (start[k] + begin), axis=0, keepdims=True).astype(jnp.int32)
        used = jnp.sum(own, axis=0, keepdims=True) > 0
        block = k * LANE + lane
        far = (block >= half) != (tile_index == 1)
        block = jnp.where(block >= half, block - half, block) + jnp.where(far, 2048, 0)
        word = at * 4096 + block
        at_row = list_row == jnp.where(used, place // LANE, -1)
        at_col = (list_col == place % LANE).astype(jnp.float32).astype(jnp.bfloat16)
        spread = jnp.concatenate(
            [
                jnp.where(at_row, ((word >> (8 * part)) & 255).astype(jnp.float32), 0.0)
                for part in range(4)
            ],
            axis=0,
        ).astype(jnp.bfloat16)
        lists = lists + lax.dot_general(spread, at_col, NT, preferred_element_type=jnp.float32)
    lists = lists.astype(jnp.int32)
    words = jnp.zeros((list_rows, LANE), jnp.int32)
    for part in range(4):
        words = words + (lists[part * list_rows : (part + 1) * list_rows] << (8 * part))
    word_ref[...] = words

    own_slot = 2 * tm_index + tile_index
    scalar_ref[0] = rung
    scalar_ref[1] = tm_index
    scalar_ref[2] = jnp.sum(jnp.where(slot == own_slot, pixels, 0.0)[:, :1]).astype(jnp.int32)
    for group in range(GROUPS + 1):
        ahead = jnp.where(turn * GROUPS < group * (slots // 2), count * mine, 0.0)
        scalar_ref[3 + group] = jnp.sum(ahead[:, :1]).astype(jnp.int32)


def widen_kernel(in_ref, out_ref):
    frames, half, _ = in_ref.shape
    for f in range(frames):

        def widen(i, _, f=f):
            begin = pl.multiple_of(i * STEP, STEP)
            rows = in_ref[f, pl.ds(begin, STEP), :].astype(jnp.float32)
            out_ref[pl.ds(f * (half + 1) + begin, STEP), :] = rows
            return 0

        lax.fori_loop(0, half // STEP, widen, 0)


def pack_kernel(group, word_ref, scalar_ref, near_ref, far_ref, *rest):
    out_refs, stage = rest[:-1], rest[-1]
    depth = out_refs[0].shape[0]
    frames = 8
    stride = near_ref.shape[0] // frames
    first_row = group * len(out_refs) * (depth // frames)
    lane = lax.broadcasted_iota(jnp.int32, (frames, LANE), 1)

    def place(i, count, carry):
        held, spill, last = carry
        turned, row, shift = [], [], []
        for j in range(count):
            word = word_ref[i + j]
            at = pl.ds(word & 2047, frames, stride=stride)
            x = jnp.where((word & 2048) == 0, near_ref[at, :], far_ref[at, :])
            row.append((word >> 19) - first_row)
            shift.append((word >> 12) & (LANE - 1))
            turned.append(pltpu.roll(x, shift[j], 1))
        for j in range(count):
            held = jnp.where(
                lane >= shift[j], turned[j], jnp.where(row[j] == last, held, spill)
            )
            spill, last = turned[j], row[j]
            at = pl.multiple_of(last * frames, frames)
            stage[pl.ds(at, frames), :] = held
            stage[pl.ds(at + frames, frames), :] = spill
        return held, spill, last

    begin, end = scalar_ref[3 + group], scalar_ref[4 + group]
    zero = jnp.zeros((frames, LANE), jnp.float32)
    carry = (zero, zero, jnp.int32(-1))
    groups = (end - begin) // UNROLL
    carry = lax.fori_loop(0, groups, lambda i, c: place(begin + i * UNROLL, UNROLL, c), carry)
    lax.fori_loop(begin + groups * UNROLL, end, lambda i, c: place(i, 1, c), carry)
    for d, out_ref in enumerate(out_refs):
        out_ref[...] = stage[d * depth : (d + 1) * depth, :].astype(jnp.bfloat16)


def gram_kernel(scalar_ref, *refs):
    x_refs, (out_ref, turn) = refs[:-2], refs[-2:]
    sources = len(x_refs)
    frames = out_ref.shape[0]
    local = frames // sources
    pixels = scalar_ref[2]
    tm_index = scalar_ref[1]
    lane = lax.broadcasted_iota(jnp.int32, (1, LANE), 1)

    def pair(j, carry):
        gram, total = carry
        rows = pl.ds(pl.multiple_of(j * 2 * local, 2 * local), 2 * local)
        both = [ref[rows, :].astype(jnp.float32) for ref in x_refs]
        exact, high, low = [], [], []
        for i in range(2):
            used = lane + (2 * j + i) * LANE < pixels
            x = jnp.concatenate([part[i * local : (i + 1) * local] for part in both], axis=0)
            x = jnp.where(used, x, 0.0)
            mean = jnp.where(used, jnp.sum(x, axis=0, keepdims=True) / frames, 1.0)
            scale = 1.0 / mean
            total = total + x * scale
            y = x * (scale * scale)
            top = y.astype(jnp.bfloat16)
            exact.append(x.astype(jnp.bfloat16))
            high.append(top)
            low.append((y - top.astype(jnp.float32)).astype(jnp.bfloat16))
        left = jnp.concatenate(exact, axis=1)
        right = jnp.concatenate(
            [jnp.concatenate(high, axis=1), jnp.concatenate(low, axis=1)], axis=0
        )
        gram = gram + lax.dot_general(left, right, NT, preferred_element_type=jnp.float32)
        return gram, total

    def two_pairs(j, carry):
        return pair(2 * j + 1, pair(2 * j, carry))

    def in_order(value):
        for j in range(sources):
            at = pl.multiple_of((tm_index ^ apart_of(j, sources)) * local, local)
            turn[pl.ds(at, local), :] = value[j * local : (j + 1) * local]
        return turn[...]

    carry = (jnp.zeros((frames, 2 * frames), jnp.float32), jnp.zeros((frames, LANE), jnp.float32))
    pairs = (pixels + 2 * LANE - 1) // (2 * LANE)
    carry = lax.fori_loop(0, pairs // 2, two_pairs, carry)
    gram, total = lax.fori_loop(pairs // 2 * 2, pairs, pair, carry)
    gram = in_order(gram[:, :frames] + gram[:, frames:])
    gram = in_order(gram.T)
    total = in_order(total)
    first = jnp.sum(total, axis=1, keepdims=True)
    second = jnp.sum(total.T, axis=0, keepdims=True)
    out_ref[...] = pixels.astype(jnp.float32) * gram / (first * second)


def on_device_routed(frames, block_cycle, block_valid, cycle_owner):
    tm_count = lax.axis_size("tm")
    local_frames, half, _ = frames.shape
    frame_count = tm_count * local_frames
    list_rows = -(-block_cycle.shape[0] // (8 * LANE)) * 8
    vmem = pl.BlockSpec(memory_space=pltpu.VMEM)
    smem = pl.BlockSpec(memory_space=pltpu.SMEM)
    params = pltpu.CompilerParams(vmem_limit_bytes=VMEM_LIMIT)

    def widen(part):
        return pl.pallas_call(
            widen_kernel,
            out_shape=jax.ShapeDtypeStruct((local_frames * (half + 1), LANE), jnp.float32),
            in_specs=[vmem],
            out_specs=vmem,
            compiler_params=params,
            name="widen",
        )(part)

    far = lax.ppermute(frames, "tile", [(0, 1), (1, 0)])
    words, scalars = pl.pallas_call(
        plan_kernel,
        out_shape=(
            jax.ShapeDtypeStruct((list_rows, LANE), jnp.int32),
            jax.ShapeDtypeStruct((4 + GROUPS,), jnp.int32),
        ),
        in_specs=[pl.BlockSpec(memory_space=pltpu.HBM)] * 3,
        out_specs=(vmem, smem),
        scratch_shapes=[
            pltpu.SMEM(cycle_owner.shape, jnp.int32),
            pltpu.VMEM(block_cycle.shape, jnp.int32),
            pltpu.VMEM(block_valid.shape, jnp.int32),
            pltpu.SemaphoreType.DMA((3,)),
        ],
        compiler_params=params,
        name="plan",
    )(cycle_owner, block_cycle, block_valid)
    near_pool = widen(frames)
    far_pool = widen(far)
    members = tm_count // GROUPS

    def branch(size):
        depth = size * local_frames

        def run(words, scalars, near_pool, far_pool):
            got = []
            for group in range(GROUPS):
                send = pl.pallas_call(
                    functools.partial(pack_kernel, group),
                    out_shape=(jax.ShapeDtypeStruct((depth, LANE), jnp.bfloat16),) * members,
                    in_specs=[smem, smem, vmem, vmem],
                    out_specs=(vmem,) * members,
                    scratch_shapes=[pltpu.VMEM((members * depth + local_frames, LANE), jnp.float32)],
                    compiler_params=params,
                    cost_estimate=pl.CostEstimate(
                        flops=2_000_000, bytes_accessed=16_000_000, transcendentals=0
                    ),
                    name="pack",
                )(words, scalars, near_pool, far_pool)
                for j in range(members):
                    apart = apart_of(group * members + j, tm_count)
                    pairs = [(i, i ^ apart) for i in range(tm_count)]
                    got.append(lax.ppermute(send[j], "tm", pairs) if apart else send[j])
            return pl.pallas_call(
                gram_kernel,
                out_shape=jax.ShapeDtypeStruct((frame_count, frame_count), jnp.float32),
                in_specs=[smem] + [vmem] * tm_count,
                out_specs=vmem,
                scratch_shapes=[pltpu.VMEM((frame_count, LANE), jnp.float32)],
                compiler_params=params,
                name="gram",
            )(scalars, *got)

        return run

    return lax.switch(
        scalars[0],
        [branch(size) for size in LADDER],
        words.reshape(-1),
        scalars,
        near_pool,
        far_pool,
    )


def normalize(pixel_intensity, valid_count, lanes):
    lane_index = jnp.arange(lanes, dtype=jnp.int32)
    valid_mask = lane_index[None, :] < valid_count[:, None]
    pixel_mean = jnp.sum(pixel_intensity, axis=0) / pixel_intensity.shape[0]
    guarded_average = jnp.where(valid_mask, pixel_mean, jnp.float32(1.0))
    return jnp.where(valid_mask[None], pixel_intensity / guarded_average[None], jnp.float32(0.0))


def on_device_summed(frames, block_cycle, block_valid, cycle_owner):
    tm_count = lax.axis_size("tm")
    tile_count = lax.axis_size("tile")
    tm_index = lax.axis_index("tm")
    tile_index = lax.axis_index("tile")
    local_frames = frames.shape[0]
    half = frames.shape[1]
    lanes = frames.shape[2]
    cycle_count = cycle_owner.shape[0]
    frame_count = local_frames * tm_count
    cycle_range = jnp.arange(cycle_count, dtype=jnp.int32)
    member_all = (block_cycle[None, :] == cycle_owner[:, None]).astype(jnp.float32)
    pixel_total = jnp.dot(
        member_all, block_valid.astype(jnp.float32), precision=lax.Precision.HIGHEST
    )
    row_count = cycle_count * frame_count // (tm_count * tile_count)
    block_local = half // tm_count
    reshaped = frames.reshape(local_frames, tm_count, block_local, lanes)
    arrived = lax.all_to_all(reshaped, "tm", split_axis=1, concat_axis=0, tiled=True)
    pixel_intensity = arrived.reshape(frame_count, block_local, lanes).astype(jnp.float32)
    offset = (tile_index * tm_count + tm_index) * block_local
    cycle_ids = lax.dynamic_slice_in_dim(block_cycle, offset, block_local, 0)
    valid_count = lax.dynamic_slice_in_dim(block_valid, offset, block_local, 0)
    members = (cycle_ids[None, :] == cycle_owner[:, None]).astype(jnp.float32)
    normalized_frames = normalize(pixel_intensity, valid_count, lanes)
    gram_matrices = jnp.einsum(
        "rnk,jnk->nrj", normalized_frames, normalized_frames, precision=lax.Precision.HIGHEST
    )
    partial_value = jnp.dot(
        members,
        gram_matrices.reshape(block_local, frame_count * frame_count),
        precision=lax.Precision.HIGHEST,
    )
    partial_value = partial_value.reshape(cycle_count * frame_count, frame_count)
    frame_sums = jnp.dot(
        members, jnp.sum(normalized_frames, axis=2).T, precision=lax.Precision.HIGHEST
    )
    owned = lax.psum_scatter(partial_value, ("tm", "tile"), scatter_dimension=0, tiled=True)
    frame_total = lax.psum(frame_sums, ("tm", "tile"))
    row_start = (tm_index * tile_count + tile_index) * row_count
    row_global = row_start + jnp.arange(row_count, dtype=jnp.int32)
    slot_index = row_global // frame_count
    frame_time_index = row_global % frame_count
    select = (slot_index[:, None] == cycle_range[None, :]).astype(jnp.float32)
    row_sums = jnp.dot(select, frame_total, precision=lax.Precision.HIGHEST)
    row_pixels = jnp.dot(select, pixel_total, precision=lax.Precision.HIGHEST)
    time_pick = (
        jnp.arange(frame_count, dtype=jnp.int32)[None, :] == frame_time_index[:, None]
    ).astype(jnp.float32)
    first_sums = jnp.sum(row_sums * time_pick, axis=1)
    return row_pixels[:, None] * owned / (first_sums[:, None] * row_sums)


def solution(mesh):
    in_specs = (P("tm", ("series", "tile"), None), P("series"), P("series"), P())
    out_specs = P(("series", "tm", "tile"), None)

    def on_device(frames, block_cycle, block_valid, cycle_owner):
        routed = (
            mesh.shape["tile"] == 2
            and mesh.shape["tm"] * 2 == cycle_owner.shape[0]
            and frames.shape[0] == 8
            and mesh.shape["tm"] * 8 == LANE
            and block_cycle.shape[0] <= 4096
        )
        body = on_device_routed if routed else on_device_summed
        return body(frames, block_cycle, block_valid, cycle_owner)

    return jax.shard_map(
        on_device, mesh=mesh, in_specs=in_specs, out_specs=out_specs, check_vma=False
    )
```

```python
import functools

import jax
import jax.numpy as jnp
from jax import lax
from jax.experimental import pallas as pl
from jax.experimental.pallas import tpu as pltpu
from jax.sharding import PartitionSpec as P

LANE = 128
UNROLL = 16
GROUPS = 4
STEP = 128
VMEM_LIMIT = 24 * 1024 * 1024
LADDER = (16, 24, 32, 36, 40, 42, 44, 46, 48, 52, 56, 64, 80, 104, 144)
NT = (((1,), (1,)), ((), ()))


def apart_of(turn, count):
    side = count // 2
    return (side if turn % 2 == 0 else 0) + side - 1 - turn // 2


def plan_kernel(
    owner_in, cycle_in, valid_in, word_ref, scalar_ref, owner_ref, cycle_ref, valid_ref, arrived
):
    tm_index, tile_index = lax.axis_index("tm"), lax.axis_index("tile")
    fetches = [
        pltpu.make_async_copy(source, target, arrived.at[i])
        for i, (source, target) in enumerate(
            ((owner_in, owner_ref), (cycle_in, cycle_ref), (valid_in, valid_ref))
        )
    ]
    for fetch in fetches:
        fetch.start()
    for fetch in fetches:
        fetch.wait()
    chunks = cycle_ref.shape[0] // LANE
    slots = owner_ref.shape[0]
    half = cycle_ref.shape[0] // 2
    list_rows = word_ref.shape[0]
    slot = lax.broadcasted_iota(jnp.int32, (slots, LANE), 0)
    mine = (slot % 2 == tile_index).astype(jnp.float32)
    owner = jnp.zeros((slots, LANE), jnp.int32)
    for s in range(slots):
        owner = jnp.where(slot == s, owner_ref[s], owner)

    member, weighted = [], []
    for k in range(chunks):
        cut = slice(k * LANE, (k + 1) * LANE)
        hit = (cycle_ref[cut].reshape(1, LANE) == owner).astype(jnp.float32)
        member.append(hit)
        weighted.append(hit * valid_ref[cut].reshape(1, LANE).astype(jnp.float32))
    stacked = jnp.concatenate(member + weighted, axis=0).astype(jnp.bfloat16)
    before = lax.broadcasted_iota(jnp.int32, (LANE, 2 * LANE), 0)
    column = lax.broadcasted_iota(jnp.int32, (LANE, 2 * LANE), 1)
    prefix = ((before < column) | (column >= LANE)).astype(jnp.float32).astype(jnp.bfloat16)
    sums = jnp.dot(stacked, prefix, preferred_element_type=jnp.float32)

    count = jnp.zeros((slots, LANE), jnp.float32)
    pixels = jnp.zeros((slots, LANE), jnp.float32)
    rank, start = [], []
    for k in range(chunks):
        low = slice(k * slots, (k + 1) * slots)
        high = slice((chunks + k) * slots, (chunks + k + 1) * slots)
        rank.append(count + sums[low, :LANE])
        start.append(pixels + sums[high, :LANE])
        count = count + sums[low, LANE:]
        pixels = pixels + sums[high, LANE:]

    rows = (jnp.max(pixels).astype(jnp.int32) + LANE - 1) // LANE
    rung = jnp.int32(0)
    size = jnp.int32(LADDER[0])
    for smaller, larger in zip(LADDER[:-1], LADDER[1:]):
        rung = rung + (rows > smaller).astype(jnp.int32)
        size = jnp.where(rows > smaller, larger, size)

    def turn_of(index):
        apart = (index // 2) ^ tm_index
        side = slots // 4
        return 2 * (side - 1 - apart % side) + (apart < side).astype(jnp.int32)

    row = turn_of(lax.broadcasted_iota(jnp.int32, (slots, slots), 0))
    index = lax.broadcasted_iota(jnp.int32, (slots, slots), 1)
    earlier = ((turn_of(index) < row) & (index % 2 == tile_index)).astype(jnp.float32)
    turn = turn_of(slot)
    base = jnp.dot(
        earlier, count, precision=lax.Precision.HIGHEST, preferred_element_type=jnp.float32
    )
    begin = (turn * size * LANE).astype(jnp.float32)

    list_row = lax.broadcasted_iota(jnp.int32, (list_rows, LANE), 0)
    list_col = lax.broadcasted_iota(jnp.int32, (LANE, LANE), 0)
    lane = lax.broadcasted_iota(jnp.int32, (1, LANE), 1)
    lists = jnp.zeros((4 * list_rows, LANE), jnp.float32)
    for k in range(chunks):
        own = member[k] * mine
        place = jnp.sum(own * (rank[k] + base), axis=0, keepdims=True).astype(jnp.int32)
        at = jnp.sum(own * (start[k] + begin), axis=0, keepdims=True).astype(jnp.int32)
        used = jnp.sum(own, axis=0, keepdims=True) > 0
        block = k * LANE + lane
        far = (block >= half) != (tile_index == 1)
        block = jnp.where(block >= half, block - half, block) + jnp.where(far, 2048, 0)
        word = at * 4096 + block
        at_row = list_row == jnp.where(used, place // LANE, -1)
        at_col = (list_col == place % LANE).astype(jnp.float32).astype(jnp.bfloat16)
        spread = jnp.concatenate(
            [
                jnp.where(at_row, ((word >> (8 * part)) & 255).astype(jnp.float32), 0.0)
                for part in range(4)
            ],
            axis=0,
        ).astype(jnp.bfloat16)
        lists = lists + lax.dot_general(spread, at_col, NT, preferred_element_type=jnp.float32)
    lists = lists.astype(jnp.int32)
    words = jnp.zeros((list_rows, LANE), jnp.int32)
    for part in range(4):
        words = words + (lists[part * list_rows : (part + 1) * list_rows] << (8 * part))
    word_ref[...] = words

    own_slot = 2 * tm_index + tile_index
    scalar_ref[0] = rung
    scalar_ref[1] = tm_index
    scalar_ref[2] = jnp.sum(jnp.where(slot == own_slot, pixels, 0.0)[:, :1]).astype(jnp.int32)
    for group in range(GROUPS + 1):
        ahead = jnp.where(turn * GROUPS < group * (slots // 2), count * mine, 0.0)
        scalar_ref[3 + group] = jnp.sum(ahead[:, :1]).astype(jnp.int32)


def widen_kernel(in_ref, out_ref):
    frames, half, _ = in_ref.shape

    def widen(i, _):
        begin = pl.multiple_of(i * STEP, STEP)
        rows = in_ref[:, pl.ds(begin, STEP), :].astype(jnp.float32)
        out_ref[pl.ds(begin, STEP)] = jnp.transpose(rows, (1, 0, 2))
        return 0

    lax.fori_loop(0, half // STEP, widen, 0)


def pack_kernel(group, word_ref, scalar_ref, near_ref, far_ref, after_ref, *rest):
    out_refs, stage = rest[:-1], rest[-1]
    depth = out_refs[0].shape[0]
    frames = near_ref.shape[1]
    first_row = group * len(out_refs) * (depth // frames)
    lane = lax.broadcasted_iota(jnp.int32, (frames, LANE), 1)

    def place(i, count, carry):
        held, spill, last = carry
        turned, row, shift = [], [], []
        for j in range(count):
            word = word_ref[i + j]
            block = word & 2047
            x = jnp.where((word & 2048) == 0, near_ref[block], far_ref[block])
            row.append((word >> 19) - first_row)
            shift.append((word >> 12) & (LANE - 1))
            turned.append(pltpu.roll(x, shift[j], 1))
        for j in range(count):
            held = jnp.where(
                lane >= shift[j], turned[j], jnp.where(row[j] == last, held, spill)
            )
            spill, last = turned[j], row[j]
            at = pl.multiple_of(last * frames, frames)
            stage[pl.ds(at, frames), :] = held
            stage[pl.ds(at + frames, frames), :] = spill
        return held, spill, last

    begin, end = scalar_ref[3 + group], scalar_ref[4 + group]
    zero = jnp.zeros((frames, LANE), jnp.float32)
    carry = (zero, zero, jnp.int32(-1))
    groups = (end - begin) // UNROLL
    carry = lax.fori_loop(0, groups, lambda i, c: place(begin + i * UNROLL, UNROLL, c), carry)
    lax.fori_loop(begin + groups * UNROLL, end, lambda i, c: place(i, 1, c), carry)
    for d, out_ref in enumerate(out_refs):
        out_ref[...] = stage[d * depth : (d + 1) * depth, :].astype(jnp.bfloat16)


def gram_kernel(scalar_ref, *refs):
    x_refs, (out_ref, turn) = refs[:-2], refs[-2:]
    sources = len(x_refs)
    frames = out_ref.shape[0]
    local = frames // sources
    pixels = scalar_ref[2]
    tm_index = scalar_ref[1]
    lane = lax.broadcasted_iota(jnp.int32, (1, LANE), 1)

    def pair(j, carry):
        gram, total = carry
        rows = pl.ds(pl.multiple_of(j * 2 * local, 2 * local), 2 * local)
        both = [ref[rows, :].astype(jnp.float32) for ref in x_refs]
        exact, high, low = [], [], []
        for i in range(2):
            used = lane + (2 * j + i) * LANE < pixels
            x = jnp.concatenate([part[i * local : (i + 1) * local] for part in both], axis=0)
            x = jnp.where(used, x, 0.0)
            mean = jnp.where(used, jnp.sum(x, axis=0, keepdims=True) / frames, 1.0)
            scale = 1.0 / mean
            total = total + x * scale
            y = x * (scale * scale)
            top = y.astype(jnp.bfloat16)
            exact.append(x.astype(jnp.bfloat16))
            high.append(top)
            low.append((y - top.astype(jnp.float32)).astype(jnp.bfloat16))
        left = jnp.concatenate(exact, axis=1)
        right = jnp.concatenate(
            [jnp.concatenate(high, axis=1), jnp.concatenate(low, axis=1)], axis=0
        )
        gram = gram + lax.dot_general(left, right, NT, preferred_element_type=jnp.float32)
        return gram, total

    def two_pairs(j, carry):
        return pair(2 * j + 1, pair(2 * j, carry))

    def in_order(value):
        for j in range(sources):
            at = pl.multiple_of((tm_index ^ apart_of(j, sources)) * local, local)
            turn[pl.ds(at, local), :] = value[j * local : (j + 1) * local]
        return turn[...]

    carry = (jnp.zeros((frames, 2 * frames), jnp.float32), jnp.zeros((frames, LANE), jnp.float32))
    pairs = (pixels + 2 * LANE - 1) // (2 * LANE)
    carry = lax.fori_loop(0, pairs // 2, two_pairs, carry)
    gram, total = lax.fori_loop(pairs // 2 * 2, pairs, pair, carry)
    gram = in_order(gram[:, :frames] + gram[:, frames:])
    gram = in_order(gram.T)
    total = in_order(total)
    first = jnp.sum(total, axis=1, keepdims=True)
    second = jnp.sum(total.T, axis=0, keepdims=True)
    out_ref[...] = pixels.astype(jnp.float32) * gram / (first * second)


def on_device_routed(frames, block_cycle, block_valid, cycle_owner):
    tm_count = lax.axis_size("tm")
    local_frames, half, _ = frames.shape
    frame_count = tm_count * local_frames
    list_rows = -(-block_cycle.shape[0] // (8 * LANE)) * 8
    vmem = pl.BlockSpec(memory_space=pltpu.VMEM)
    smem = pl.BlockSpec(memory_space=pltpu.SMEM)
    params = pltpu.CompilerParams(vmem_limit_bytes=VMEM_LIMIT)

    def widen(part):
        return pl.pallas_call(
            widen_kernel,
            out_shape=jax.ShapeDtypeStruct((half, local_frames, LANE), jnp.float32),
            in_specs=[vmem],
            out_specs=vmem,
            compiler_params=params,
            name="widen",
        )(part)

    far = lax.ppermute(frames, "tile", [(0, 1), (1, 0)])
    words, scalars = pl.pallas_call(
        plan_kernel,
        out_shape=(
            jax.ShapeDtypeStruct((list_rows, LANE), jnp.int32),
            jax.ShapeDtypeStruct((4 + GROUPS,), jnp.int32),
        ),
        in_specs=[pl.BlockSpec(memory_space=pltpu.HBM)] * 3,
        out_specs=(vmem, smem),
        scratch_shapes=[
            pltpu.SMEM(cycle_owner.shape, jnp.int32),
            pltpu.VMEM(block_cycle.shape, jnp.int32),
            pltpu.VMEM(block_valid.shape, jnp.int32),
            pltpu.SemaphoreType.DMA((3,)),
        ],
        compiler_params=params,
        name="plan",
    )(cycle_owner, block_cycle, block_valid)
    near_pool = widen(frames)
    far_pool = widen(far)
    members = tm_count // GROUPS

    def branch(size):
        depth = size * local_frames

        def run(words, scalars, near_pool, far_pool):
            got = []
            after = scalars
            for group in range(GROUPS):
                send = pl.pallas_call(
                    functools.partial(pack_kernel, group),
                    out_shape=(jax.ShapeDtypeStruct((depth, LANE), jnp.bfloat16),) * members,
                    in_specs=[smem, smem, vmem, vmem, pl.BlockSpec(memory_space=pl.ANY)],
                    out_specs=(vmem,) * members,
                    scratch_shapes=[pltpu.VMEM((members * depth + local_frames, LANE), jnp.float32)],
                    compiler_params=params,
                    cost_estimate=pl.CostEstimate(
                        flops=2_000_000, bytes_accessed=16_000_000, transcendentals=0
                    ),
                    name="pack",
                )(words, scalars, near_pool, far_pool, after)
                after = send[-1]
                for j in range(members):
                    apart = apart_of(group * members + j, tm_count)
                    pairs = [(i, i ^ apart) for i in range(tm_count)]
                    got.append(lax.ppermute(send[j], "tm", pairs) if apart else send[j])
            return pl.pallas_call(
                gram_kernel,
                out_shape=jax.ShapeDtypeStruct((frame_count, frame_count), jnp.float32),
                in_specs=[smem] + [vmem] * tm_count,
                out_specs=vmem,
                scratch_shapes=[pltpu.VMEM((frame_count, LANE), jnp.float32)],
                compiler_params=params,
                name="gram",
            )(scalars, *got)

        return run

    return lax.switch(
        scalars[0],
        [branch(size) for size in LADDER],
        words.reshape(-1),
        scalars,
        near_pool,
        far_pool,
    )


def normalize(pixel_intensity, valid_count, lanes):
    lane_index = jnp.arange(lanes, dtype=jnp.int32)
    valid_mask = lane_index[None, :] < valid_count[:, None]
    pixel_mean = jnp.sum(pixel_intensity, axis=0) / pixel_intensity.shape[0]
    guarded_average = jnp.where(valid_mask, pixel_mean, jnp.float32(1.0))
    return jnp.where(valid_mask[None], pixel_intensity / guarded_average[None], jnp.float32(0.0))


def on_device_summed(frames, block_cycle, block_valid, cycle_owner):
    tm_count = lax.axis_size("tm")
    tile_count = lax.axis_size("tile")
    tm_index = lax.axis_index("tm")
    tile_index = lax.axis_index("tile")
    local_frames = frames.shape[0]
    half = frames.shape[1]
    lanes = frames.shape[2]
    cycle_count = cycle_owner.shape[0]
    frame_count = local_frames * tm_count
    cycle_range = jnp.arange(cycle_count, dtype=jnp.int32)
    member_all = (block_cycle[None, :] == cycle_owner[:, None]).astype(jnp.float32)
    pixel_total = jnp.dot(
        member_all, block_valid.astype(jnp.float32), precision=lax.Precision.HIGHEST
    )
    row_count = cycle_count * frame_count // (tm_count * tile_count)
    block_local = half // tm_count
    reshaped = frames.reshape(local_frames, tm_count, block_local, lanes)
    arrived = lax.all_to_all(reshaped, "tm", split_axis=1, concat_axis=0, tiled=True)
    pixel_intensity = arrived.reshape(frame_count, block_local, lanes).astype(jnp.float32)
    offset = (tile_index * tm_count + tm_index) * block_local
    cycle_ids = lax.dynamic_slice_in_dim(block_cycle, offset, block_local, 0)
    valid_count = lax.dynamic_slice_in_dim(block_valid, offset, block_local, 0)
    members = (cycle_ids[None, :] == cycle_owner[:, None]).astype(jnp.float32)
    normalized_frames = normalize(pixel_intensity, valid_count, lanes)
    gram_matrices = jnp.einsum(
        "rnk,jnk->nrj", normalized_frames, normalized_frames, precision=lax.Precision.HIGHEST
    )
    partial_value = jnp.dot(
        members,
        gram_matrices.reshape(block_local, frame_count * frame_count),
        precision=lax.Precision.HIGHEST,
    )
    partial_value = partial_value.reshape(cycle_count * frame_count, frame_count)
    frame_sums = jnp.dot(
        members, jnp.sum(normalized_frames, axis=2).T, precision=lax.Precision.HIGHEST
    )
    owned = lax.psum_scatter(partial_value, ("tm", "tile"), scatter_dimension=0, tiled=True)
    frame_total = lax.psum(frame_sums, ("tm", "tile"))
    row_start = (tm_index * tile_count + tile_index) * row_count
    row_global = row_start + jnp.arange(row_count, dtype=jnp.int32)
    slot_index = row_global // frame_count
    frame_time_index = row_global % frame_count
    select = (slot_index[:, None] == cycle_range[None, :]).astype(jnp.float32)
    row_sums = jnp.dot(select, frame_total, precision=lax.Precision.HIGHEST)
    row_pixels = jnp.dot(select, pixel_total, precision=lax.Precision.HIGHEST)
    time_pick = (
        jnp.arange(frame_count, dtype=jnp.int32)[None, :] == frame_time_index[:, None]
    ).astype(jnp.float32)
    first_sums = jnp.sum(row_sums * time_pick, axis=1)
    return row_pixels[:, None] * owned / (first_sums[:, None] * row_sums)


def solution(mesh):
    in_specs = (P("tm", ("series", "tile"), None), P("series"), P("series"), P())
    out_specs = P(("series", "tm", "tile"), None)

    def on_device(frames, block_cycle, block_valid, cycle_owner):
        routed = (
            mesh.shape["tile"] == 2
            and mesh.shape["tm"] * 2 == cycle_owner.shape[0]
            and frames.shape[0] == 8
            and mesh.shape["tm"] * 8 == LANE
            and block_cycle.shape[0] <= 4096
        )
        body = on_device_routed if routed else on_device_summed
        return body(frames, block_cycle, block_valid, cycle_owner)

    return jax.shard_map(
        on_device, mesh=mesh, in_specs=in_specs, out_specs=out_specs, check_vma=False
    )
```

```python
import functools

import jax
import jax.numpy as jnp
from jax import lax
from jax.experimental import pallas as pl
from jax.experimental.pallas import tpu as pltpu
from jax.sharding import PartitionSpec as P

LANE = 128
UNROLL = 16
GROUPS = 2
STEP = 128
VMEM_LIMIT = 24 * 1024 * 1024
LADDER = (16, 24, 32, 36, 40, 42, 44, 46, 48, 52, 56, 64, 80, 104, 144)
NT = (((1,), (1,)), ((), ()))


def apart_of(turn, count):
    side = count // 2
    return (side if turn % 2 == 0 else 0) + side - 1 - turn // 2


def plan_kernel(
    owner_in, cycle_in, valid_in, word_ref, scalar_ref, owner_ref, cycle_ref, valid_ref, arrived
):
    tm_index, tile_index = lax.axis_index("tm"), lax.axis_index("tile")
    fetches = [
        pltpu.make_async_copy(source, target, arrived.at[i])
        for i, (source, target) in enumerate(
            ((owner_in, owner_ref), (cycle_in, cycle_ref), (valid_in, valid_ref))
        )
    ]
    for fetch in fetches:
        fetch.start()
    for fetch in fetches:
        fetch.wait()
    chunks = cycle_ref.shape[0] // LANE
    slots = owner_ref.shape[0]
    half = cycle_ref.shape[0] // 2
    list_rows = word_ref.shape[0]
    slot = lax.broadcasted_iota(jnp.int32, (slots, LANE), 0)
    mine = (slot % 2 == tile_index).astype(jnp.float32)
    owner = jnp.zeros((slots, LANE), jnp.int32)
    for s in range(slots):
        owner = jnp.where(slot == s, owner_ref[s], owner)

    member, weighted = [], []
    for k in range(chunks):
        cut = slice(k * LANE, (k + 1) * LANE)
        hit = (cycle_ref[cut].reshape(1, LANE) == owner).astype(jnp.float32)
        member.append(hit)
        weighted.append(hit * valid_ref[cut].reshape(1, LANE).astype(jnp.float32))
    stacked = jnp.concatenate(member + weighted, axis=0).astype(jnp.bfloat16)
    before = lax.broadcasted_iota(jnp.int32, (LANE, 2 * LANE), 0)
    column = lax.broadcasted_iota(jnp.int32, (LANE, 2 * LANE), 1)
    prefix = ((before < column) | (column >= LANE)).astype(jnp.float32).astype(jnp.bfloat16)
    sums = jnp.dot(stacked, prefix, preferred_element_type=jnp.float32)

    count = jnp.zeros((slots, LANE), jnp.float32)
    pixels = jnp.zeros((slots, LANE), jnp.float32)
    rank, start = [], []
    for k in range(chunks):
        low = slice(k * slots, (k + 1) * slots)
        high = slice((chunks + k) * slots, (chunks + k + 1) * slots)
        rank.append(count + sums[low, :LANE])
        start.append(pixels + sums[high, :LANE])
        count = count + sums[low, LANE:]
        pixels = pixels + sums[high, LANE:]

    rows = (jnp.max(pixels).astype(jnp.int32) + LANE - 1) // LANE
    rung = jnp.int32(0)
    size = jnp.int32(LADDER[0])
    for smaller, larger in zip(LADDER[:-1], LADDER[1:]):
        rung = rung + (rows > smaller).astype(jnp.int32)
        size = jnp.where(rows > smaller, larger, size)

    def turn_of(index):
        apart = (index // 2) ^ tm_index
        side = slots // 4
        return 2 * (side - 1 - apart % side) + (apart < side).astype(jnp.int32)

    row = turn_of(lax.broadcasted_iota(jnp.int32, (slots, slots), 0))
    index = lax.broadcasted_iota(jnp.int32, (slots, slots), 1)
    earlier = ((turn_of(index) < row) & (index % 2 == tile_index)).astype(jnp.float32)
    turn = turn_of(slot)
    base = jnp.dot(
        earlier, count, precision=lax.Precision.HIGHEST, preferred_element_type=jnp.float32
    )
    begin = (turn * size * LANE).astype(jnp.float32)

    list_row = lax.broadcasted_iota(jnp.int32, (list_rows, LANE), 0)
    list_col = lax.broadcasted_iota(jnp.int32, (LANE, LANE), 0)
    lane = lax.broadcasted_iota(jnp.int32, (1, LANE), 1)
    lists = jnp.zeros((4 * list_rows, LANE), jnp.float32)
    for k in range(chunks):
        own = member[k] * mine
        place = jnp.sum(own * (rank[k] + base), axis=0, keepdims=True).astype(jnp.int32)
        at = jnp.sum(own * (start[k] + begin), axis=0, keepdims=True).astype(jnp.int32)
        used = jnp.sum(own, axis=0, keepdims=True) > 0
        block = k * LANE + lane
        far = (block >= half) != (tile_index == 1)
        block = jnp.where(block >= half, block - half, block) + jnp.where(far, 2048, 0)
        word = at * 4096 + block
        at_row = list_row == jnp.where(used, place // LANE, -1)
        at_col = (list_col == place % LANE).astype(jnp.float32).astype(jnp.bfloat16)
        spread = jnp.concatenate(
            [
                jnp.where(at_row, ((word >> (8 * part)) & 255).astype(jnp.float32), 0.0)
                for part in range(4)
            ],
            axis=0,
        ).astype(jnp.bfloat16)
        lists = lists + lax.dot_general(spread, at_col, NT, preferred_element_type=jnp.float32)
    lists = lists.astype(jnp.int32)
    words = jnp.zeros((list_rows, LANE), jnp.int32)
    for part in range(4):
        words = words + (lists[part * list_rows : (part + 1) * list_rows] << (8 * part))
    index = LANE * lax.broadcasted_iota(jnp.int32, (list_rows, LANE), 0)
    index = index + lax.broadcasted_iota(jnp.int32, (list_rows, LANE), 1)
    total = jnp.sum(count[:, :1] * mine[:, :1]).astype(jnp.int32)
    word_ref[...] = jnp.where(index < total, words, (slots // 2 * size) << 19)

    own_slot = 2 * tm_index + tile_index
    scalar_ref[0] = rung
    scalar_ref[1] = tm_index
    scalar_ref[2] = jnp.sum(jnp.where(slot == own_slot, pixels, 0.0)[:, :1]).astype(jnp.int32)
    for group in range(GROUPS + 1):
        ahead = jnp.where(turn * GROUPS < group * (slots // 2), count * mine, 0.0)
        scalar_ref[3 + group] = jnp.sum(ahead[:, :1]).astype(jnp.int32)


def widen_kernel(in_ref, out_ref):
    frames, half, _ = in_ref.shape

    def widen(i, _):
        begin = pl.multiple_of(i * STEP, STEP)
        rows = in_ref[:, pl.ds(begin, STEP), :].astype(jnp.float32)
        out_ref[pl.ds(begin, STEP)] = jnp.transpose(rows, (1, 0, 2))
        return 0

    lax.fori_loop(0, half // STEP, widen, 0)


def pack_kernel(group, word_ref, scalar_ref, near_ref, far_ref, after_ref, *rest):
    out_refs, stage = rest[:-1], rest[-1]
    depth = out_refs[0].shape[0]
    frames = near_ref.shape[1]
    first_row = group * len(out_refs) * (depth // frames)
    lane = lax.broadcasted_iota(jnp.int32, (frames, LANE), 1)

    begin, end = scalar_ref[3 + group], scalar_ref[4 + group]
    spare = len(out_refs) * (depth // frames)

    def fetch(at):
        turned = []
        for j in range(UNROLL):
            word = word_ref[at + j]
            block = word & 2047
            x = jnp.where((word & 2048) == 0, near_ref[block], far_ref[block])
            turned.append(pltpu.roll(x, (word >> 12) & (LANE - 1), 1))
        return turned

    def place(i, carry):
        held, spill, last, turned = carry
        at = begin + i * UNROLL
        coming = fetch(at + UNROLL)
        for j in range(UNROLL):
            word = word_ref[at + j]
            row = jnp.minimum((word >> 19) - first_row, spare)
            own = lane >= ((word >> 12) & (LANE - 1))
            fresh = jnp.where(own, turned[j], spill)
            held = jnp.where(own | (row != last), fresh, held)
            spill, last = turned[j], row
            to = pl.multiple_of(row * frames, frames)
            stage[pl.ds(to, frames), :] = held
            stage[pl.ds(to + frames, frames), :] = spill
        return held, spill, last, coming

    zero = jnp.zeros((frames, LANE), jnp.float32)
    carry = (zero, zero, jnp.int32(-1), fetch(begin))
    lax.fori_loop(0, (end - begin + UNROLL - 1) // UNROLL, place, carry)
    for d, out_ref in enumerate(out_refs):
        out_ref[...] = stage[d * depth : (d + 1) * depth, :].astype(jnp.bfloat16)


def gram_kernel(scalar_ref, *refs):
    x_refs, (out_ref, turn) = refs[:-2], refs[-2:]
    sources = len(x_refs)
    frames = out_ref.shape[0]
    local = frames // sources
    pixels = scalar_ref[2]
    tm_index = scalar_ref[1]
    lane = lax.broadcasted_iota(jnp.int32, (1, LANE), 1)

    def pair(j, carry):
        gram, total = carry
        rows = pl.ds(pl.multiple_of(j * 2 * local, 2 * local), 2 * local)
        both = [ref[rows, :].astype(jnp.float32) for ref in x_refs]
        exact, high, low = [], [], []
        for i in range(2):
            used = lane + (2 * j + i) * LANE < pixels
            x = jnp.concatenate([part[i * local : (i + 1) * local] for part in both], axis=0)
            x = jnp.where(used, x, 0.0)
            mean = jnp.where(used, jnp.sum(x, axis=0, keepdims=True) / frames, 1.0)
            scale = 1.0 / mean
            total = total + x * scale
            y = x * (scale * scale)
            top = y.astype(jnp.bfloat16)
            exact.append(x.astype(jnp.bfloat16))
            high.append(top)
            low.append((y - top.astype(jnp.float32)).astype(jnp.bfloat16))
        left = jnp.concatenate(exact, axis=1)
        right = jnp.concatenate(
            [jnp.concatenate(high, axis=1), jnp.concatenate(low, axis=1)], axis=0
        )
        gram = gram + lax.dot_general(left, right, NT, preferred_element_type=jnp.float32)
        return gram, total

    def two_pairs(j, carry):
        return pair(2 * j + 1, pair(2 * j, carry))

    def in_order(value):
        for j in range(sources):
            at = pl.multiple_of((tm_index ^ apart_of(j, sources)) * local, local)
            turn[pl.ds(at, local), :] = value[j * local : (j + 1) * local]
        return turn[...]

    carry = (jnp.zeros((frames, 2 * frames), jnp.float32), jnp.zeros((frames, LANE), jnp.float32))
    pairs = (pixels + 2 * LANE - 1) // (2 * LANE)
    carry = lax.fori_loop(0, pairs // 2, two_pairs, carry)
    gram, total = lax.fori_loop(pairs // 2 * 2, pairs, pair, carry)
    gram = in_order(gram[:, :frames] + gram[:, frames:])
    gram = in_order(gram.T)
    total = in_order(total)
    first = jnp.sum(total, axis=1, keepdims=True)
    second = jnp.sum(total.T, axis=0, keepdims=True)
    out_ref[...] = pixels.astype(jnp.float32) * gram / (first * second)


def on_device_routed(frames, block_cycle, block_valid, cycle_owner):
    tm_count = lax.axis_size("tm")
    local_frames, half, _ = frames.shape
    frame_count = tm_count * local_frames
    list_rows = -(-(block_cycle.shape[0] + 2 * UNROLL) // (8 * LANE)) * 8
    vmem = pl.BlockSpec(memory_space=pltpu.VMEM)
    smem = pl.BlockSpec(memory_space=pltpu.SMEM)
    params = pltpu.CompilerParams(vmem_limit_bytes=VMEM_LIMIT)

    def widen(part):
        return pl.pallas_call(
            widen_kernel,
            out_shape=jax.ShapeDtypeStruct((half, local_frames, LANE), jnp.float32),
            in_specs=[vmem],
            out_specs=vmem,
            compiler_params=params,
            name="widen",
        )(part)

    far = lax.ppermute(frames, "tile", [(0, 1), (1, 0)])
    words, scalars = pl.pallas_call(
        plan_kernel,
        out_shape=(
            jax.ShapeDtypeStruct((list_rows, LANE), jnp.int32),
            jax.ShapeDtypeStruct((4 + GROUPS,), jnp.int32),
        ),
        in_specs=[pl.BlockSpec(memory_space=pltpu.HBM)] * 3,
        out_specs=(vmem, smem),
        scratch_shapes=[
            pltpu.SMEM(cycle_owner.shape, jnp.int32),
            pltpu.VMEM(block_cycle.shape, jnp.int32),
            pltpu.VMEM(block_valid.shape, jnp.int32),
            pltpu.SemaphoreType.DMA((3,)),
        ],
        compiler_params=params,
        name="plan",
    )(cycle_owner, block_cycle, block_valid)
    near_pool = widen(frames)
    far_pool = widen(far)
    members = tm_count // GROUPS

    def branch(size):
        depth = size * local_frames

        def run(words, scalars, near_pool, far_pool):
            got = []
            after = scalars
            for group in range(GROUPS):
                send = pl.pallas_call(
                    functools.partial(pack_kernel, group),
                    out_shape=(jax.ShapeDtypeStruct((depth, LANE), jnp.bfloat16),) * members,
                    in_specs=[smem, smem, vmem, vmem, pl.BlockSpec(memory_space=pl.ANY)],
                    out_specs=(vmem,) * members,
                    scratch_shapes=[
                        pltpu.VMEM((members * depth + 2 * local_frames, LANE), jnp.float32)
                    ],
                    compiler_params=params,
                    cost_estimate=pl.CostEstimate(
                        flops=2_000_000, bytes_accessed=16_000_000, transcendentals=0
                    ),
                    name="pack",
                )(words, scalars, near_pool, far_pool, after)
                after = send[-1]
                for j in range(members):
                    apart = apart_of(group * members + j, tm_count)
                    pairs = [(i, i ^ apart) for i in range(tm_count)]
                    got.append(lax.ppermute(send[j], "tm", pairs) if apart else send[j])
            return pl.pallas_call(
                gram_kernel,
                out_shape=jax.ShapeDtypeStruct((frame_count, frame_count), jnp.float32),
                in_specs=[smem] + [vmem] * tm_count,
                out_specs=vmem,
                scratch_shapes=[pltpu.VMEM((frame_count, LANE), jnp.float32)],
                compiler_params=params,
                name="gram",
            )(scalars, *got)

        return run

    return lax.switch(
        scalars[0],
        [branch(size) for size in LADDER],
        words.reshape(-1),
        scalars,
        near_pool,
        far_pool,
    )


def normalize(pixel_intensity, valid_count, lanes):
    lane_index = jnp.arange(lanes, dtype=jnp.int32)
    valid_mask = lane_index[None, :] < valid_count[:, None]
    pixel_mean = jnp.sum(pixel_intensity, axis=0) / pixel_intensity.shape[0]
    guarded_average = jnp.where(valid_mask, pixel_mean, jnp.float32(1.0))
    return jnp.where(valid_mask[None], pixel_intensity / guarded_average[None], jnp.float32(0.0))


def on_device_summed(frames, block_cycle, block_valid, cycle_owner):
    tm_count = lax.axis_size("tm")
    tile_count = lax.axis_size("tile")
    tm_index = lax.axis_index("tm")
    tile_index = lax.axis_index("tile")
    local_frames = frames.shape[0]
    half = frames.shape[1]
    lanes = frames.shape[2]
    cycle_count = cycle_owner.shape[0]
    frame_count = local_frames * tm_count
    cycle_range = jnp.arange(cycle_count, dtype=jnp.int32)
    member_all = (block_cycle[None, :] == cycle_owner[:, None]).astype(jnp.float32)
    pixel_total = jnp.dot(
        member_all, block_valid.astype(jnp.float32), precision=lax.Precision.HIGHEST
    )
    row_count = cycle_count * frame_count // (tm_count * tile_count)
    block_local = half // tm_count
    reshaped = frames.reshape(local_frames, tm_count, block_local, lanes)
    arrived = lax.all_to_all(reshaped, "tm", split_axis=1, concat_axis=0, tiled=True)
    pixel_intensity = arrived.reshape(frame_count, block_local, lanes).astype(jnp.float32)
    offset = (tile_index * tm_count + tm_index) * block_local
    cycle_ids = lax.dynamic_slice_in_dim(block_cycle, offset, block_local, 0)
    valid_count = lax.dynamic_slice_in_dim(block_valid, offset, block_local, 0)
    members = (cycle_ids[None, :] == cycle_owner[:, None]).astype(jnp.float32)
    normalized_frames = normalize(pixel_intensity, valid_count, lanes)
    gram_matrices = jnp.einsum(
        "rnk,jnk->nrj", normalized_frames, normalized_frames, precision=lax.Precision.HIGHEST
    )
    partial_value = jnp.dot(
        members,
        gram_matrices.reshape(block_local, frame_count * frame_count),
        precision=lax.Precision.HIGHEST,
    )
    partial_value = partial_value.reshape(cycle_count * frame_count, frame_count)
    frame_sums = jnp.dot(
        members, jnp.sum(normalized_frames, axis=2).T, precision=lax.Precision.HIGHEST
    )
    owned = lax.psum_scatter(partial_value, ("tm", "tile"), scatter_dimension=0, tiled=True)
    frame_total = lax.psum(frame_sums, ("tm", "tile"))
    row_start = (tm_index * tile_count + tile_index) * row_count
    row_global = row_start + jnp.arange(row_count, dtype=jnp.int32)
    slot_index = row_global // frame_count
    frame_time_index = row_global % frame_count
    select = (slot_index[:, None] == cycle_range[None, :]).astype(jnp.float32)
    row_sums = jnp.dot(select, frame_total, precision=lax.Precision.HIGHEST)
    row_pixels = jnp.dot(select, pixel_total, precision=lax.Precision.HIGHEST)
    time_pick = (
        jnp.arange(frame_count, dtype=jnp.int32)[None, :] == frame_time_index[:, None]
    ).astype(jnp.float32)
    first_sums = jnp.sum(row_sums * time_pick, axis=1)
    return row_pixels[:, None] * owned / (first_sums[:, None] * row_sums)


def solution(mesh):
    in_specs = (P("tm", ("series", "tile"), None), P("series"), P("series"), P())
    out_specs = P(("series", "tm", "tile"), None)

    def on_device(frames, block_cycle, block_valid, cycle_owner):
        routed = (
            mesh.shape["tile"] == 2
            and mesh.shape["tm"] * 2 == cycle_owner.shape[0]
            and frames.shape[0] == 8
            and mesh.shape["tm"] * 8 == LANE
            and block_cycle.shape[0] <= 4096
        )
        body = on_device_routed if routed else on_device_summed
        return body(frames, block_cycle, block_valid, cycle_owner)

    return jax.shard_map(
        on_device, mesh=mesh, in_specs=in_specs, out_specs=out_specs, check_vma=False
    )
```

```python
import functools

import jax
import jax.numpy as jnp
from jax import lax
from jax.experimental import pallas as pl
from jax.experimental.pallas import tpu as pltpu
from jax.sharding import PartitionSpec as P

LANE = 128
UNROLL = 32
GROUPS = 2
STEP = 128
VMEM_LIMIT = 24 * 1024 * 1024
LADDER = (24, 32, 36, 40, 42, 44, 46, 50, 64, 96, 144)
NT = (((1,), (1,)), ((), ()))


def apart_of(turn, count):
    side = count // 2
    return (side if turn % 2 == 0 else 0) + side - 1 - turn // 2


def plan_kernel(
    owner_in, cycle_in, valid_in, word_ref, scalar_ref, owner_ref, cycle_ref, valid_ref, arrived
):
    tm_index, tile_index = lax.axis_index("tm"), lax.axis_index("tile")
    fetches = [
        pltpu.make_async_copy(source, target, arrived.at[i])
        for i, (source, target) in enumerate(
            ((owner_in, owner_ref), (cycle_in, cycle_ref), (valid_in, valid_ref))
        )
    ]
    for fetch in fetches:
        fetch.start()
    for fetch in fetches:
        fetch.wait()
    chunks = cycle_ref.shape[0] // LANE
    slots = owner_ref.shape[0]
    half = cycle_ref.shape[0] // 2
    list_rows = word_ref.shape[0]
    slot = lax.broadcasted_iota(jnp.int32, (slots, LANE), 0)
    mine = (slot % 2 == tile_index).astype(jnp.float32)
    owner = jnp.zeros((slots, LANE), jnp.int32)
    for s in range(slots):
        owner = jnp.where(slot == s, owner_ref[s], owner)

    member, weighted = [], []
    for k in range(chunks):
        cut = slice(k * LANE, (k + 1) * LANE)
        hit = (cycle_ref[cut].reshape(1, LANE) == owner).astype(jnp.float32)
        member.append(hit)
        weighted.append(hit * valid_ref[cut].reshape(1, LANE).astype(jnp.float32))
    stacked = jnp.concatenate(member + weighted, axis=0).astype(jnp.bfloat16)
    before = lax.broadcasted_iota(jnp.int32, (LANE, 2 * LANE), 0)
    column = lax.broadcasted_iota(jnp.int32, (LANE, 2 * LANE), 1)
    prefix = ((before < column) | (column >= LANE)).astype(jnp.float32).astype(jnp.bfloat16)
    sums = jnp.dot(stacked, prefix, preferred_element_type=jnp.float32)

    count = jnp.zeros((slots, LANE), jnp.float32)
    pixels = jnp.zeros((slots, LANE), jnp.float32)
    rank, start = [], []
    for k in range(chunks):
        low = slice(k * slots, (k + 1) * slots)
        high = slice((chunks + k) * slots, (chunks + k + 1) * slots)
        rank.append(count + sums[low, :LANE])
        start.append(pixels + sums[high, :LANE])
        count = count + sums[low, LANE:]
        pixels = pixels + sums[high, LANE:]

    rows = (jnp.max(pixels).astype(jnp.int32) + LANE - 1) // LANE
    rung = jnp.int32(0)
    size = jnp.int32(LADDER[0])
    for smaller, larger in zip(LADDER[:-1], LADDER[1:]):
        rung = rung + (rows > smaller).astype(jnp.int32)
        size = jnp.where(rows > smaller, larger, size)

    def turn_of(index):
        apart = (index // 2) ^ tm_index
        side = slots // 4
        return 2 * (side - 1 - apart % side) + (apart < side).astype(jnp.int32)

    row = turn_of(lax.broadcasted_iota(jnp.int32, (slots, slots), 0))
    index = lax.broadcasted_iota(jnp.int32, (slots, slots), 1)
    earlier = ((turn_of(index) < row) & (index % 2 == tile_index)).astype(jnp.float32)
    turn = turn_of(slot)
    base = jnp.dot(
        earlier, count, precision=lax.Precision.HIGHEST, preferred_element_type=jnp.float32
    )
    begin = (turn * size * LANE).astype(jnp.float32)

    list_row = lax.broadcasted_iota(jnp.int32, (list_rows, LANE), 0)
    list_col = lax.broadcasted_iota(jnp.int32, (LANE, LANE), 0)
    lane = lax.broadcasted_iota(jnp.int32, (1, LANE), 1)
    lists = jnp.zeros((4 * list_rows, LANE), jnp.float32)
    for k in range(chunks):
        own = member[k] * mine
        place = jnp.sum(own * (rank[k] + base), axis=0, keepdims=True).astype(jnp.int32)
        at = jnp.sum(own * (start[k] + begin), axis=0, keepdims=True).astype(jnp.int32)
        used = jnp.sum(own, axis=0, keepdims=True) > 0
        block = k * LANE + lane
        far = (block >= half) != (tile_index == 1)
        block = jnp.where(block >= half, block - half, block) + jnp.where(far, half, 0)
        pixel_count = jnp.sum(own * weighted[k], axis=0, keepdims=True).astype(jnp.int32)
        wraps = at % LANE + pixel_count >= LANE
        word = at * 4096 + block + jnp.where(wraps, jnp.int32(-(2**31)), 0)
        at_row = list_row == jnp.where(used, place // LANE, -1)
        at_col = (list_col == place % LANE).astype(jnp.float32).astype(jnp.bfloat16)
        spread = jnp.concatenate(
            [
                jnp.where(at_row, ((word >> (8 * part)) & 255).astype(jnp.float32), 0.0)
                for part in range(4)
            ],
            axis=0,
        ).astype(jnp.bfloat16)
        lists = lists + lax.dot_general(spread, at_col, NT, preferred_element_type=jnp.float32)
    lists = lists.astype(jnp.int32)
    words = jnp.zeros((list_rows, LANE), jnp.int32)
    for part in range(4):
        words = words + (lists[part * list_rows : (part + 1) * list_rows] << (8 * part))
    index = LANE * lax.broadcasted_iota(jnp.int32, (list_rows, LANE), 0)
    index = index + lax.broadcasted_iota(jnp.int32, (list_rows, LANE), 1)
    total = jnp.sum(count[:, :1] * mine[:, :1]).astype(jnp.int32)
    word_ref[...] = jnp.where(index < total, words, (slots // 2 * size) << 19)

    own_slot = 2 * tm_index + tile_index
    scalar_ref[0] = rung
    scalar_ref[1] = tm_index
    scalar_ref[2] = jnp.sum(jnp.where(slot == own_slot, pixels, 0.0)[:, :1]).astype(jnp.int32)
    for group in range(GROUPS + 1):
        ahead = jnp.where(turn * GROUPS < group * (slots // 2), count * mine, 0.0)
        scalar_ref[3 + group] = jnp.sum(ahead[:, :1]).astype(jnp.int32)


def widen_kernel(part, in_ref, *rest):
    out_ref = rest[-1]
    half = in_ref.shape[1]

    def widen(i, _):
        begin = pl.multiple_of(i * STEP, STEP)
        rows = in_ref[:, pl.ds(begin, STEP), :].astype(jnp.float32)
        out_ref[pl.ds(part * half + begin, STEP)] = jnp.transpose(rows, (1, 0, 2))
        return 0

    lax.fori_loop(0, half // STEP, widen, 0)


def pack_kernel(group, word_ref, scalar_ref, pool_ref, *rest):
    out_refs, stage = rest[:-1], rest[-1]
    depth = out_refs[0].shape[0]
    frames = pool_ref.shape[1]
    lane = lax.broadcasted_iota(jnp.int32, (frames, LANE), 1)
    begin, end = scalar_ref[3 + group], scalar_ref[4 + group]

    def place(i, held):
        at = begin + i * UNROLL
        turned = []
        for j in range(UNROLL):
            word = word_ref[at + j]
            turned.append(pltpu.roll(pool_ref[word & 4095], (word >> 12) & (LANE - 1), 1))
        for j in range(UNROLL):
            word = word_ref[at + j]
            shift = (word >> 12) & (LANE - 1)
            row = pl.multiple_of((word >> 16) & 0x7FF8, frames)
            stage[pl.ds(row, frames), :] = jnp.where(lane >= shift, turned[j], held)
            stage[pl.ds(row + frames, frames), :] = turned[j]
            held = jnp.where(lane >= jnp.where(word < 0, 0, shift), turned[j], held)
        return held

    held = jnp.zeros((frames, LANE), jnp.float32)
    lax.fori_loop(0, (end - begin + UNROLL - 1) // UNROLL, place, held)

    step = depth if depth <= 512 else LANE
    for d, out_ref in enumerate(out_refs):
        base = (group * len(out_refs) + d) * depth

        def narrow(i, _, out_ref=out_ref, base=base):
            row = pl.multiple_of(i * step, step)
            out_ref[pl.ds(row, step), :] = stage[pl.ds(base + row, step), :].astype(jnp.bfloat16)
            return 0

        if step == depth:
            narrow(0, 0)
        else:
            lax.fori_loop(0, depth // step, narrow, 0)


def gram_kernel(scalar_ref, *refs):
    x_refs, (out_ref, turn) = refs[:-2], refs[-2:]
    sources = len(x_refs)
    frames = out_ref.shape[0]
    local = frames // sources
    pixels = scalar_ref[2]
    tm_index = scalar_ref[1]
    lane = lax.broadcasted_iota(jnp.int32, (1, LANE), 1)

    last = x_refs[0].shape[0] // (2 * local) - 1

    def pair(j, carry):
        gram, total = carry
        rows = pl.ds(pl.multiple_of(jnp.minimum(j, last) * 2 * local, 2 * local), 2 * local)
        both = [ref[rows, :].astype(jnp.float32) for ref in x_refs]
        exact, high, low = [], [], []
        for i in range(2):
            used = lane + (2 * j + i) * LANE < pixels
            x = jnp.concatenate([part[i * local : (i + 1) * local] for part in both], axis=0)
            x = jnp.where(used, x, 0.0)
            mean = jnp.where(used, jnp.sum(x, axis=0, keepdims=True) / frames, 1.0)
            scale = 1.0 / mean
            total = total + x * scale
            y = x * (scale * scale)
            top = y.astype(jnp.bfloat16)
            exact.append(x.astype(jnp.bfloat16))
            high.append(top)
            low.append((y - top.astype(jnp.float32)).astype(jnp.bfloat16))
        left = jnp.concatenate(exact, axis=1)
        right = jnp.concatenate(
            [jnp.concatenate(high, axis=1), jnp.concatenate(low, axis=1)], axis=0
        )
        gram = gram + lax.dot_general(left, right, NT, preferred_element_type=jnp.float32)
        return gram, total

    def two_pairs(j, carry):
        return pair(2 * j + 1, pair(2 * j, carry))

    def in_order(value):
        for j in range(sources):
            at = pl.multiple_of((tm_index ^ apart_of(j, sources)) * local, local)
            turn[pl.ds(at, local), :] = value[j * local : (j + 1) * local]
        return turn[...]

    carry = (jnp.zeros((frames, 2 * frames), jnp.float32), jnp.zeros((frames, LANE), jnp.float32))
    pairs = (pixels + 2 * LANE - 1) // (2 * LANE)
    gram, total = lax.fori_loop(0, (pairs + 1) // 2, two_pairs, carry)
    gram = in_order(gram[:, :frames] + gram[:, frames:])
    gram = in_order(gram.T)
    total = in_order(total)
    first = jnp.sum(total, axis=1, keepdims=True)
    second = jnp.sum(total.T, axis=0, keepdims=True)
    out_ref[...] = pixels.astype(jnp.float32) * gram / (first * second)


def on_device_routed(frames, block_cycle, block_valid, cycle_owner):
    tm_count = lax.axis_size("tm")
    local_frames, half, _ = frames.shape
    frame_count = tm_count * local_frames
    list_rows = -(-(block_cycle.shape[0] + UNROLL) // (8 * LANE)) * 8
    vmem = pl.BlockSpec(memory_space=pltpu.VMEM)
    smem = pl.BlockSpec(memory_space=pltpu.SMEM)
    params = pltpu.CompilerParams(vmem_limit_bytes=VMEM_LIMIT)

    def widen(*given):
        return pl.pallas_call(
            functools.partial(widen_kernel, len(given) - 1),
            out_shape=jax.ShapeDtypeStruct((2 * half, local_frames, LANE), jnp.float32),
            in_specs=[vmem] * len(given),
            out_specs=vmem,
            input_output_aliases={1: 0} if len(given) > 1 else {},
            compiler_params=params,
            name="widen",
        )(*given)

    far = lax.ppermute(frames, "tile", [(0, 1), (1, 0)])
    words, scalars = pl.pallas_call(
        plan_kernel,
        out_shape=(
            jax.ShapeDtypeStruct((list_rows, LANE), jnp.int32),
            jax.ShapeDtypeStruct((4 + GROUPS,), jnp.int32),
        ),
        in_specs=[pl.BlockSpec(memory_space=pltpu.HBM)] * 3,
        out_specs=(vmem, smem),
        scratch_shapes=[
            pltpu.SMEM(cycle_owner.shape, jnp.int32),
            pltpu.VMEM(block_cycle.shape, jnp.int32),
            pltpu.VMEM(block_valid.shape, jnp.int32),
            pltpu.SemaphoreType.DMA((3,)),
        ],
        compiler_params=params,
        name="plan",
    )(cycle_owner, block_cycle, block_valid)
    pool = widen(far, widen(frames))
    members = tm_count // GROUPS

    def branch(size):
        depth = size * local_frames

        def run(words, scalars, pool):
            got = []
            for group in range(GROUPS):
                send = pl.pallas_call(
                    functools.partial(pack_kernel, group),
                    out_shape=(jax.ShapeDtypeStruct((depth, LANE), jnp.bfloat16),) * members,
                    in_specs=[smem, smem, vmem],
                    out_specs=(vmem,) * members,
                    scratch_shapes=[
                        pltpu.VMEM(((tm_count * size + 2) * local_frames, LANE), jnp.float32)
                    ],
                    compiler_params=params,
                    cost_estimate=pl.CostEstimate(
                        flops=2_000_000, bytes_accessed=16_000_000, transcendentals=0
                    ),
                    name="pack",
                )(words, scalars, pool)
                for j in range(members):
                    apart = apart_of(group * members + j, tm_count)
                    pairs = [(i, i ^ apart) for i in range(tm_count)]
                    got.append(lax.ppermute(send[j], "tm", pairs) if apart else send[j])
            return pl.pallas_call(
                gram_kernel,
                out_shape=jax.ShapeDtypeStruct((frame_count, frame_count), jnp.float32),
                in_specs=[smem] + [vmem] * tm_count,
                out_specs=vmem,
                scratch_shapes=[pltpu.VMEM((frame_count, LANE), jnp.float32)],
                compiler_params=params,
                name="gram",
            )(scalars, *got)

        return run

    return lax.switch(
        scalars[0],
        [branch(size) for size in LADDER],
        words.reshape(-1),
        scalars,
        pool,
    )


def normalize(pixel_intensity, valid_count, lanes):
    lane_index = jnp.arange(lanes, dtype=jnp.int32)
    valid_mask = lane_index[None, :] < valid_count[:, None]
    pixel_mean = jnp.sum(pixel_intensity, axis=0) / pixel_intensity.shape[0]
    guarded_average = jnp.where(valid_mask, pixel_mean, jnp.float32(1.0))
    return jnp.where(valid_mask[None], pixel_intensity / guarded_average[None], jnp.float32(0.0))


def on_device_summed(frames, block_cycle, block_valid, cycle_owner):
    tm_count = lax.axis_size("tm")
    tile_count = lax.axis_size("tile")
    tm_index = lax.axis_index("tm")
    tile_index = lax.axis_index("tile")
    local_frames = frames.shape[0]
    half = frames.shape[1]
    lanes = frames.shape[2]
    cycle_count = cycle_owner.shape[0]
    frame_count = local_frames * tm_count
    cycle_range = jnp.arange(cycle_count, dtype=jnp.int32)
    member_all = (block_cycle[None, :] == cycle_owner[:, None]).astype(jnp.float32)
    pixel_total = jnp.dot(
        member_all, block_valid.astype(jnp.float32), precision=lax.Precision.HIGHEST
    )
    row_count = cycle_count * frame_count // (tm_count * tile_count)
    block_local = half // tm_count
    reshaped = frames.reshape(local_frames, tm_count, block_local, lanes)
    arrived = lax.all_to_all(reshaped, "tm", split_axis=1, concat_axis=0, tiled=True)
    pixel_intensity = arrived.reshape(frame_count, block_local, lanes).astype(jnp.float32)
    offset = (tile_index * tm_count + tm_index) * block_local
    cycle_ids = lax.dynamic_slice_in_dim(block_cycle, offset, block_local, 0)
    valid_count = lax.dynamic_slice_in_dim(block_valid, offset, block_local, 0)
    members = (cycle_ids[None, :] == cycle_owner[:, None]).astype(jnp.float32)
    normalized_frames = normalize(pixel_intensity, valid_count, lanes)
    gram_matrices = jnp.einsum(
        "rnk,jnk->nrj", normalized_frames, normalized_frames, precision=lax.Precision.HIGHEST
    )
    partial_value = jnp.dot(
        members,
        gram_matrices.reshape(block_local, frame_count * frame_count),
        precision=lax.Precision.HIGHEST,
    )
    partial_value = partial_value.reshape(cycle_count * frame_count, frame_count)
    frame_sums = jnp.dot(
        members, jnp.sum(normalized_frames, axis=2).T, precision=lax.Precision.HIGHEST
    )
    owned = lax.psum_scatter(partial_value, ("tm", "tile"), scatter_dimension=0, tiled=True)
    frame_total = lax.psum(frame_sums, ("tm", "tile"))
    row_start = (tm_index * tile_count + tile_index) * row_count
    row_global = row_start + jnp.arange(row_count, dtype=jnp.int32)
    slot_index = row_global // frame_count
    frame_time_index = row_global % frame_count
    select = (slot_index[:, None] == cycle_range[None, :]).astype(jnp.float32)
    row_sums = jnp.dot(select, frame_total, precision=lax.Precision.HIGHEST)
    row_pixels = jnp.dot(select, pixel_total, precision=lax.Precision.HIGHEST)
    time_pick = (
        jnp.arange(frame_count, dtype=jnp.int32)[None, :] == frame_time_index[:, None]
    ).astype(jnp.float32)
    first_sums = jnp.sum(row_sums * time_pick, axis=1)
    return row_pixels[:, None] * owned / (first_sums[:, None] * row_sums)


def solution(mesh):
    in_specs = (P("tm", ("series", "tile"), None), P("series"), P("series"), P())
    out_specs = P(("series", "tm", "tile"), None)

    def on_device(frames, block_cycle, block_valid, cycle_owner):
        routed = (
            mesh.shape["tile"] == 2
            and mesh.shape["tm"] * 2 == cycle_owner.shape[0]
            and frames.shape[0] == 8
            and mesh.shape["tm"] * 8 == LANE
            and block_cycle.shape[0] <= 4096
        )
        body = on_device_routed if routed else on_device_summed
        return body(frames, block_cycle, block_valid, cycle_owner)

    return jax.shard_map(
        on_device, mesh=mesh, in_specs=in_specs, out_specs=out_specs, check_vma=False
    )
```

```python
import functools

import jax
import jax.numpy as jnp
from jax import lax
from jax.experimental import pallas as pl
from jax.experimental.pallas import tpu as pltpu
from jax.sharding import PartitionSpec as P

LANE = 128
UNROLL = 32
FIRST = 5
STEP = 128
VMEM_LIMIT = 24 * 1024 * 1024
LADDER = (24, 32, 36, 40, 42, 44, 46, 50, 64, 96, 144)
NT = (((1,), (1,)), ((), ()))


def exchange_order(count):
    side = count // 2
    across = [count - 1 - i for i in range(side)]
    beside = [side - 1 - i for i in range(side)]
    order = across[:3] + beside[:1] + across[3:4]
    for far, near in zip(across[4:], beside[1:]):
        order += [near, far]
    return order + [apart for apart in beside if apart not in order]


def group_ends(count):
    return (0, FIRST, count)


def plan_kernel(
    owner_in, cycle_in, valid_in, word_ref, scalar_ref, owner_ref, cycle_ref, valid_ref, arrived
):
    tm_index, tile_index = lax.axis_index("tm"), lax.axis_index("tile")
    fetches = [
        pltpu.make_async_copy(source, target, arrived.at[i])
        for i, (source, target) in enumerate(
            ((owner_in, owner_ref), (cycle_in, cycle_ref), (valid_in, valid_ref))
        )
    ]
    for fetch in fetches:
        fetch.start()
    for fetch in fetches:
        fetch.wait()
    chunks = cycle_ref.shape[0] // LANE
    slots = owner_ref.shape[0]
    half = cycle_ref.shape[0] // 2
    list_rows = word_ref.shape[0]
    slot = lax.broadcasted_iota(jnp.int32, (slots, LANE), 0)
    mine = (slot % 2 == tile_index).astype(jnp.float32)
    owner = jnp.zeros((slots, LANE), jnp.int32)
    for s in range(slots):
        owner = jnp.where(slot == s, owner_ref[s], owner)

    member, weighted = [], []
    for k in range(chunks):
        cut = slice(k * LANE, (k + 1) * LANE)
        hit = (cycle_ref[cut].reshape(1, LANE) == owner).astype(jnp.float32)
        member.append(hit)
        weighted.append(hit * valid_ref[cut].reshape(1, LANE).astype(jnp.float32))
    stacked = jnp.concatenate(member + weighted, axis=0).astype(jnp.bfloat16)
    before = lax.broadcasted_iota(jnp.int32, (LANE, 2 * LANE), 0)
    column = lax.broadcasted_iota(jnp.int32, (LANE, 2 * LANE), 1)
    prefix = ((before < column) | (column >= LANE)).astype(jnp.float32).astype(jnp.bfloat16)
    sums = jnp.dot(stacked, prefix, preferred_element_type=jnp.float32)

    count = jnp.zeros((slots, LANE), jnp.float32)
    pixels = jnp.zeros((slots, LANE), jnp.float32)
    rank, start = [], []
    for k in range(chunks):
        low = slice(k * slots, (k + 1) * slots)
        high = slice((chunks + k) * slots, (chunks + k + 1) * slots)
        rank.append(count + sums[low, :LANE])
        start.append(pixels + sums[high, :LANE])
        count = count + sums[low, LANE:]
        pixels = pixels + sums[high, LANE:]

    rows = (jnp.max(pixels).astype(jnp.int32) + LANE - 1) // LANE
    rung = jnp.int32(0)
    size = jnp.int32(LADDER[0])
    for smaller, larger in zip(LADDER[:-1], LADDER[1:]):
        rung = rung + (rows > smaller).astype(jnp.int32)
        size = jnp.where(rows > smaller, larger, size)

    def turn_of(index):
        apart = (index // 2) ^ tm_index
        turn = jnp.zeros_like(apart)
        for place, each in enumerate(exchange_order(slots // 2)):
            turn = jnp.where(apart == each, place, turn)
        return turn

    row = turn_of(lax.broadcasted_iota(jnp.int32, (slots, slots), 0))
    index = lax.broadcasted_iota(jnp.int32, (slots, slots), 1)
    earlier = ((turn_of(index) < row) & (index % 2 == tile_index)).astype(jnp.float32)
    turn = turn_of(slot)
    base = jnp.dot(
        earlier, count, precision=lax.Precision.HIGHEST, preferred_element_type=jnp.float32
    )
    begin = (turn * size * LANE).astype(jnp.float32)

    list_row = lax.broadcasted_iota(jnp.int32, (list_rows, LANE), 0)
    list_col = lax.broadcasted_iota(jnp.int32, (LANE, LANE), 0)
    lane = lax.broadcasted_iota(jnp.int32, (1, LANE), 1)
    lists = jnp.zeros((4 * list_rows, LANE), jnp.float32)
    for k in range(chunks):
        own = member[k] * mine
        place = jnp.sum(own * (rank[k] + base), axis=0, keepdims=True).astype(jnp.int32)
        at = jnp.sum(own * (start[k] + begin), axis=0, keepdims=True).astype(jnp.int32)
        used = jnp.sum(own, axis=0, keepdims=True) > 0
        block = k * LANE + lane
        far = (block >= half) != (tile_index == 1)
        block = jnp.where(block >= half, block - half, block) + jnp.where(far, half, 0)
        pixel_count = jnp.sum(own * weighted[k], axis=0, keepdims=True).astype(jnp.int32)
        wraps = at % LANE + pixel_count >= LANE
        word = at * 4096 + block + jnp.where(wraps, jnp.int32(-(2**31)), 0)
        at_row = list_row == jnp.where(used, place // LANE, -1)
        at_col = (list_col == place % LANE).astype(jnp.float32).astype(jnp.bfloat16)
        spread = jnp.concatenate(
            [
                jnp.where(at_row, ((word >> (8 * part)) & 255).astype(jnp.float32), 0.0)
                for part in range(4)
            ],
            axis=0,
        ).astype(jnp.bfloat16)
        lists = lists + lax.dot_general(spread, at_col, NT, preferred_element_type=jnp.float32)
    lists = lists.astype(jnp.int32)
    words = jnp.zeros((list_rows, LANE), jnp.int32)
    for part in range(4):
        words = words + (lists[part * list_rows : (part + 1) * list_rows] << (8 * part))
    index = LANE * lax.broadcasted_iota(jnp.int32, (list_rows, LANE), 0)
    index = index + lax.broadcasted_iota(jnp.int32, (list_rows, LANE), 1)
    total = jnp.sum(count[:, :1] * mine[:, :1]).astype(jnp.int32)
    word_ref[...] = jnp.where(index < total, words, (slots // 2 * size) << 19)

    own_slot = 2 * tm_index + tile_index
    scalar_ref[0] = rung
    scalar_ref[1] = tm_index
    scalar_ref[2] = jnp.sum(jnp.where(slot == own_slot, pixels, 0.0)[:, :1]).astype(jnp.int32)
    for group, end in enumerate(group_ends(slots // 2)):
        ahead = jnp.where(turn < end, count * mine, 0.0)
        scalar_ref[3 + group] = jnp.sum(ahead[:, :1]).astype(jnp.int32)


def widen_kernel(part, in_ref, *rest):
    out_ref = rest[-1]
    half = in_ref.shape[1]

    def widen(i, _):
        begin = pl.multiple_of(i * STEP, STEP)
        rows = in_ref[:, pl.ds(begin, STEP), :].astype(jnp.float32)
        out_ref[pl.ds(part * half + begin, STEP)] = jnp.transpose(rows, (1, 0, 2))
        return 0

    lax.fori_loop(0, half // STEP, widen, 0)


def pack_kernel(group, first, word_ref, scalar_ref, pool_ref, after_ref, *rest):
    out_refs, stage = rest[:-1], rest[-1]
    depth = out_refs[0].shape[0]
    frames = pool_ref.shape[1]
    lane = lax.broadcasted_iota(jnp.int32, (frames, LANE), 1)
    begin, end = scalar_ref[3 + group], scalar_ref[4 + group]

    def place(i, held):
        at = begin + i * UNROLL
        turned = []
        for j in range(UNROLL):
            word = word_ref[at + j]
            turned.append(pltpu.roll(pool_ref[word & 4095], (word >> 12) & (LANE - 1), 1))
        for j in range(UNROLL):
            word = word_ref[at + j]
            shift = (word >> 12) & (LANE - 1)
            row = pl.multiple_of((word >> 16) & 0x7FF8, frames)
            stage[pl.ds(row, frames), :] = jnp.where(lane >= shift, turned[j], held)
            stage[pl.ds(row + frames, frames), :] = turned[j]
            held = jnp.where(lane >= jnp.where(word < 0, 0, shift), turned[j], held)
        return held

    held = jnp.zeros((frames, LANE), jnp.float32)
    lax.fori_loop(0, (end - begin + UNROLL - 1) // UNROLL, place, held)

    step = depth if depth <= 512 else LANE
    for d, out_ref in enumerate(out_refs):
        base = (first + d) * depth

        def narrow(i, _, out_ref=out_ref, base=base):
            row = pl.multiple_of(i * step, step)
            out_ref[pl.ds(row, step), :] = stage[pl.ds(base + row, step), :].astype(jnp.bfloat16)
            return 0

        if step == depth:
            narrow(0, 0)
        else:
            lax.fori_loop(0, depth // step, narrow, 0)


def gram_kernel(scalar_ref, *refs):
    x_refs, (out_ref, turn) = refs[:-2], refs[-2:]
    sources = len(x_refs)
    frames = out_ref.shape[0]
    local = frames // sources
    pixels = scalar_ref[2]
    tm_index = scalar_ref[1]
    lane = lax.broadcasted_iota(jnp.int32, (1, LANE), 1)

    last = x_refs[0].shape[0] // (2 * local) - 1

    def pair(j, carry):
        gram, total = carry
        rows = pl.ds(pl.multiple_of(jnp.minimum(j, last) * 2 * local, 2 * local), 2 * local)
        both = [ref[rows, :].astype(jnp.float32) for ref in x_refs]
        exact, high, low = [], [], []
        for i in range(2):
            used = lane + (2 * j + i) * LANE < pixels
            x = jnp.concatenate([part[i * local : (i + 1) * local] for part in both], axis=0)
            x = jnp.where(used, x, 0.0)
            mean = jnp.where(used, jnp.sum(x, axis=0, keepdims=True) / frames, 1.0)
            scale = 1.0 / mean
            total = total + x * scale
            y = x * (scale * scale)
            top = y.astype(jnp.bfloat16)
            exact.append(x.astype(jnp.bfloat16))
            high.append(top)
            low.append((y - top.astype(jnp.float32)).astype(jnp.bfloat16))
        left = jnp.concatenate(exact, axis=1)
        right = jnp.concatenate(
            [jnp.concatenate(high, axis=1), jnp.concatenate(low, axis=1)], axis=0
        )
        gram = gram + lax.dot_general(left, right, NT, preferred_element_type=jnp.float32)
        return gram, total

    def two_pairs(j, carry):
        return pair(2 * j + 1, pair(2 * j, carry))

    order = exchange_order(sources)

    def in_order(value):
        for j in range(sources):
            at = pl.multiple_of((tm_index ^ order[j]) * local, local)
            turn[pl.ds(at, local), :] = value[j * local : (j + 1) * local]
        return turn[...]

    carry = (jnp.zeros((frames, 2 * frames), jnp.float32), jnp.zeros((frames, LANE), jnp.float32))
    pairs = (pixels + 2 * LANE - 1) // (2 * LANE)
    gram, total = lax.fori_loop(0, (pairs + 1) // 2, two_pairs, carry)
    gram = in_order(gram[:, :frames] + gram[:, frames:])
    gram = in_order(gram.T)
    total = in_order(total)
    first = jnp.sum(total, axis=1, keepdims=True)
    second = jnp.sum(total.T, axis=0, keepdims=True)
    out_ref[...] = pixels.astype(jnp.float32) * gram / (first * second)


def on_device_routed(frames, block_cycle, block_valid, cycle_owner):
    tm_count = lax.axis_size("tm")
    local_frames, half, _ = frames.shape
    frame_count = tm_count * local_frames
    ends = group_ends(tm_count)
    order = exchange_order(tm_count)
    list_rows = -(-(block_cycle.shape[0] + UNROLL) // (8 * LANE)) * 8
    vmem = pl.BlockSpec(memory_space=pltpu.VMEM)
    smem = pl.BlockSpec(memory_space=pltpu.SMEM)
    params = pltpu.CompilerParams(vmem_limit_bytes=VMEM_LIMIT)

    def widen(*given):
        return pl.pallas_call(
            functools.partial(widen_kernel, len(given) - 1),
            out_shape=jax.ShapeDtypeStruct((2 * half, local_frames, LANE), jnp.float32),
            in_specs=[vmem] * len(given),
            out_specs=vmem,
            input_output_aliases={1: 0} if len(given) > 1 else {},
            compiler_params=params,
            name="widen",
        )(*given)

    far = lax.ppermute(frames, "tile", [(0, 1), (1, 0)])
    words, scalars = pl.pallas_call(
        plan_kernel,
        out_shape=(
            jax.ShapeDtypeStruct((list_rows, LANE), jnp.int32),
            jax.ShapeDtypeStruct((3 + len(ends),), jnp.int32),
        ),
        in_specs=[pl.BlockSpec(memory_space=pltpu.HBM)] * 3,
        out_specs=(vmem, smem),
        scratch_shapes=[
            pltpu.SMEM(cycle_owner.shape, jnp.int32),
            pltpu.VMEM(block_cycle.shape, jnp.int32),
            pltpu.VMEM(block_valid.shape, jnp.int32),
            pltpu.SemaphoreType.DMA((3,)),
        ],
        compiler_params=params,
        name="plan",
    )(cycle_owner, block_cycle, block_valid)
    pool = widen(far, widen(frames))

    def branch(size):
        depth = size * local_frames

        def run(words, scalars, pool):
            got = []
            after = scalars
            for group, (first, end) in enumerate(zip(ends[:-1], ends[1:])):
                members = end - first
                send = pl.pallas_call(
                    functools.partial(pack_kernel, group, first),
                    out_shape=(jax.ShapeDtypeStruct((depth, LANE), jnp.bfloat16),) * members,
                    in_specs=[smem, smem, vmem, pl.BlockSpec(memory_space=pl.ANY)],
                    out_specs=(vmem,) * members,
                    scratch_shapes=[
                        pltpu.VMEM(((tm_count * size + 2) * local_frames, LANE), jnp.float32)
                    ],
                    compiler_params=params,
                    cost_estimate=pl.CostEstimate(
                        flops=2_000_000, bytes_accessed=16_000_000, transcendentals=0
                    ),
                    name="pack",
                )(words, scalars, pool, after)
                for part, apart in zip(send, order[first:end]):
                    pairs = [(i, i ^ apart) for i in range(tm_count)]
                    got.append(lax.ppermute(part, "tm", pairs) if apart else part)
                after = got[first]
            return pl.pallas_call(
                gram_kernel,
                out_shape=jax.ShapeDtypeStruct((frame_count, frame_count), jnp.float32),
                in_specs=[smem] + [vmem] * tm_count,
                out_specs=vmem,
                scratch_shapes=[pltpu.VMEM((frame_count, LANE), jnp.float32)],
                compiler_params=params,
                name="gram",
            )(scalars, *got)

        return run

    return lax.switch(
        scalars[0],
        [branch(size) for size in LADDER],
        words.reshape(-1),
        scalars,
        pool,
    )


def normalize(pixel_intensity, valid_count, lanes):
    lane_index = jnp.arange(lanes, dtype=jnp.int32)
    valid_mask = lane_index[None, :] < valid_count[:, None]
    pixel_mean = jnp.sum(pixel_intensity, axis=0) / pixel_intensity.shape[0]
    guarded_average = jnp.where(valid_mask, pixel_mean, jnp.float32(1.0))
    return jnp.where(valid_mask[None], pixel_intensity / guarded_average[None], jnp.float32(0.0))


def on_device_summed(frames, block_cycle, block_valid, cycle_owner):
    tm_count = lax.axis_size("tm")
    tile_count = lax.axis_size("tile")
    tm_index = lax.axis_index("tm")
    tile_index = lax.axis_index("tile")
    local_frames = frames.shape[0]
    half = frames.shape[1]
    lanes = frames.shape[2]
    cycle_count = cycle_owner.shape[0]
    frame_count = local_frames * tm_count
    cycle_range = jnp.arange(cycle_count, dtype=jnp.int32)
    member_all = (block_cycle[None, :] == cycle_owner[:, None]).astype(jnp.float32)
    pixel_total = jnp.dot(
        member_all, block_valid.astype(jnp.float32), precision=lax.Precision.HIGHEST
    )
    row_count = cycle_count * frame_count // (tm_count * tile_count)
    block_local = half // tm_count
    reshaped = frames.reshape(local_frames, tm_count, block_local, lanes)
    arrived = lax.all_to_all(reshaped, "tm", split_axis=1, concat_axis=0, tiled=True)
    pixel_intensity = arrived.reshape(frame_count, block_local, lanes).astype(jnp.float32)
    offset = (tile_index * tm_count + tm_index) * block_local
    cycle_ids = lax.dynamic_slice_in_dim(block_cycle, offset, block_local, 0)
    valid_count = lax.dynamic_slice_in_dim(block_valid, offset, block_local, 0)
    members = (cycle_ids[None, :] == cycle_owner[:, None]).astype(jnp.float32)
    normalized_frames = normalize(pixel_intensity, valid_count, lanes)
    gram_matrices = jnp.einsum(
        "rnk,jnk->nrj", normalized_frames, normalized_frames, precision=lax.Precision.HIGHEST
    )
    partial_value = jnp.dot(
        members,
        gram_matrices.reshape(block_local, frame_count * frame_count),
        precision=lax.Precision.HIGHEST,
    )
    partial_value = partial_value.reshape(cycle_count * frame_count, frame_count)
    frame_sums = jnp.dot(
        members, jnp.sum(normalized_frames, axis=2).T, precision=lax.Precision.HIGHEST
    )
    owned = lax.psum_scatter(partial_value, ("tm", "tile"), scatter_dimension=0, tiled=True)
    frame_total = lax.psum(frame_sums, ("tm", "tile"))
    row_start = (tm_index * tile_count + tile_index) * row_count
    row_global = row_start + jnp.arange(row_count, dtype=jnp.int32)
    slot_index = row_global // frame_count
    frame_time_index = row_global % frame_count
    select = (slot_index[:, None] == cycle_range[None, :]).astype(jnp.float32)
    row_sums = jnp.dot(select, frame_total, precision=lax.Precision.HIGHEST)
    row_pixels = jnp.dot(select, pixel_total, precision=lax.Precision.HIGHEST)
    time_pick = (
        jnp.arange(frame_count, dtype=jnp.int32)[None, :] == frame_time_index[:, None]
    ).astype(jnp.float32)
    first_sums = jnp.sum(row_sums * time_pick, axis=1)
    return row_pixels[:, None] * owned / (first_sums[:, None] * row_sums)


def solution(mesh):
    in_specs = (P("tm", ("series", "tile"), None), P("series"), P("series"), P())
    out_specs = P(("series", "tm", "tile"), None)

    def on_device(frames, block_cycle, block_valid, cycle_owner):
        routed = (
            mesh.shape["tile"] == 2
            and mesh.shape["tm"] * 2 == cycle_owner.shape[0]
            and frames.shape[0] == 8
            and mesh.shape["tm"] * 8 == LANE
            and block_cycle.shape[0] <= 4096
        )
        body = on_device_routed if routed else on_device_summed
        return body(frames, block_cycle, block_valid, cycle_owner)

    return jax.shard_map(
        on_device, mesh=mesh, in_specs=in_specs, out_specs=out_specs, check_vma=False
    )
```

```python
import functools

import jax
import jax.numpy as jnp
from jax import lax
from jax.experimental import pallas as pl
from jax.experimental.pallas import tpu as pltpu
from jax.sharding import PartitionSpec as P

LANE = 128
UNROLL = 32
FIRST = 3
STEP = 128
VMEM_LIMIT = 24 * 1024 * 1024
LADDER = (32, 40, 42, 44, 46, 56, 144)
NT = (((1,), (1,)), ((), ()))


def exchange_order(count):
    side = count // 2
    across = [count - 1 - i for i in range(side)]
    beside = [side - 1 - i for i in range(side)]
    order = across[:FIRST]
    for far, near in zip(across[FIRST:], beside):
        order += [far, near]
    return order + [apart for apart in beside if apart not in order]


def group_ends(count):
    return (0, FIRST, count)


def plan_kernel(
    owner_in, cycle_in, valid_in, word_ref, scalar_ref, owner_ref, cycle_ref, valid_ref, arrived
):
    tm_index, tile_index = lax.axis_index("tm"), lax.axis_index("tile")
    fetches = [
        pltpu.make_async_copy(source, target, arrived.at[i])
        for i, (source, target) in enumerate(
            ((owner_in, owner_ref), (cycle_in, cycle_ref), (valid_in, valid_ref))
        )
    ]
    for fetch in fetches:
        fetch.start()
    for fetch in fetches:
        fetch.wait()
    chunks = cycle_ref.shape[0] // LANE
    slots = owner_ref.shape[0]
    half = cycle_ref.shape[0] // 2
    list_rows = word_ref.shape[0]
    slot = lax.broadcasted_iota(jnp.int32, (slots, LANE), 0)
    mine = (slot % 2 == tile_index).astype(jnp.float32)
    owner = jnp.zeros((slots, LANE), jnp.int32)
    for s in range(slots):
        owner = jnp.where(slot == s, owner_ref[s], owner)

    member, weighted = [], []
    for k in range(chunks):
        cut = slice(k * LANE, (k + 1) * LANE)
        hit = (cycle_ref[cut].reshape(1, LANE) == owner).astype(jnp.float32)
        member.append(hit)
        weighted.append(hit * valid_ref[cut].reshape(1, LANE).astype(jnp.float32))
    stacked = jnp.concatenate(member + weighted, axis=0).astype(jnp.bfloat16)
    before = lax.broadcasted_iota(jnp.int32, (LANE, 2 * LANE), 0)
    column = lax.broadcasted_iota(jnp.int32, (LANE, 2 * LANE), 1)
    prefix = ((before < column) | (column >= LANE)).astype(jnp.float32).astype(jnp.bfloat16)
    sums = jnp.dot(stacked, prefix, preferred_element_type=jnp.float32)

    count = jnp.zeros((slots, LANE), jnp.float32)
    pixels = jnp.zeros((slots, LANE), jnp.float32)
    rank, start = [], []
    for k in range(chunks):
        low = slice(k * slots, (k + 1) * slots)
        high = slice((chunks + k) * slots, (chunks + k + 1) * slots)
        rank.append(count + sums[low, :LANE])
        start.append(pixels + sums[high, :LANE])
        count = count + sums[low, LANE:]
        pixels = pixels + sums[high, LANE:]

    rows = (jnp.max(pixels).astype(jnp.int32) + LANE - 1) // LANE
    rung = jnp.int32(0)
    size = jnp.int32(LADDER[0])
    for smaller, larger in zip(LADDER[:-1], LADDER[1:]):
        rung = rung + (rows > smaller).astype(jnp.int32)
        size = jnp.where(rows > smaller, larger, size)

    def turn_of(index):
        apart = (index // 2) ^ tm_index
        turn = jnp.zeros_like(apart)
        for place, each in enumerate(exchange_order(slots // 2)):
            turn = jnp.where(apart == each, place, turn)
        return turn

    row = turn_of(lax.broadcasted_iota(jnp.int32, (slots, slots), 0))
    index = lax.broadcasted_iota(jnp.int32, (slots, slots), 1)
    earlier = ((turn_of(index) < row) & (index % 2 == tile_index)).astype(jnp.float32)
    turn = turn_of(slot)
    base = jnp.dot(
        earlier, count, precision=lax.Precision.HIGHEST, preferred_element_type=jnp.float32
    )
    begin = (turn * size * LANE).astype(jnp.float32)

    list_row = lax.broadcasted_iota(jnp.int32, (list_rows, LANE), 0)
    list_col = lax.broadcasted_iota(jnp.int32, (LANE, LANE), 0)
    lane = lax.broadcasted_iota(jnp.int32, (1, LANE), 1)
    lists = jnp.zeros((4 * list_rows, LANE), jnp.float32)
    for k in range(chunks):
        own = member[k] * mine
        place = jnp.sum(own * (rank[k] + base), axis=0, keepdims=True).astype(jnp.int32)
        at = jnp.sum(own * (start[k] + begin), axis=0, keepdims=True).astype(jnp.int32)
        used = jnp.sum(own, axis=0, keepdims=True) > 0
        block = k * LANE + lane
        far = (block >= half) != (tile_index == 1)
        block = jnp.where(block >= half, block - half, block) + jnp.where(far, half, 0)
        pixel_count = jnp.sum(own * weighted[k], axis=0, keepdims=True).astype(jnp.int32)
        wraps = at % LANE + pixel_count >= LANE
        word = at * 4096 + block + jnp.where(wraps, jnp.int32(-(2**31)), 0)
        at_row = list_row == jnp.where(used, place // LANE, -1)
        at_col = (list_col == place % LANE).astype(jnp.float32).astype(jnp.bfloat16)
        spread = jnp.concatenate(
            [
                jnp.where(at_row, ((word >> (8 * part)) & 255).astype(jnp.float32), 0.0)
                for part in range(4)
            ],
            axis=0,
        ).astype(jnp.bfloat16)
        lists = lists + lax.dot_general(spread, at_col, NT, preferred_element_type=jnp.float32)
    lists = lists.astype(jnp.int32)
    words = jnp.zeros((list_rows, LANE), jnp.int32)
    for part in range(4):
        words = words + (lists[part * list_rows : (part + 1) * list_rows] << (8 * part))
    index = LANE * lax.broadcasted_iota(jnp.int32, (list_rows, LANE), 0)
    index = index + lax.broadcasted_iota(jnp.int32, (list_rows, LANE), 1)
    total = jnp.sum(count[:, :1] * mine[:, :1]).astype(jnp.int32)
    word_ref[...] = jnp.where(index < total, words, (slots // 2 * size) << 19)

    own_slot = 2 * tm_index + tile_index
    scalar_ref[0] = rung
    scalar_ref[1] = tm_index
    scalar_ref[2] = jnp.sum(jnp.where(slot == own_slot, pixels, 0.0)[:, :1]).astype(jnp.int32)
    for group, end in enumerate(group_ends(slots // 2)):
        ahead = jnp.where(turn < end, count * mine, 0.0)
        scalar_ref[3 + group] = jnp.sum(ahead[:, :1]).astype(jnp.int32)


def widen_kernel(part, in_ref, *rest):
    out_ref = rest[-1]
    half = in_ref.shape[1]

    def widen(i, _):
        begin = pl.multiple_of(i * STEP, STEP)
        rows = in_ref[:, pl.ds(begin, STEP), :].astype(jnp.float32)
        out_ref[pl.ds(part * half + begin, STEP)] = jnp.transpose(rows, (1, 0, 2))
        return 0

    lax.fori_loop(0, half // STEP, widen, 0)


def pack_kernel(group, first, word_ref, scalar_ref, pool_ref, after_ref, *rest):
    out_refs, stage = rest[:-1], rest[-1]
    depth = out_refs[0].shape[0]
    frames = pool_ref.shape[1]
    lane = lax.broadcasted_iota(jnp.int32, (frames, LANE), 1)
    begin, end = scalar_ref[3 + group], scalar_ref[4 + group]

    def place(i, held):
        at = begin + i * UNROLL
        turned = []
        for j in range(UNROLL):
            word = word_ref[at + j]
            turned.append(pltpu.roll(pool_ref[word & 4095], (word >> 12) & (LANE - 1), 1))
        for j in range(UNROLL):
            word = word_ref[at + j]
            shift = (word >> 12) & (LANE - 1)
            row = pl.multiple_of((word >> 16) & 0x7FF8, frames)
            stage[pl.ds(row, frames), :] = jnp.where(lane >= shift, turned[j], held)
            stage[pl.ds(row + frames, frames), :] = turned[j]
            held = jnp.where(lane >= jnp.where(word < 0, 0, shift), turned[j], held)
        return held

    held = jnp.zeros((frames, LANE), jnp.float32)
    lax.fori_loop(0, (end - begin + UNROLL - 1) // UNROLL, place, held)

    step = depth if depth <= 512 else LANE
    for d, out_ref in enumerate(out_refs):
        base = (first + d) * depth

        def narrow(i, _, out_ref=out_ref, base=base):
            row = pl.multiple_of(i * step, step)
            out_ref[pl.ds(row, step), :] = stage[pl.ds(base + row, step), :].astype(jnp.bfloat16)
            return 0

        if step == depth:
            narrow(0, 0)
        else:
            lax.fori_loop(0, depth // step, narrow, 0)


def gram_kernel(scalar_ref, *refs):
    x_refs, (out_ref, turn, scales, totals) = refs[:-4], refs[-4:]
    sources = len(x_refs)
    frames = out_ref.shape[0]
    local = frames // sources
    size = x_refs[0].shape[0] // local
    tm_index, pixels = scalar_ref[1], scalar_ref[2]
    pairs = (pixels + 2 * LANE - 1) // (2 * LANE)
    lane = lax.broadcasted_iota(jnp.int32, (1, LANE), 1)
    row = lax.broadcasted_iota(jnp.int32, (8, LANE), 0)

    def scale(i, _):
        begin = jnp.minimum(8 * i, size - 8)
        part = pl.ds(pl.multiple_of(begin * local, 2 * local), 8 * local)
        each = x_refs[0][part, :].astype(jnp.float32)
        for ref in x_refs[1:]:
            each = each + ref[part, :].astype(jnp.float32)
        mean = jnp.sum(each.reshape(8, local, LANE), axis=1) / frames
        used = lane + (begin + row) * LANE < pixels
        scales[pl.ds(begin, 8), :] = jnp.where(used, 1.0 / jnp.where(used, mean, 1.0), 0.0)
        return 0

    lax.fori_loop(0, (pairs + 3) // 4, scale, 0)
    totals[...] = jnp.zeros(totals.shape, jnp.float32)

    def pair(j, gram):
        rows = pl.ds(pl.multiple_of(j * 2 * local, 2 * local), 2 * local)
        both = [ref[rows, :].astype(jnp.float32) for ref in x_refs]
        exact, high, low = [], [], []
        total = totals[...]
        for i in range(2):
            used = lane + (2 * j + i) * LANE < pixels
            x = jnp.concatenate([part[i * local : (i + 1) * local] for part in both], axis=0)
            x = jnp.where(used, x, 0.0)
            factor = scales[pl.ds(2 * j + i, 1), :]
            normed = x * factor
            total = total + normed
            y = normed * factor
            top = y.astype(jnp.bfloat16)
            exact.append(x.astype(jnp.bfloat16))
            high.append(top)
            low.append((y - top.astype(jnp.float32)).astype(jnp.bfloat16))
        totals[...] = total
        left = jnp.concatenate(exact, axis=1)
        right = jnp.concatenate(
            [jnp.concatenate(high, axis=1), jnp.concatenate(low, axis=1)], axis=0
        )
        return gram + lax.dot_general(left, right, NT, preferred_element_type=jnp.float32)

    order = exchange_order(sources)

    def in_order(value):
        for j in range(sources):
            at = pl.multiple_of((tm_index ^ order[j]) * local, local)
            turn[pl.ds(at, local), :] = value[j * local : (j + 1) * local]
        return turn[...]

    gram = lax.fori_loop(0, pairs, pair, jnp.zeros((frames, 2 * frames), jnp.float32))
    gram = in_order(gram[:, :frames] + gram[:, frames:])
    gram = in_order(gram.T)
    total = in_order(totals[...])
    first = jnp.sum(total, axis=1, keepdims=True)
    second = jnp.sum(total.T, axis=0, keepdims=True)
    out_ref[...] = pixels.astype(jnp.float32) * gram / (first * second)


def on_device_routed(frames, block_cycle, block_valid, cycle_owner):
    tm_count = lax.axis_size("tm")
    local_frames, half, _ = frames.shape
    frame_count = tm_count * local_frames
    ends = group_ends(tm_count)
    order = exchange_order(tm_count)
    list_rows = -(-(block_cycle.shape[0] + UNROLL) // (8 * LANE)) * 8
    vmem = pl.BlockSpec(memory_space=pltpu.VMEM)
    smem = pl.BlockSpec(memory_space=pltpu.SMEM)
    params = pltpu.CompilerParams(vmem_limit_bytes=VMEM_LIMIT)

    def widen(part, *given):
        return pl.pallas_call(
            functools.partial(widen_kernel, part),
            out_shape=jax.ShapeDtypeStruct((2 * half, local_frames, LANE), jnp.float32),
            in_specs=[vmem] * len(given),
            out_specs=vmem,
            input_output_aliases={1: 0} if part else {},
            compiler_params=params,
            name="widen",
        )(*given)

    far = lax.ppermute(frames, "tile", [(0, 1), (1, 0)])
    words, scalars = pl.pallas_call(
        plan_kernel,
        out_shape=(
            jax.ShapeDtypeStruct((list_rows, LANE), jnp.int32),
            jax.ShapeDtypeStruct((3 + len(ends),), jnp.int32),
        ),
        in_specs=[pl.BlockSpec(memory_space=pltpu.HBM)] * 3,
        out_specs=(vmem, smem),
        scratch_shapes=[
            pltpu.SMEM(cycle_owner.shape, jnp.int32),
            pltpu.VMEM(block_cycle.shape, jnp.int32),
            pltpu.VMEM(block_valid.shape, jnp.int32),
            pltpu.SemaphoreType.DMA((3,)),
        ],
        compiler_params=params,
        name="plan",
    )(cycle_owner, block_cycle, block_valid)
    pool = widen(1, far, widen(0, frames))

    def branch(size):
        depth = size * local_frames

        def run(words, scalars, pool):
            got = []
            after = scalars
            for group, (first, end) in enumerate(zip(ends[:-1], ends[1:])):
                members = end - first
                send = pl.pallas_call(
                    functools.partial(pack_kernel, group, first),
                    out_shape=(jax.ShapeDtypeStruct((depth, LANE), jnp.bfloat16),) * members,
                    in_specs=[smem, smem, vmem, pl.BlockSpec(memory_space=pl.ANY)],
                    out_specs=(vmem,) * members,
                    scratch_shapes=[
                        pltpu.VMEM(((tm_count * size + 2) * local_frames, LANE), jnp.float32)
                    ],
                    compiler_params=params,
                    cost_estimate=pl.CostEstimate(
                        flops=2_000_000, bytes_accessed=16_000_000, transcendentals=0
                    ),
                    name="pack",
                )(words, scalars, pool, after)
                for part, apart in zip(send, order[first:end]):
                    pairs = [(i, i ^ apart) for i in range(tm_count)]
                    got.append(lax.ppermute(part, "tm", pairs) if apart else part)
                after = got[first]
            return pl.pallas_call(
                gram_kernel,
                out_shape=jax.ShapeDtypeStruct((frame_count, frame_count), jnp.float32),
                in_specs=[smem] + [vmem] * tm_count,
                out_specs=vmem,
                scratch_shapes=[
                    pltpu.VMEM((frame_count, LANE), jnp.float32),
                    pltpu.VMEM((size, LANE), jnp.float32),
                    pltpu.VMEM((frame_count, LANE), jnp.float32),
                ],
                compiler_params=params,
                name="gram",
            )(scalars, *got)

        return run

    return lax.switch(
        scalars[0],
        [branch(size) for size in LADDER],
        words.reshape(-1),
        scalars,
        pool,
    )


def normalize(pixel_intensity, valid_count, lanes):
    lane_index = jnp.arange(lanes, dtype=jnp.int32)
    valid_mask = lane_index[None, :] < valid_count[:, None]
    pixel_mean = jnp.sum(pixel_intensity, axis=0) / pixel_intensity.shape[0]
    guarded_average = jnp.where(valid_mask, pixel_mean, jnp.float32(1.0))
    return jnp.where(valid_mask[None], pixel_intensity / guarded_average[None], jnp.float32(0.0))


def on_device_summed(frames, block_cycle, block_valid, cycle_owner):
    tm_count = lax.axis_size("tm")
    tile_count = lax.axis_size("tile")
    tm_index = lax.axis_index("tm")
    tile_index = lax.axis_index("tile")
    local_frames = frames.shape[0]
    half = frames.shape[1]
    lanes = frames.shape[2]
    cycle_count = cycle_owner.shape[0]
    frame_count = local_frames * tm_count
    cycle_range = jnp.arange(cycle_count, dtype=jnp.int32)
    member_all = (block_cycle[None, :] == cycle_owner[:, None]).astype(jnp.float32)
    pixel_total = jnp.dot(
        member_all, block_valid.astype(jnp.float32), precision=lax.Precision.HIGHEST
    )
    row_count = cycle_count * frame_count // (tm_count * tile_count)
    block_local = half // tm_count
    reshaped = frames.reshape(local_frames, tm_count, block_local, lanes)
    arrived = lax.all_to_all(reshaped, "tm", split_axis=1, concat_axis=0, tiled=True)
    pixel_intensity = arrived.reshape(frame_count, block_local, lanes).astype(jnp.float32)
    offset = (tile_index * tm_count + tm_index) * block_local
    cycle_ids = lax.dynamic_slice_in_dim(block_cycle, offset, block_local, 0)
    valid_count = lax.dynamic_slice_in_dim(block_valid, offset, block_local, 0)
    members = (cycle_ids[None, :] == cycle_owner[:, None]).astype(jnp.float32)
    normalized_frames = normalize(pixel_intensity, valid_count, lanes)
    gram_matrices = jnp.einsum(
        "rnk,jnk->nrj", normalized_frames, normalized_frames, precision=lax.Precision.HIGHEST
    )
    partial_value = jnp.dot(
        members,
        gram_matrices.reshape(block_local, frame_count * frame_count),
        precision=lax.Precision.HIGHEST,
    )
    partial_value = partial_value.reshape(cycle_count * frame_count, frame_count)
    frame_sums = jnp.dot(
        members, jnp.sum(normalized_frames, axis=2).T, precision=lax.Precision.HIGHEST
    )
    owned = lax.psum_scatter(partial_value, ("tm", "tile"), scatter_dimension=0, tiled=True)
    frame_total = lax.psum(frame_sums, ("tm", "tile"))
    row_start = (tm_index * tile_count + tile_index) * row_count
    row_global = row_start + jnp.arange(row_count, dtype=jnp.int32)
    slot_index = row_global // frame_count
    frame_time_index = row_global % frame_count
    select = (slot_index[:, None] == cycle_range[None, :]).astype(jnp.float32)
    row_sums = jnp.dot(select, frame_total, precision=lax.Precision.HIGHEST)
    row_pixels = jnp.dot(select, pixel_total, precision=lax.Precision.HIGHEST)
    time_pick = (
        jnp.arange(frame_count, dtype=jnp.int32)[None, :] == frame_time_index[:, None]
    ).astype(jnp.float32)
    first_sums = jnp.sum(row_sums * time_pick, axis=1)
    return row_pixels[:, None] * owned / (first_sums[:, None] * row_sums)


def solution(mesh):
    in_specs = (P("tm", ("series", "tile"), None), P("series"), P("series"), P())
    out_specs = P(("series", "tm", "tile"), None)

    def on_device(frames, block_cycle, block_valid, cycle_owner):
        routed = (
            mesh.shape["tile"] == 2
            and mesh.shape["tm"] * 2 == cycle_owner.shape[0]
            and frames.shape[0] == 8
            and mesh.shape["tm"] * 8 == LANE
            and block_cycle.shape[0] <= 4096
        )
        body = on_device_routed if routed else on_device_summed
        return body(frames, block_cycle, block_valid, cycle_owner)

    return jax.shard_map(
        on_device, mesh=mesh, in_specs=in_specs, out_specs=out_specs, check_vma=False
    )
```

```python
import functools

import jax
import jax.numpy as jnp
from jax import lax
from jax.experimental import pallas as pl
from jax.experimental.pallas import tpu as pltpu
from jax.sharding import PartitionSpec as P

LANE = 128
UNROLL = 64
QUAD = 4
STEP = 128
VMEM_LIMIT = 24 * 1024 * 1024
LADDER = (32, 38, 40, 42, 44, 46, 56, 144)
NT = (((1,), (1,)), ((), ()))


def exchange_order(count):
    side = count // 2
    order = []
    for i in range(side):
        order += [count - 1 - i, side - 1 - i]
    return order


def plan_kernel(
    owner_in, cycle_in, valid_in, word_ref, scalar_ref, owner_ref, cycle_ref, valid_ref, arrived
):
    tm_index, tile_index = lax.axis_index("tm"), lax.axis_index("tile")
    fetches = [
        pltpu.make_async_copy(source, target, arrived.at[i])
        for i, (source, target) in enumerate(
            ((owner_in, owner_ref), (cycle_in, cycle_ref), (valid_in, valid_ref))
        )
    ]
    for fetch in fetches:
        fetch.start()
    for fetch in fetches:
        fetch.wait()
    chunks = cycle_ref.shape[0] // LANE
    slots = owner_ref.shape[0]
    half = cycle_ref.shape[0] // 2
    list_rows = word_ref.shape[0]
    slot = lax.broadcasted_iota(jnp.int32, (slots, LANE), 0)
    mine = (slot % 2 == tile_index).astype(jnp.float32)
    owner = jnp.zeros((slots, LANE), jnp.int32)
    for s in range(slots):
        owner = jnp.where(slot == s, owner_ref[s], owner)

    member, weighted = [], []
    for k in range(chunks):
        cut = slice(k * LANE, (k + 1) * LANE)
        hit = (cycle_ref[cut].reshape(1, LANE) == owner).astype(jnp.float32)
        member.append(hit)
        weighted.append(hit * valid_ref[cut].reshape(1, LANE).astype(jnp.float32))
    stacked = jnp.concatenate(member + weighted, axis=0).astype(jnp.bfloat16)
    before = lax.broadcasted_iota(jnp.int32, (LANE, 2 * LANE), 0)
    column = lax.broadcasted_iota(jnp.int32, (LANE, 2 * LANE), 1)
    prefix = ((before < column) | (column >= LANE)).astype(jnp.float32).astype(jnp.bfloat16)
    sums = jnp.dot(stacked, prefix, preferred_element_type=jnp.float32)

    count = jnp.zeros((slots, LANE), jnp.float32)
    pixels = jnp.zeros((slots, LANE), jnp.float32)
    rank, start = [], []
    for k in range(chunks):
        low = slice(k * slots, (k + 1) * slots)
        high = slice((chunks + k) * slots, (chunks + k + 1) * slots)
        rank.append(count + sums[low, :LANE])
        start.append(pixels + sums[high, :LANE])
        count = count + sums[low, LANE:]
        pixels = pixels + sums[high, LANE:]

    rows = (jnp.max(pixels).astype(jnp.int32) + LANE - 1) // LANE
    rung = jnp.int32(0)
    size = jnp.int32(LADDER[0])
    for smaller, larger in zip(LADDER[:-1], LADDER[1:]):
        rung = rung + (rows > smaller).astype(jnp.int32)
        size = jnp.where(rows > smaller, larger, size)

    def turn_of(index):
        apart = (index // 2) ^ tm_index
        turn = jnp.zeros_like(apart)
        for place, each in enumerate(exchange_order(slots // 2)):
            turn = jnp.where(apart == each, place, turn)
        return turn

    row = turn_of(lax.broadcasted_iota(jnp.int32, (slots, slots), 0))
    index = lax.broadcasted_iota(jnp.int32, (slots, slots), 1)
    earlier = ((turn_of(index) < row) & (index % 2 == tile_index)).astype(jnp.float32)
    turn = turn_of(slot)
    base = jnp.dot(
        earlier, count, precision=lax.Precision.HIGHEST, preferred_element_type=jnp.float32
    )
    begin = (turn * size * LANE).astype(jnp.float32)

    list_row = lax.broadcasted_iota(jnp.int32, (list_rows, LANE), 0)
    list_col = lax.broadcasted_iota(jnp.int32, (LANE, LANE), 0)
    lane = lax.broadcasted_iota(jnp.int32, (1, LANE), 1)
    lists = jnp.zeros((4 * list_rows, LANE), jnp.float32)
    for k in range(chunks):
        own = member[k] * mine
        place = jnp.sum(own * (rank[k] + base), axis=0, keepdims=True).astype(jnp.int32)
        at = jnp.sum(own * (start[k] + begin), axis=0, keepdims=True).astype(jnp.int32)
        used = jnp.sum(own, axis=0, keepdims=True) > 0
        block = k * LANE + lane
        far = (block >= half) != (tile_index == 1)
        block = jnp.where(block >= half, block - half, block) + jnp.where(far, half, 0)
        pixel_count = jnp.sum(own * weighted[k], axis=0, keepdims=True).astype(jnp.int32)
        wraps = at % LANE + pixel_count >= LANE
        word = at * 4096 + block + jnp.where(wraps, jnp.int32(-(2**31)), 0)
        at_row = list_row == jnp.where(used, place // LANE, -1)
        at_col = (list_col == place % LANE).astype(jnp.float32).astype(jnp.bfloat16)
        spread = jnp.concatenate(
            [
                jnp.where(at_row, ((word >> (8 * part)) & 255).astype(jnp.float32), 0.0)
                for part in range(4)
            ],
            axis=0,
        ).astype(jnp.bfloat16)
        lists = lists + lax.dot_general(spread, at_col, NT, preferred_element_type=jnp.float32)
    lists = lists.astype(jnp.int32)
    words = jnp.zeros((list_rows, LANE), jnp.int32)
    for part in range(4):
        words = words + (lists[part * list_rows : (part + 1) * list_rows] << (8 * part))
    index = LANE * lax.broadcasted_iota(jnp.int32, (list_rows, LANE), 0)
    index = index + lax.broadcasted_iota(jnp.int32, (list_rows, LANE), 1)
    total = jnp.sum(count[:, :1] * mine[:, :1]).astype(jnp.int32)
    word_ref[...] = jnp.where(index < total, words, (slots // 2 * size) << 19)

    own_slot = 2 * tm_index + tile_index
    scalar_ref[0] = rung
    scalar_ref[1] = tm_index
    scalar_ref[2] = jnp.sum(jnp.where(slot == own_slot, pixels, 0.0)[:, :1]).astype(jnp.int32)
    scalar_ref[3] = total


def widen_kernel(part, in_ref, *rest):
    out_ref = rest[-1]
    half = in_ref.shape[1]

    def widen(i, _):
        begin = pl.multiple_of(i * STEP, STEP)
        rows = in_ref[:, pl.ds(begin, STEP), :].astype(jnp.float32)
        out_ref[pl.ds(part * half + begin, STEP)] = jnp.transpose(rows, (1, 0, 2))
        return 0

    lax.fori_loop(0, half // STEP, widen, 0)


def pack_kernel(word_ref, scalar_ref, pool_ref, *rest):
    out_refs, stage = rest[:-1], rest[-1]
    depth = out_refs[0].shape[0]
    frames = pool_ref.shape[1]
    lane = lax.broadcasted_iota(jnp.int32, (frames, LANE), 1)

    def place(i, held):
        at = i * UNROLL
        turned = []
        for j in range(UNROLL):
            word = word_ref[at + j]
            turned.append(pltpu.roll(pool_ref[word & 4095], (word >> 12) & (LANE - 1), 1))
        for j in range(UNROLL):
            word = word_ref[at + j]
            shift = (word >> 12) & (LANE - 1)
            row = pl.multiple_of((word >> 16) & 0x7FF8, frames)
            stage[pl.ds(row, frames), :] = jnp.where(lane >= shift, turned[j], held)
            stage[pl.ds(row + frames, frames), :] = turned[j]
            held = jnp.where(lane >= jnp.where(word < 0, 0, shift), turned[j], held)
        return held

    held = jnp.zeros((frames, LANE), jnp.float32)
    lax.fori_loop(0, (scalar_ref[3] + UNROLL - 1) // UNROLL, place, held)

    step = depth if depth <= 512 else LANE
    for d, out_ref in enumerate(out_refs):
        base = d * depth

        def narrow(i, _, out_ref=out_ref, base=base):
            row = pl.multiple_of(i * step, step)
            out_ref[pl.ds(row, step), :] = stage[pl.ds(base + row, step), :].astype(jnp.bfloat16)
            return 0

        if step == depth:
            narrow(0, 0)
        else:
            lax.fori_loop(0, depth // step, narrow, 0)


def gram_kernel(scalar_ref, *refs):
    x_refs, (out_ref, turn, grams, totals) = refs[:-4], refs[-4:]
    sources = len(x_refs)
    frames = out_ref.shape[0]
    local = frames // sources
    last = x_refs[0].shape[0] // (2 * local) - 1
    tm_index, pixels = scalar_ref[1], scalar_ref[2]
    lane = lax.broadcasted_iota(jnp.int32, (1, LANE), 1)
    grams[...] = jnp.zeros(grams.shape, jnp.float32)
    totals[...] = jnp.zeros(totals.shape, jnp.float32)

    def several(step, _):
        exact, high, low = [], [], []
        total = totals[...]
        for k in range(QUAD):
            j = QUAD * step + k
            rows = pl.ds(pl.multiple_of(jnp.minimum(j, last) * 2 * local, 2 * local), 2 * local)
            both = [ref[rows, :].astype(jnp.float32) for ref in x_refs]
            for i in range(2):
                used = lane + (2 * j + i) * LANE < pixels
                x = jnp.concatenate([part[i * local : (i + 1) * local] for part in both], axis=0)
                x = jnp.where(used, x, 0.0)
                mean = jnp.where(used, jnp.sum(x, axis=0, keepdims=True) / frames, 1.0)
                scale = 1.0 / mean
                total = total + x * scale
                y = x * (scale * scale)
                top = y.astype(jnp.bfloat16)
                exact.append(x.astype(jnp.bfloat16))
                high.append(top)
                low.append((y - top.astype(jnp.float32)).astype(jnp.bfloat16))
        totals[...] = total
        left = jnp.concatenate(exact, axis=1)
        right = jnp.concatenate(
            [jnp.concatenate(high, axis=1), jnp.concatenate(low, axis=1)], axis=0
        )
        grams[...] += lax.dot_general(left, right, NT, preferred_element_type=jnp.float32)
        return 0

    pairs = (pixels + 2 * LANE - 1) // (2 * LANE)
    lax.fori_loop(0, (pairs + QUAD - 1) // QUAD, several, 0)
    order = exchange_order(sources)

    def in_order(value):
        for j in range(sources):
            at = pl.multiple_of((tm_index ^ order[j]) * local, local)
            turn[pl.ds(at, local), :] = value[j * local : (j + 1) * local]
        return turn[...]

    gram = in_order(grams[:, :frames] + grams[:, frames:])
    gram = in_order(gram.T)
    total = in_order(totals[...])
    first = jnp.sum(total, axis=1, keepdims=True)
    second = jnp.sum(total.T, axis=0, keepdims=True)
    out_ref[...] = pixels.astype(jnp.float32) * gram / (first * second)


def on_device_routed(frames, block_cycle, block_valid, cycle_owner):
    tm_count = lax.axis_size("tm")
    local_frames, half, _ = frames.shape
    frame_count = tm_count * local_frames
    order = exchange_order(tm_count)
    list_rows = -(-(block_cycle.shape[0] + UNROLL) // (8 * LANE)) * 8
    vmem = pl.BlockSpec(memory_space=pltpu.VMEM)
    smem = pl.BlockSpec(memory_space=pltpu.SMEM)
    params = pltpu.CompilerParams(vmem_limit_bytes=VMEM_LIMIT)

    def widen(part, *given):
        return pl.pallas_call(
            functools.partial(widen_kernel, part),
            out_shape=jax.ShapeDtypeStruct((2 * half, local_frames, LANE), jnp.float32),
            in_specs=[vmem] * len(given),
            out_specs=vmem,
            input_output_aliases={1: 0} if part else {},
            compiler_params=params,
            name="widen",
        )(*given)

    far = lax.ppermute(frames, "tile", [(0, 1), (1, 0)])
    words, scalars = pl.pallas_call(
        plan_kernel,
        out_shape=(
            jax.ShapeDtypeStruct((list_rows, LANE), jnp.int32),
            jax.ShapeDtypeStruct((4,), jnp.int32),
        ),
        in_specs=[pl.BlockSpec(memory_space=pltpu.HBM)] * 3,
        out_specs=(vmem, smem),
        scratch_shapes=[
            pltpu.SMEM(cycle_owner.shape, jnp.int32),
            pltpu.VMEM(block_cycle.shape, jnp.int32),
            pltpu.VMEM(block_valid.shape, jnp.int32),
            pltpu.SemaphoreType.DMA((3,)),
        ],
        compiler_params=params,
        name="plan",
    )(cycle_owner, block_cycle, block_valid)
    pool = widen(1, far, widen(0, frames))

    def branch(size):
        depth = size * local_frames

        def run(words, scalars, pool):
            send = pl.pallas_call(
                pack_kernel,
                out_shape=(jax.ShapeDtypeStruct((depth, LANE), jnp.bfloat16),) * tm_count,
                in_specs=[smem, smem, vmem],
                out_specs=(vmem,) * tm_count,
                scratch_shapes=[
                    pltpu.VMEM(((tm_count * size + 2) * local_frames, LANE), jnp.float32)
                ],
                compiler_params=params,
                name="pack",
            )(words, scalars, pool)
            got = []
            for part, apart in zip(send, order):
                pairs = [(i, i ^ apart) for i in range(tm_count)]
                got.append(lax.ppermute(part, "tm", pairs) if apart else part)
            return pl.pallas_call(
                gram_kernel,
                out_shape=jax.ShapeDtypeStruct((frame_count, frame_count), jnp.float32),
                in_specs=[smem] + [vmem] * tm_count,
                out_specs=vmem,
                scratch_shapes=[
                    pltpu.VMEM((frame_count, LANE), jnp.float32),
                    pltpu.VMEM((frame_count, 2 * frame_count), jnp.float32),
                    pltpu.VMEM((frame_count, LANE), jnp.float32),
                ],
                compiler_params=params,
                name="gram",
            )(scalars, *got)

        return run

    return lax.switch(
        scalars[0],
        [branch(size) for size in LADDER],
        words.reshape(-1),
        scalars,
        pool,
    )


def normalize(pixel_intensity, valid_count, lanes):
    lane_index = jnp.arange(lanes, dtype=jnp.int32)
    valid_mask = lane_index[None, :] < valid_count[:, None]
    pixel_mean = jnp.sum(pixel_intensity, axis=0) / pixel_intensity.shape[0]
    guarded_average = jnp.where(valid_mask, pixel_mean, jnp.float32(1.0))
    return jnp.where(valid_mask[None], pixel_intensity / guarded_average[None], jnp.float32(0.0))


def on_device_summed(frames, block_cycle, block_valid, cycle_owner):
    tm_count = lax.axis_size("tm")
    tile_count = lax.axis_size("tile")
    tm_index = lax.axis_index("tm")
    tile_index = lax.axis_index("tile")
    local_frames = frames.shape[0]
    half = frames.shape[1]
    lanes = frames.shape[2]
    cycle_count = cycle_owner.shape[0]
    frame_count = local_frames * tm_count
    cycle_range = jnp.arange(cycle_count, dtype=jnp.int32)
    member_all = (block_cycle[None, :] == cycle_owner[:, None]).astype(jnp.float32)
    pixel_total = jnp.dot(
        member_all, block_valid.astype(jnp.float32), precision=lax.Precision.HIGHEST
    )
    row_count = cycle_count * frame_count // (tm_count * tile_count)
    block_local = half // tm_count
    reshaped = frames.reshape(local_frames, tm_count, block_local, lanes)
    arrived = lax.all_to_all(reshaped, "tm", split_axis=1, concat_axis=0, tiled=True)
    pixel_intensity = arrived.reshape(frame_count, block_local, lanes).astype(jnp.float32)
    offset = (tile_index * tm_count + tm_index) * block_local
    cycle_ids = lax.dynamic_slice_in_dim(block_cycle, offset, block_local, 0)
    valid_count = lax.dynamic_slice_in_dim(block_valid, offset, block_local, 0)
    members = (cycle_ids[None, :] == cycle_owner[:, None]).astype(jnp.float32)
    normalized_frames = normalize(pixel_intensity, valid_count, lanes)
    gram_matrices = jnp.einsum(
        "rnk,jnk->nrj", normalized_frames, normalized_frames, precision=lax.Precision.HIGHEST
    )
    partial_value = jnp.dot(
        members,
        gram_matrices.reshape(block_local, frame_count * frame_count),
        precision=lax.Precision.HIGHEST,
    )
    partial_value = partial_value.reshape(cycle_count * frame_count, frame_count)
    frame_sums = jnp.dot(
        members, jnp.sum(normalized_frames, axis=2).T, precision=lax.Precision.HIGHEST
    )
    owned = lax.psum_scatter(partial_value, ("tm", "tile"), scatter_dimension=0, tiled=True)
    frame_total = lax.psum(frame_sums, ("tm", "tile"))
    row_start = (tm_index * tile_count + tile_index) * row_count
    row_global = row_start + jnp.arange(row_count, dtype=jnp.int32)
    slot_index = row_global // frame_count
    frame_time_index = row_global % frame_count
    select = (slot_index[:, None] == cycle_range[None, :]).astype(jnp.float32)
    row_sums = jnp.dot(select, frame_total, precision=lax.Precision.HIGHEST)
    row_pixels = jnp.dot(select, pixel_total, precision=lax.Precision.HIGHEST)
    time_pick = (
        jnp.arange(frame_count, dtype=jnp.int32)[None, :] == frame_time_index[:, None]
    ).astype(jnp.float32)
    first_sums = jnp.sum(row_sums * time_pick, axis=1)
    return row_pixels[:, None] * owned / (first_sums[:, None] * row_sums)


def solution(mesh):
    in_specs = (P("tm", ("series", "tile"), None), P("series"), P("series"), P())
    out_specs = P(("series", "tm", "tile"), None)

    def on_device(frames, block_cycle, block_valid, cycle_owner):
        routed = (
            mesh.shape["tile"] == 2
            and mesh.shape["tm"] * 2 == cycle_owner.shape[0]
            and frames.shape[0] == 8
            and mesh.shape["tm"] * 8 == LANE
            and block_cycle.shape[0] <= 4096
        )
        body = on_device_routed if routed else on_device_summed
        return body(frames, block_cycle, block_valid, cycle_owner)

    return jax.shard_map(
        on_device, mesh=mesh, in_specs=in_specs, out_specs=out_specs, check_vma=False
    )
```

```python
import functools

import jax
import jax.numpy as jnp
from jax import lax
from jax.experimental import pallas as pl
from jax.experimental.pallas import tpu as pltpu
from jax.sharding import PartitionSpec as P

LANE = 128
UNROLL = 32
QUAD = 4
FIRST = 5
STEP = 128
VMEM_LIMIT = 24 * 1024 * 1024
LADDER = (32, 38, 40, 42, 44, 46, 56, 144)
NT = (((1,), (1,)), ((), ()))


def exchange_order(count):
    side = count // 2
    order = []
    for i in range(side):
        order += [count - 1 - i, side - 1 - i]
    return order


def group_ends(count):
    return (0, FIRST, count)


def plan_kernel(owner_in, cycle_in, valid_in, *rest):
    block_ref, row_ref, lane_ref, cut_ref, scalar_ref = rest[:5]
    owner_ref, cycle_ref, valid_ref, arrived = rest[5:]
    tm_index, tile_index = lax.axis_index("tm"), lax.axis_index("tile")
    fetches = [
        pltpu.make_async_copy(source, target, arrived.at[i])
        for i, (source, target) in enumerate(
            ((owner_in, owner_ref), (cycle_in, cycle_ref), (valid_in, valid_ref))
        )
    ]
    for fetch in fetches:
        fetch.start()
    for fetch in fetches:
        fetch.wait()
    chunks = cycle_ref.shape[0] // LANE
    slots = owner_ref.shape[0]
    half = cycle_ref.shape[0] // 2
    list_rows = block_ref.shape[0]
    slot = lax.broadcasted_iota(jnp.int32, (slots, LANE), 0)
    mine = (slot % 2 == tile_index).astype(jnp.float32)
    owner = jnp.zeros((slots, LANE), jnp.int32)
    for s in range(slots):
        owner = jnp.where(slot == s, owner_ref[s], owner)

    member, weighted = [], []
    for k in range(chunks):
        cut = slice(k * LANE, (k + 1) * LANE)
        hit = (cycle_ref[cut].reshape(1, LANE) == owner).astype(jnp.float32)
        member.append(hit)
        weighted.append(hit * valid_ref[cut].reshape(1, LANE).astype(jnp.float32))
    stacked = jnp.concatenate(member + weighted, axis=0).astype(jnp.bfloat16)
    before = lax.broadcasted_iota(jnp.int32, (LANE, 2 * LANE), 0)
    column = lax.broadcasted_iota(jnp.int32, (LANE, 2 * LANE), 1)
    prefix = ((before < column) | (column >= LANE)).astype(jnp.float32).astype(jnp.bfloat16)
    sums = jnp.dot(stacked, prefix, preferred_element_type=jnp.float32)

    count = jnp.zeros((slots, LANE), jnp.float32)
    pixels = jnp.zeros((slots, LANE), jnp.float32)
    rank, start = [], []
    for k in range(chunks):
        low = slice(k * slots, (k + 1) * slots)
        high = slice((chunks + k) * slots, (chunks + k + 1) * slots)
        rank.append(count + sums[low, :LANE])
        start.append(pixels + sums[high, :LANE])
        count = count + sums[low, LANE:]
        pixels = pixels + sums[high, LANE:]

    rows = (jnp.max(pixels).astype(jnp.int32) + LANE - 1) // LANE
    rung = jnp.int32(0)
    size = jnp.int32(LADDER[0])
    for smaller, larger in zip(LADDER[:-1], LADDER[1:]):
        rung = rung + (rows > smaller).astype(jnp.int32)
        size = jnp.where(rows > smaller, larger, size)

    def turn_of(index):
        apart = (index // 2) ^ tm_index
        turn = jnp.zeros_like(apart)
        for place, each in enumerate(exchange_order(slots // 2)):
            turn = jnp.where(apart == each, place, turn)
        return turn

    row = turn_of(lax.broadcasted_iota(jnp.int32, (slots, slots), 0))
    index = lax.broadcasted_iota(jnp.int32, (slots, slots), 1)
    earlier = ((turn_of(index) < row) & (index % 2 == tile_index)).astype(jnp.float32)
    turn = turn_of(slot)
    base = jnp.dot(
        earlier, count, precision=lax.Precision.HIGHEST, preferred_element_type=jnp.float32
    )
    begin = (turn * size * LANE).astype(jnp.float32)

    list_row = lax.broadcasted_iota(jnp.int32, (list_rows, LANE), 0)
    list_col = lax.broadcasted_iota(jnp.int32, (LANE, LANE), 0)
    lane = lax.broadcasted_iota(jnp.int32, (1, LANE), 1)
    lists = jnp.zeros((4 * list_rows, LANE), jnp.float32)
    for k in range(chunks):
        own = member[k] * mine
        place = jnp.sum(own * (rank[k] + base), axis=0, keepdims=True).astype(jnp.int32)
        at = jnp.sum(own * (start[k] + begin), axis=0, keepdims=True).astype(jnp.int32)
        used = jnp.sum(own, axis=0, keepdims=True) > 0
        block = k * LANE + lane
        far = (block >= half) != (tile_index == 1)
        block = jnp.where(block >= half, block - half, block) + jnp.where(far, half, 0)
        pixel_count = jnp.sum(own * weighted[k], axis=0, keepdims=True).astype(jnp.int32)
        wraps = at % LANE + pixel_count >= LANE
        word = at * 4096 + block + jnp.where(wraps, jnp.int32(-(2**31)), 0)
        at_row = list_row == jnp.where(used, place // LANE, -1)
        at_col = (list_col == place % LANE).astype(jnp.float32).astype(jnp.bfloat16)
        spread = jnp.concatenate(
            [
                jnp.where(at_row, ((word >> (8 * part)) & 255).astype(jnp.float32), 0.0)
                for part in range(4)
            ],
            axis=0,
        ).astype(jnp.bfloat16)
        lists = lists + lax.dot_general(spread, at_col, NT, preferred_element_type=jnp.float32)
    lists = lists.astype(jnp.int32)
    words = jnp.zeros((list_rows, LANE), jnp.int32)
    for part in range(4):
        words = words + (lists[part * list_rows : (part + 1) * list_rows] << (8 * part))
    index = LANE * lax.broadcasted_iota(jnp.int32, (list_rows, LANE), 0)
    index = index + lax.broadcasted_iota(jnp.int32, (list_rows, LANE), 1)
    total = jnp.sum(count[:, :1] * mine[:, :1]).astype(jnp.int32)
    words = jnp.where(index < total, words, (slots // 2 * size) << 19)
    lane_of = (words >> 12) & (LANE - 1)
    block_ref[...] = words & 4095
    row_ref[...] = (words >> 19) & 4095
    lane_ref[...] = lane_of
    cut_ref[...] = jnp.where(words < 0, 0, lane_of)

    own_slot = 2 * tm_index + tile_index
    scalar_ref[0] = rung
    scalar_ref[1] = tm_index
    scalar_ref[2] = jnp.sum(jnp.where(slot == own_slot, pixels, 0.0)[:, :1]).astype(jnp.int32)
    for group, end in enumerate(group_ends(slots // 2)):
        ahead = jnp.where(turn < end, count * mine, 0.0)
        scalar_ref[3 + group] = jnp.sum(ahead[:, :1]).astype(jnp.int32)


def widen_kernel(part, in_ref, *rest):
    out_ref = rest[-1]
    half = in_ref.shape[1]

    def widen(i, _):
        begin = pl.multiple_of(i * STEP, STEP)
        rows = in_ref[:, pl.ds(begin, STEP), :].astype(jnp.float32)
        out_ref[pl.ds(part * half + begin, STEP)] = jnp.transpose(rows, (1, 0, 2))
        return 0

    lax.fori_loop(0, half // STEP, widen, 0)


def pack_kernel(
    group, first, block_ref, row_ref, lane_ref, cut_ref, scalar_ref, pool_ref, after_ref, *rest
):
    out_refs, stage = rest[:-1], rest[-1]
    depth = out_refs[0].shape[0]
    frames = pool_ref.shape[1]
    lane = lax.broadcasted_iota(jnp.int32, (frames, LANE), 1)
    begin, end = scalar_ref[3 + group], scalar_ref[4 + group]

    def place(i, held):
        at = begin + i * UNROLL
        turned = [
            pltpu.roll(pool_ref[block_ref[at + j]], lane_ref[at + j], 1) for j in range(UNROLL)
        ]
        for j in range(UNROLL):
            row = row_ref[at + j]
            stage[row] = jnp.where(lane >= lane_ref[at + j], turned[j], held)
            stage[row + 1] = turned[j]
            held = jnp.where(lane >= cut_ref[at + j], turned[j], held)
        return held

    held = jnp.zeros((frames, LANE), jnp.float32)
    lax.fori_loop(0, (end - begin + UNROLL - 1) // UNROLL, place, held)

    step = depth if depth <= 512 else LANE
    for d, out_ref in enumerate(out_refs):
        base = (first + d) * (depth // frames)

        def narrow(i, _, out_ref=out_ref, base=base):
            part = stage[pl.ds(base + i * (step // frames), step // frames)].reshape(step, LANE)
            out_ref[pl.ds(pl.multiple_of(i * step, step), step), :] = part.astype(jnp.bfloat16)
            return 0

        if step == depth:
            narrow(0, 0)
        else:
            lax.fori_loop(0, depth // step, narrow, 0)


def gram_kernel(scalar_ref, *refs):
    x_refs, (out_ref, turn, grams, totals) = refs[:-4], refs[-4:]
    sources = len(x_refs)
    frames = out_ref.shape[0]
    local = frames // sources
    last = x_refs[0].shape[0] // (2 * local) - 1
    tm_index, pixels = scalar_ref[1], scalar_ref[2]
    lane = lax.broadcasted_iota(jnp.int32, (1, LANE), 1)
    grams[...] = jnp.zeros(grams.shape, jnp.float32)
    totals[...] = jnp.zeros(totals.shape, jnp.float32)

    def several(step, _):
        exact, high, low = [], [], []
        total = totals[...]
        for k in range(QUAD):
            j = QUAD * step + k
            rows = pl.ds(pl.multiple_of(jnp.minimum(j, last) * 2 * local, 2 * local), 2 * local)
            both = [ref[rows, :].astype(jnp.float32) for ref in x_refs]
            for i in range(2):
                used = lane + (2 * j + i) * LANE < pixels
                x = jnp.concatenate([part[i * local : (i + 1) * local] for part in both], axis=0)
                x = jnp.where(used, x, 0.0)
                mean = jnp.where(used, jnp.sum(x, axis=0, keepdims=True) / frames, 1.0)
                scale = 1.0 / mean
                total = total + x * scale
                y = x * (scale * scale)
                top = y.astype(jnp.bfloat16)
                exact.append(x.astype(jnp.bfloat16))
                high.append(top)
                low.append((y - top.astype(jnp.float32)).astype(jnp.bfloat16))
        totals[...] = total
        left = jnp.concatenate(exact, axis=1)
        right = jnp.concatenate(
            [jnp.concatenate(high, axis=1), jnp.concatenate(low, axis=1)], axis=0
        )
        grams[...] += lax.dot_general(left, right, NT, preferred_element_type=jnp.float32)
        return 0

    pairs = (pixels + 2 * LANE - 1) // (2 * LANE)
    lax.fori_loop(0, (pairs + QUAD - 1) // QUAD, several, 0)
    order = exchange_order(sources)

    def in_order(value):
        for j in range(sources):
            at = pl.multiple_of((tm_index ^ order[j]) * local, local)
            turn[pl.ds(at, local), :] = value[j * local : (j + 1) * local]
        return turn[...]

    gram = in_order(grams[:, :frames] + grams[:, frames:])
    gram = in_order(gram.T)
    total = in_order(totals[...])
    first = jnp.sum(total, axis=1, keepdims=True)
    second = jnp.sum(total.T, axis=0, keepdims=True)
    out_ref[...] = pixels.astype(jnp.float32) * gram / (first * second)


def on_device_routed(frames, block_cycle, block_valid, cycle_owner):
    tm_count = lax.axis_size("tm")
    local_frames, half, _ = frames.shape
    frame_count = tm_count * local_frames
    order = exchange_order(tm_count)
    ends = group_ends(tm_count)
    list_rows = -(-(block_cycle.shape[0] + UNROLL) // (8 * LANE)) * 8
    vmem = pl.BlockSpec(memory_space=pltpu.VMEM)
    smem = pl.BlockSpec(memory_space=pltpu.SMEM)
    params = pltpu.CompilerParams(vmem_limit_bytes=VMEM_LIMIT)

    def widen(part, *given):
        return pl.pallas_call(
            functools.partial(widen_kernel, part),
            out_shape=jax.ShapeDtypeStruct((2 * half, local_frames, LANE), jnp.float32),
            in_specs=[vmem] * len(given),
            out_specs=vmem,
            input_output_aliases={1: 0} if part else {},
            compiler_params=params,
            name="widen",
        )(*given)

    far = lax.ppermute(frames, "tile", [(0, 1), (1, 0)])
    *lists, scalars = pl.pallas_call(
        plan_kernel,
        out_shape=(
            *[jax.ShapeDtypeStruct((list_rows, LANE), jnp.int32)] * 4,
            jax.ShapeDtypeStruct((3 + len(ends),), jnp.int32),
        ),
        in_specs=[pl.BlockSpec(memory_space=pltpu.HBM)] * 3,
        out_specs=(vmem,) * 4 + (smem,),
        scratch_shapes=[
            pltpu.SMEM(cycle_owner.shape, jnp.int32),
            pltpu.VMEM(block_cycle.shape, jnp.int32),
            pltpu.VMEM(block_valid.shape, jnp.int32),
            pltpu.SemaphoreType.DMA((3,)),
        ],
        compiler_params=params,
        name="plan",
    )(cycle_owner, block_cycle, block_valid)
    pool = widen(1, far, widen(0, frames))

    def branch(size):
        depth = size * local_frames

        def run(lists, scalars, pool):
            got = []
            after = scalars
            for group, (first, end) in enumerate(zip(ends[:-1], ends[1:])):
                send = pl.pallas_call(
                    functools.partial(pack_kernel, group, first),
                    out_shape=(jax.ShapeDtypeStruct((depth, LANE), jnp.bfloat16),) * (end - first),
                    in_specs=[smem] * 5 + [vmem, pl.BlockSpec(memory_space=pl.ANY)],
                    out_specs=(vmem,) * (end - first),
                    scratch_shapes=[
                        pltpu.VMEM((tm_count * size + 2, local_frames, LANE), jnp.float32)
                    ],
                    compiler_params=params,
                    name="pack",
                )(*lists, scalars, pool, after)
                for part, apart in zip(send, order[first:end]):
                    pairs = [(i, i ^ apart) for i in range(tm_count)]
                    got.append(lax.ppermute(part, "tm", pairs) if apart else part)
                after = got[first]
            return pl.pallas_call(
                gram_kernel,
                out_shape=jax.ShapeDtypeStruct((frame_count, frame_count), jnp.float32),
                in_specs=[smem] + [vmem] * tm_count,
                out_specs=vmem,
                scratch_shapes=[
                    pltpu.VMEM((frame_count, LANE), jnp.float32),
                    pltpu.VMEM((frame_count, 2 * frame_count), jnp.float32),
                    pltpu.VMEM((frame_count, LANE), jnp.float32),
                ],
                compiler_params=params,
                name="gram",
            )(scalars, *got)

        return run

    return lax.switch(
        scalars[0],
        [branch(size) for size in LADDER],
        [each.reshape(-1) for each in lists],
        scalars,
        pool,
    )


def normalize(pixel_intensity, valid_count, lanes):
    lane_index = jnp.arange(lanes, dtype=jnp.int32)
    valid_mask = lane_index[None, :] < valid_count[:, None]
    pixel_mean = jnp.sum(pixel_intensity, axis=0) / pixel_intensity.shape[0]
    guarded_average = jnp.where(valid_mask, pixel_mean, jnp.float32(1.0))
    return jnp.where(valid_mask[None], pixel_intensity / guarded_average[None], jnp.float32(0.0))


def on_device_summed(frames, block_cycle, block_valid, cycle_owner):
    tm_count = lax.axis_size("tm")
    tile_count = lax.axis_size("tile")
    tm_index = lax.axis_index("tm")
    tile_index = lax.axis_index("tile")
    local_frames = frames.shape[0]
    half = frames.shape[1]
    lanes = frames.shape[2]
    cycle_count = cycle_owner.shape[0]
    frame_count = local_frames * tm_count
    cycle_range = jnp.arange(cycle_count, dtype=jnp.int32)
    member_all = (block_cycle[None, :] == cycle_owner[:, None]).astype(jnp.float32)
    pixel_total = jnp.dot(
        member_all, block_valid.astype(jnp.float32), precision=lax.Precision.HIGHEST
    )
    row_count = cycle_count * frame_count // (tm_count * tile_count)
    block_local = half // tm_count
    reshaped = frames.reshape(local_frames, tm_count, block_local, lanes)
    arrived = lax.all_to_all(reshaped, "tm", split_axis=1, concat_axis=0, tiled=True)
    pixel_intensity = arrived.reshape(frame_count, block_local, lanes).astype(jnp.float32)
    offset = (tile_index * tm_count + tm_index) * block_local
    cycle_ids = lax.dynamic_slice_in_dim(block_cycle, offset, block_local, 0)
    valid_count = lax.dynamic_slice_in_dim(block_valid, offset, block_local, 0)
    members = (cycle_ids[None, :] == cycle_owner[:, None]).astype(jnp.float32)
    normalized_frames = normalize(pixel_intensity, valid_count, lanes)
    gram_matrices = jnp.einsum(
        "rnk,jnk->nrj", normalized_frames, normalized_frames, precision=lax.Precision.HIGHEST
    )
    partial_value = jnp.dot(
        members,
        gram_matrices.reshape(block_local, frame_count * frame_count),
        precision=lax.Precision.HIGHEST,
    )
    partial_value = partial_value.reshape(cycle_count * frame_count, frame_count)
    frame_sums = jnp.dot(
        members, jnp.sum(normalized_frames, axis=2).T, precision=lax.Precision.HIGHEST
    )
    owned = lax.psum_scatter(partial_value, ("tm", "tile"), scatter_dimension=0, tiled=True)
    frame_total = lax.psum(frame_sums, ("tm", "tile"))
    row_start = (tm_index * tile_count + tile_index) * row_count
    row_global = row_start + jnp.arange(row_count, dtype=jnp.int32)
    slot_index = row_global // frame_count
    frame_time_index = row_global % frame_count
    select = (slot_index[:, None] == cycle_range[None, :]).astype(jnp.float32)
    row_sums = jnp.dot(select, frame_total, precision=lax.Precision.HIGHEST)
    row_pixels = jnp.dot(select, pixel_total, precision=lax.Precision.HIGHEST)
    time_pick = (
        jnp.arange(frame_count, dtype=jnp.int32)[None, :] == frame_time_index[:, None]
    ).astype(jnp.float32)
    first_sums = jnp.sum(row_sums * time_pick, axis=1)
    return row_pixels[:, None] * owned / (first_sums[:, None] * row_sums)


def solution(mesh):
    in_specs = (P("tm", ("series", "tile"), None), P("series"), P("series"), P())
    out_specs = P(("series", "tm", "tile"), None)

    def on_device(frames, block_cycle, block_valid, cycle_owner):
        routed = (
            mesh.shape["tile"] == 2
            and mesh.shape["tm"] * 2 == cycle_owner.shape[0]
            and frames.shape[0] == 8
            and mesh.shape["tm"] * 8 == LANE
            and block_cycle.shape[0] <= 4096
        )
        body = on_device_routed if routed else on_device_summed
        return body(frames, block_cycle, block_valid, cycle_owner)

    return jax.shard_map(
        on_device, mesh=mesh, in_specs=in_specs, out_specs=out_specs, check_vma=False
    )
```

```python
import functools

import jax
import jax.numpy as jnp
from jax import lax
from jax.experimental import pallas as pl
from jax.experimental.pallas import tpu as pltpu
from jax.sharding import PartitionSpec as P

LANE = 128
UNROLL = 32
QUAD = 4
FIRST = 5
STEP = 384
VMEM_LIMIT = 24 * 1024 * 1024
LADDER = (32, 38, 40, 42, 44, 46, 56, 144)
NT = (((1,), (1,)), ((), ()))


def exchange_order(count):
    side = count // 2
    order = []
    for i in range(side):
        order += [count - 1 - i, side - 1 - i]
    return order


def group_ends(count):
    return (0, FIRST, count)


def plan_kernel(owner_in, cycle_in, valid_in, *rest):
    block_ref, row_ref, lane_ref, cut_ref, scalar_ref = rest[:5]
    owner_ref, cycle_ref, valid_ref, arrived = rest[5:]
    tm_index, tile_index = lax.axis_index("tm"), lax.axis_index("tile")
    fetches = [
        pltpu.make_async_copy(source, target, arrived.at[i])
        for i, (source, target) in enumerate(
            ((owner_in, owner_ref), (cycle_in, cycle_ref), (valid_in, valid_ref))
        )
    ]
    for fetch in fetches:
        fetch.start()
    for fetch in fetches:
        fetch.wait()
    chunks = cycle_ref.shape[0] // LANE
    slots = owner_ref.shape[0]
    half = cycle_ref.shape[0] // 2
    list_rows = block_ref.shape[0]
    slot = lax.broadcasted_iota(jnp.int32, (slots, LANE), 0)
    mine = (slot % 2 == tile_index).astype(jnp.float32)
    owner = jnp.zeros((slots, LANE), jnp.int32)
    for s in range(slots):
        owner = jnp.where(slot == s, owner_ref[s], owner)

    member, weighted = [], []
    for k in range(chunks):
        cut = slice(k * LANE, (k + 1) * LANE)
        hit = (cycle_ref[cut].reshape(1, LANE) == owner).astype(jnp.float32)
        member.append(hit)
        weighted.append(hit * valid_ref[cut].reshape(1, LANE).astype(jnp.float32))
    stacked = jnp.concatenate(member + weighted, axis=0).astype(jnp.bfloat16)
    before = lax.broadcasted_iota(jnp.int32, (LANE, 2 * LANE), 0)
    column = lax.broadcasted_iota(jnp.int32, (LANE, 2 * LANE), 1)
    prefix = ((before < column) | (column >= LANE)).astype(jnp.float32).astype(jnp.bfloat16)
    sums = jnp.dot(stacked, prefix, preferred_element_type=jnp.float32)

    count = jnp.zeros((slots, LANE), jnp.float32)
    pixels = jnp.zeros((slots, LANE), jnp.float32)
    rank, start = [], []
    for k in range(chunks):
        low = slice(k * slots, (k + 1) * slots)
        high = slice((chunks + k) * slots, (chunks + k + 1) * slots)
        rank.append(count + sums[low, :LANE])
        start.append(pixels + sums[high, :LANE])
        count = count + sums[low, LANE:]
        pixels = pixels + sums[high, LANE:]

    rows = (jnp.max(pixels).astype(jnp.int32) + LANE - 1) // LANE
    rung = jnp.int32(0)
    size = jnp.int32(LADDER[0])
    for smaller, larger in zip(LADDER[:-1], LADDER[1:]):
        rung = rung + (rows > smaller).astype(jnp.int32)
        size = jnp.where(rows > smaller, larger, size)

    def turn_of(index):
        apart = (index // 2) ^ tm_index
        turn = jnp.zeros_like(apart)
        for place, each in enumerate(exchange_order(slots // 2)):
            turn = jnp.where(apart == each, place, turn)
        return turn

    row = turn_of(lax.broadcasted_iota(jnp.int32, (slots, slots), 0))
    index = lax.broadcasted_iota(jnp.int32, (slots, slots), 1)
    earlier = ((turn_of(index) < row) & (index % 2 == tile_index)).astype(jnp.float32)
    turn = turn_of(slot)
    base = jnp.dot(
        earlier, count, precision=lax.Precision.HIGHEST, preferred_element_type=jnp.float32
    )
    begin = (turn * size * LANE).astype(jnp.float32)

    list_row = lax.broadcasted_iota(jnp.int32, (list_rows, LANE), 0)
    list_col = lax.broadcasted_iota(jnp.int32, (LANE, LANE), 0)
    lane = lax.broadcasted_iota(jnp.int32, (1, LANE), 1)
    lists = jnp.zeros((4 * list_rows, LANE), jnp.float32)
    for k in range(chunks):
        own = member[k] * mine
        place = jnp.sum(own * (rank[k] + base), axis=0, keepdims=True).astype(jnp.int32)
        at = jnp.sum(own * (start[k] + begin), axis=0, keepdims=True).astype(jnp.int32)
        used = jnp.sum(own, axis=0, keepdims=True) > 0
        block = k * LANE + lane
        far = (block >= half) != (tile_index == 1)
        block = jnp.where(block >= half, block - half, block) + jnp.where(far, half, 0)
        pixel_count = jnp.sum(own * weighted[k], axis=0, keepdims=True).astype(jnp.int32)
        wraps = at % LANE + pixel_count >= LANE
        word = at * 4096 + block + jnp.where(wraps, jnp.int32(-(2**31)), 0)
        at_row = list_row == jnp.where(used, place // LANE, -1)
        at_col = (list_col == place % LANE).astype(jnp.float32).astype(jnp.bfloat16)
        spread = jnp.concatenate(
            [
                jnp.where(at_row, ((word >> (8 * part)) & 255).astype(jnp.float32), 0.0)
                for part in range(4)
            ],
            axis=0,
        ).astype(jnp.bfloat16)
        lists = lists + lax.dot_general(spread, at_col, NT, preferred_element_type=jnp.float32)
    lists = lists.astype(jnp.int32)
    words = jnp.zeros((list_rows, LANE), jnp.int32)
    for part in range(4):
        words = words + (lists[part * list_rows : (part + 1) * list_rows] << (8 * part))
    index = LANE * lax.broadcasted_iota(jnp.int32, (list_rows, LANE), 0)
    index = index + lax.broadcasted_iota(jnp.int32, (list_rows, LANE), 1)
    total = jnp.sum(count[:, :1] * mine[:, :1]).astype(jnp.int32)
    words = jnp.where(index < total, words, (slots // 2 * size) << 19)
    lane_of = (words >> 12) & (LANE - 1)
    block_ref[...] = words & 4095
    row_ref[...] = (words >> 19) & 4095
    lane_ref[...] = lane_of
    cut_ref[...] = jnp.where(words < 0, 0, lane_of)

    own_slot = 2 * tm_index + tile_index
    scalar_ref[0] = rung
    scalar_ref[1] = tm_index
    scalar_ref[2] = jnp.sum(jnp.where(slot == own_slot, pixels, 0.0)[:, :1]).astype(jnp.int32)
    for group, end in enumerate(group_ends(slots // 2)):
        ahead = jnp.where(turn < end, count * mine, 0.0)
        scalar_ref[3 + group] = jnp.sum(ahead[:, :1]).astype(jnp.int32)


def widen_kernel(part, in_ref, *rest):
    out_ref = rest[-1]
    frames, half, _ = in_ref.shape
    for f in range(frames):

        def widen(i, _, f=f):
            begin = pl.multiple_of(i * STEP, STEP)
            rows = in_ref[f, pl.ds(begin, STEP), :].astype(jnp.float32)
            out_ref[pl.ds(f * (2 * half + 1) + part * half + begin, STEP), :] = rows
            return 0

        lax.fori_loop(0, half // STEP, widen, 0)


def pack_kernel(
    group, first, block_ref, row_ref, lane_ref, cut_ref, scalar_ref, pool_ref, after_ref, *rest
):
    out_refs, stage = rest[:-1], rest[-1]
    depth = out_refs[0].shape[0]
    frames = 8
    stride = pool_ref.shape[0] // frames
    lane = lax.broadcasted_iota(jnp.int32, (frames, LANE), 1)
    begin, end = scalar_ref[3 + group], scalar_ref[4 + group]

    def place(i, held):
        at = begin + i * UNROLL
        turned = [
            jnp.take_along_axis(
                pool_ref[pl.ds(block_ref[at + j], frames, stride=stride), :],
                (lane - lane_ref[at + j]) & (LANE - 1),
                axis=1,
                mode="promise_in_bounds",
            )
            for j in range(UNROLL)
        ]
        for j in range(UNROLL):
            row = row_ref[at + j]
            stage[row] = jnp.where(lane >= lane_ref[at + j], turned[j], held)
            stage[row + 1] = turned[j]
            held = jnp.where(lane >= cut_ref[at + j], turned[j], held)
        return held

    held = jnp.zeros((frames, LANE), jnp.float32)
    lax.fori_loop(0, (end - begin + UNROLL - 1) // UNROLL, place, held)

    step = depth if depth <= 512 else LANE
    for d, out_ref in enumerate(out_refs):
        base = (first + d) * (depth // frames)

        def narrow(i, _, out_ref=out_ref, base=base):
            part = stage[pl.ds(base + i * (step // frames), step // frames)].reshape(step, LANE)
            out_ref[pl.ds(pl.multiple_of(i * step, step), step), :] = part.astype(jnp.bfloat16)
            return 0

        if step == depth:
            narrow(0, 0)
        else:
            lax.fori_loop(0, depth // step, narrow, 0)


def gram_kernel(scalar_ref, *refs):
    x_refs, (out_ref, turn, grams, totals) = refs[:-4], refs[-4:]
    sources = len(x_refs)
    frames = out_ref.shape[0]
    local = frames // sources
    last = x_refs[0].shape[0] // (2 * local) - 1
    tm_index, pixels = scalar_ref[1], scalar_ref[2]
    lane = lax.broadcasted_iota(jnp.int32, (1, LANE), 1)
    grams[...] = jnp.zeros(grams.shape, jnp.float32)
    totals[...] = jnp.zeros(totals.shape, jnp.float32)

    def several(step, _):
        exact, high, low = [], [], []
        total = totals[...]
        for k in range(QUAD):
            j = QUAD * step + k
            rows = pl.ds(pl.multiple_of(jnp.minimum(j, last) * 2 * local, 2 * local), 2 * local)
            both = [ref[rows, :].astype(jnp.float32) for ref in x_refs]
            for i in range(2):
                used = lane + (2 * j + i) * LANE < pixels
                x = jnp.concatenate([part[i * local : (i + 1) * local] for part in both], axis=0)
                x = jnp.where(used, x, 0.0)
                mean = jnp.where(used, jnp.sum(x, axis=0, keepdims=True) / frames, 1.0)
                scale = 1.0 / mean
                total = total + x * scale
                y = x * (scale * scale)
                top = y.astype(jnp.bfloat16)
                exact.append(x.astype(jnp.bfloat16))
                high.append(top)
                low.append((y - top.astype(jnp.float32)).astype(jnp.bfloat16))
        totals[...] = total
        left = jnp.concatenate(exact, axis=1)
        right = jnp.concatenate(
            [jnp.concatenate(high, axis=1), jnp.concatenate(low, axis=1)], axis=0
        )
        grams[...] += lax.dot_general(left, right, NT, preferred_element_type=jnp.float32)
        return 0

    pairs = (pixels + 2 * LANE - 1) // (2 * LANE)
    lax.fori_loop(0, (pairs + QUAD - 1) // QUAD, several, 0)
    order = exchange_order(sources)

    def in_order(value):
        for j in range(sources):
            at = pl.multiple_of((tm_index ^ order[j]) * local, local)
            turn[pl.ds(at, local), :] = value[j * local : (j + 1) * local]
        return turn[...]

    gram = in_order(grams[:, :frames] + grams[:, frames:])
    gram = in_order(gram.T)
    total = in_order(totals[...])
    first = jnp.sum(total, axis=1, keepdims=True)
    second = jnp.sum(total.T, axis=0, keepdims=True)
    out_ref[...] = pixels.astype(jnp.float32) * gram / (first * second)


def on_device_routed(frames, block_cycle, block_valid, cycle_owner):
    tm_count = lax.axis_size("tm")
    local_frames, half, _ = frames.shape
    frame_count = tm_count * local_frames
    order = exchange_order(tm_count)
    ends = group_ends(tm_count)
    list_rows = -(-(block_cycle.shape[0] + UNROLL) // (8 * LANE)) * 8
    vmem = pl.BlockSpec(memory_space=pltpu.VMEM)
    smem = pl.BlockSpec(memory_space=pltpu.SMEM)
    params = pltpu.CompilerParams(vmem_limit_bytes=VMEM_LIMIT)

    def widen(part, *given):
        return pl.pallas_call(
            functools.partial(widen_kernel, part),
            out_shape=jax.ShapeDtypeStruct((local_frames * (2 * half + 1), LANE), jnp.float32),
            in_specs=[vmem] * len(given),
            out_specs=vmem,
            input_output_aliases={1: 0} if part else {},
            compiler_params=params,
            name="widen",
        )(*given)

    far = lax.ppermute(frames, "tile", [(0, 1), (1, 0)])
    *lists, scalars = pl.pallas_call(
        plan_kernel,
        out_shape=(
            *[jax.ShapeDtypeStruct((list_rows, LANE), jnp.int32)] * 4,
            jax.ShapeDtypeStruct((3 + len(ends),), jnp.int32),
        ),
        in_specs=[pl.BlockSpec(memory_space=pltpu.HBM)] * 3,
        out_specs=(vmem,) * 4 + (smem,),
        scratch_shapes=[
            pltpu.SMEM(cycle_owner.shape, jnp.int32),
            pltpu.VMEM(block_cycle.shape, jnp.int32),
            pltpu.VMEM(block_valid.shape, jnp.int32),
            pltpu.SemaphoreType.DMA((3,)),
        ],
        compiler_params=params,
        name="plan",
    )(cycle_owner, block_cycle, block_valid)
    pool = widen(1, far, widen(0, frames))

    def branch(size):
        depth = size * local_frames

        def run(lists, scalars, pool):
            got = []
            after = scalars
            for group, (first, end) in enumerate(zip(ends[:-1], ends[1:])):
                send = pl.pallas_call(
                    functools.partial(pack_kernel, group, first),
                    out_shape=(jax.ShapeDtypeStruct((depth, LANE), jnp.bfloat16),) * (end - first),
                    in_specs=[smem] * 5 + [vmem, pl.BlockSpec(memory_space=pl.ANY)],
                    out_specs=(vmem,) * (end - first),
                    scratch_shapes=[
                        pltpu.VMEM((tm_count * size + 2, local_frames, LANE), jnp.float32)
                    ],
                    compiler_params=params,
                    name="pack",
                )(*lists, scalars, pool, after)
                for part, apart in zip(send, order[first:end]):
                    pairs = [(i, i ^ apart) for i in range(tm_count)]
                    got.append(lax.ppermute(part, "tm", pairs) if apart else part)
                after = got[first]
            return pl.pallas_call(
                gram_kernel,
                out_shape=jax.ShapeDtypeStruct((frame_count, frame_count), jnp.float32),
                in_specs=[smem] + [vmem] * tm_count,
                out_specs=vmem,
                scratch_shapes=[
                    pltpu.VMEM((frame_count, LANE), jnp.float32),
                    pltpu.VMEM((frame_count, 2 * frame_count), jnp.float32),
                    pltpu.VMEM((frame_count, LANE), jnp.float32),
                ],
                compiler_params=params,
                name="gram",
            )(scalars, *got)

        return run

    return lax.switch(
        scalars[0],
        [branch(size) for size in LADDER],
        [each.reshape(-1) for each in lists],
        scalars,
        pool,
    )


def normalize(pixel_intensity, valid_count, lanes):
    lane_index = jnp.arange(lanes, dtype=jnp.int32)
    valid_mask = lane_index[None, :] < valid_count[:, None]
    pixel_mean = jnp.sum(pixel_intensity, axis=0) / pixel_intensity.shape[0]
    guarded_average = jnp.where(valid_mask, pixel_mean, jnp.float32(1.0))
    return jnp.where(valid_mask[None], pixel_intensity / guarded_average[None], jnp.float32(0.0))


def on_device_summed(frames, block_cycle, block_valid, cycle_owner):
    tm_count = lax.axis_size("tm")
    tile_count = lax.axis_size("tile")
    tm_index = lax.axis_index("tm")
    tile_index = lax.axis_index("tile")
    local_frames = frames.shape[0]
    half = frames.shape[1]
    lanes = frames.shape[2]
    cycle_count = cycle_owner.shape[0]
    frame_count = local_frames * tm_count
    cycle_range = jnp.arange(cycle_count, dtype=jnp.int32)
    member_all = (block_cycle[None, :] == cycle_owner[:, None]).astype(jnp.float32)
    pixel_total = jnp.dot(
        member_all, block_valid.astype(jnp.float32), precision=lax.Precision.HIGHEST
    )
    row_count = cycle_count * frame_count // (tm_count * tile_count)
    block_local = half // tm_count
    reshaped = frames.reshape(local_frames, tm_count, block_local, lanes)
    arrived = lax.all_to_all(reshaped, "tm", split_axis=1, concat_axis=0, tiled=True)
    pixel_intensity = arrived.reshape(frame_count, block_local, lanes).astype(jnp.float32)
    offset = (tile_index * tm_count + tm_index) * block_local
    cycle_ids = lax.dynamic_slice_in_dim(block_cycle, offset, block_local, 0)
    valid_count = lax.dynamic_slice_in_dim(block_valid, offset, block_local, 0)
    members = (cycle_ids[None, :] == cycle_owner[:, None]).astype(jnp.float32)
    normalized_frames = normalize(pixel_intensity, valid_count, lanes)
    gram_matrices = jnp.einsum(
        "rnk,jnk->nrj", normalized_frames, normalized_frames, precision=lax.Precision.HIGHEST
    )
    partial_value = jnp.dot(
        members,
        gram_matrices.reshape(block_local, frame_count * frame_count),
        precision=lax.Precision.HIGHEST,
    )
    partial_value = partial_value.reshape(cycle_count * frame_count, frame_count)
    frame_sums = jnp.dot(
        members, jnp.sum(normalized_frames, axis=2).T, precision=lax.Precision.HIGHEST
    )
    owned = lax.psum_scatter(partial_value, ("tm", "tile"), scatter_dimension=0, tiled=True)
    frame_total = lax.psum(frame_sums, ("tm", "tile"))
    row_start = (tm_index * tile_count + tile_index) * row_count
    row_global = row_start + jnp.arange(row_count, dtype=jnp.int32)
    slot_index = row_global // frame_count
    frame_time_index = row_global % frame_count
    select = (slot_index[:, None] == cycle_range[None, :]).astype(jnp.float32)
    row_sums = jnp.dot(select, frame_total, precision=lax.Precision.HIGHEST)
    row_pixels = jnp.dot(select, pixel_total, precision=lax.Precision.HIGHEST)
    time_pick = (
        jnp.arange(frame_count, dtype=jnp.int32)[None, :] == frame_time_index[:, None]
    ).astype(jnp.float32)
    first_sums = jnp.sum(row_sums * time_pick, axis=1)
    return row_pixels[:, None] * owned / (first_sums[:, None] * row_sums)


def solution(mesh):
    in_specs = (P("tm", ("series", "tile"), None), P("series"), P("series"), P())
    out_specs = P(("series", "tm", "tile"), None)

    def on_device(frames, block_cycle, block_valid, cycle_owner):
        routed = (
            mesh.shape["tile"] == 2
            and mesh.shape["tm"] * 2 == cycle_owner.shape[0]
            and frames.shape[0] == 8
            and mesh.shape["tm"] * 8 == LANE
            and block_cycle.shape[0] <= 4096
        )
        body = on_device_routed if routed else on_device_summed
        return body(frames, block_cycle, block_valid, cycle_owner)

    return jax.shard_map(
        on_device, mesh=mesh, in_specs=in_specs, out_specs=out_specs, check_vma=False
    )
```

```python
import functools

import jax
import jax.numpy as jnp
from jax import lax
from jax.experimental import pallas as pl
from jax.experimental.pallas import tpu as pltpu
from jax.sharding import PartitionSpec as P

LANE = 128
UNROLL = 32
QUAD = 4
PARCELS = (
    ((15,), (1, 5, 3, 7), (14,), (13,)),
    ((12,), (2,), (6,), (11,), (4,), (10,), (9,), (8,), (0,)),
)
STEP = 128
VMEM_LIMIT = 24 * 1024 * 1024
LADDER = (32, 38, 40, 42, 44, 46, 56, 144)
NT = (((1,), (1,)), ((), ()))


def turn_order():
    return [apart for group in PARCELS for parcel in group for apart in parcel]


def group_ends():
    ends = [0]
    for group in PARCELS:
        ends.append(ends[-1] + sum(len(parcel) for parcel in group))
    return ends


def plan_kernel(owner_in, cycle_in, valid_in, *rest):
    block_ref, row_ref, lane_ref, cut_ref, scalar_ref = rest[:5]
    owner_ref, cycle_ref, valid_ref, arrived = rest[5:]
    tm_index, tile_index = lax.axis_index("tm"), lax.axis_index("tile")
    fetches = [
        pltpu.make_async_copy(source, target, arrived.at[i])
        for i, (source, target) in enumerate(
            ((owner_in, owner_ref), (cycle_in, cycle_ref), (valid_in, valid_ref))
        )
    ]
    for fetch in fetches:
        fetch.start()
    for fetch in fetches:
        fetch.wait()
    chunks = cycle_ref.shape[0] // LANE
    slots = owner_ref.shape[0]
    half = cycle_ref.shape[0] // 2
    list_rows = block_ref.shape[0]
    slot = lax.broadcasted_iota(jnp.int32, (slots, LANE), 0)
    mine = (slot % 2 == tile_index).astype(jnp.float32)
    owner = jnp.zeros((slots, LANE), jnp.int32)
    for s in range(slots):
        owner = jnp.where(slot == s, owner_ref[s], owner)

    member, weighted = [], []
    for k in range(chunks):
        cut = slice(k * LANE, (k + 1) * LANE)
        hit = (cycle_ref[cut].reshape(1, LANE) == owner).astype(jnp.float32)
        member.append(hit)
        weighted.append(hit * valid_ref[cut].reshape(1, LANE).astype(jnp.float32))
    stacked = jnp.concatenate(member + weighted, axis=0).astype(jnp.bfloat16)
    before = lax.broadcasted_iota(jnp.int32, (LANE, 2 * LANE), 0)
    column = lax.broadcasted_iota(jnp.int32, (LANE, 2 * LANE), 1)
    prefix = ((before < column) | (column >= LANE)).astype(jnp.float32).astype(jnp.bfloat16)
    sums = jnp.dot(stacked, prefix, preferred_element_type=jnp.float32)

    count = jnp.zeros((slots, LANE), jnp.float32)
    pixels = jnp.zeros((slots, LANE), jnp.float32)
    rank, start = [], []
    for k in range(chunks):
        low = slice(k * slots, (k + 1) * slots)
        high = slice((chunks + k) * slots, (chunks + k + 1) * slots)
        rank.append(count + sums[low, :LANE])
        start.append(pixels + sums[high, :LANE])
        count = count + sums[low, LANE:]
        pixels = pixels + sums[high, LANE:]

    rows = (jnp.max(pixels).astype(jnp.int32) + LANE - 1) // LANE
    rung = jnp.int32(0)
    size = jnp.int32(LADDER[0])
    for smaller, larger in zip(LADDER[:-1], LADDER[1:]):
        rung = rung + (rows > smaller).astype(jnp.int32)
        size = jnp.where(rows > smaller, larger, size)

    def turn_of(index):
        apart = (index // 2) ^ tm_index
        turn = jnp.zeros_like(apart)
        for place, each in enumerate(turn_order()):
            turn = jnp.where(apart == each, place, turn)
        return turn

    row = turn_of(lax.broadcasted_iota(jnp.int32, (slots, slots), 0))
    index = lax.broadcasted_iota(jnp.int32, (slots, slots), 1)
    earlier = ((turn_of(index) < row) & (index % 2 == tile_index)).astype(jnp.float32)
    turn = turn_of(slot)
    base = jnp.dot(
        earlier, count, precision=lax.Precision.HIGHEST, preferred_element_type=jnp.float32
    )
    begin = (turn * size * LANE).astype(jnp.float32)

    list_row = lax.broadcasted_iota(jnp.int32, (list_rows, LANE), 0)
    list_col = lax.broadcasted_iota(jnp.int32, (LANE, LANE), 0)
    lane = lax.broadcasted_iota(jnp.int32, (1, LANE), 1)
    lists = jnp.zeros((4 * list_rows, LANE), jnp.float32)
    for k in range(chunks):
        own = member[k] * mine
        place = jnp.sum(own * (rank[k] + base), axis=0, keepdims=True).astype(jnp.int32)
        at = jnp.sum(own * (start[k] + begin), axis=0, keepdims=True).astype(jnp.int32)
        used = jnp.sum(own, axis=0, keepdims=True) > 0
        block = k * LANE + lane
        far = (block >= half) != (tile_index == 1)
        block = jnp.where(block >= half, block - half, block) + jnp.where(far, half, 0)
        pixel_count = jnp.sum(own * weighted[k], axis=0, keepdims=True).astype(jnp.int32)
        wraps = at % LANE + pixel_count >= LANE
        word = at * 4096 + block + jnp.where(wraps, jnp.int32(-(2**31)), 0)
        at_row = list_row == jnp.where(used, place // LANE, -1)
        at_col = (list_col == place % LANE).astype(jnp.float32).astype(jnp.bfloat16)
        spread = jnp.concatenate(
            [
                jnp.where(at_row, ((word >> (8 * part)) & 255).astype(jnp.float32), 0.0)
                for part in range(4)
            ],
            axis=0,
        ).astype(jnp.bfloat16)
        lists = lists + lax.dot_general(spread, at_col, NT, preferred_element_type=jnp.float32)
    lists = lists.astype(jnp.int32)
    words = jnp.zeros((list_rows, LANE), jnp.int32)
    for part in range(4):
        words = words + (lists[part * list_rows : (part + 1) * list_rows] << (8 * part))
    index = LANE * lax.broadcasted_iota(jnp.int32, (list_rows, LANE), 0)
    index = index + lax.broadcasted_iota(jnp.int32, (list_rows, LANE), 1)
    total = jnp.sum(count[:, :1] * mine[:, :1]).astype(jnp.int32)
    words = jnp.where(index < total, words, (slots // 2 * size) << 19)
    lane_of = (words >> 12) & (LANE - 1)
    block_ref[...] = words & 4095
    row_ref[...] = (words >> 19) & 4095
    lane_ref[...] = lane_of
    cut_ref[...] = jnp.where(words < 0, 0, lane_of)

    own_slot = 2 * tm_index + tile_index
    scalar_ref[0] = rung
    scalar_ref[1] = tm_index
    scalar_ref[2] = jnp.sum(jnp.where(slot == own_slot, pixels, 0.0)[:, :1]).astype(jnp.int32)
    for group, end in enumerate(group_ends()):
        ahead = jnp.where(turn < end, count * mine, 0.0)
        scalar_ref[3 + group] = jnp.sum(ahead[:, :1]).astype(jnp.int32)


def widen_kernel(part, in_ref, *rest):
    out_ref = rest[-1]
    half = in_ref.shape[1]

    def widen(i, _):
        begin = pl.multiple_of(i * STEP, STEP)
        rows = in_ref[:, pl.ds(begin, STEP), :].astype(jnp.float32)
        out_ref[pl.ds(part * half + begin, STEP)] = jnp.transpose(rows, (1, 0, 2))
        return 0

    lax.fori_loop(0, half // STEP, widen, 0)


def pack_kernel(
    group, first, size, block_ref, row_ref, lane_ref, cut_ref, scalar_ref, pool_ref, after_ref, *rest
):
    out_refs, stage = rest[:-1], rest[-1]
    frames = pool_ref.shape[1]
    lane = lax.broadcasted_iota(jnp.int32, (frames, LANE), 1)
    begin, end = scalar_ref[3 + group], scalar_ref[4 + group]

    def place(i, held):
        at = begin + i * UNROLL
        turned = [
            pltpu.roll(pool_ref[block_ref[at + j]], lane_ref[at + j], 1) for j in range(UNROLL)
        ]
        for j in range(UNROLL):
            row = row_ref[at + j]
            stage[row] = jnp.where(lane >= lane_ref[at + j], turned[j], held)
            stage[row + 1] = turned[j]
            held = jnp.where(lane >= cut_ref[at + j], turned[j], held)
        return held

    held = jnp.zeros((frames, LANE), jnp.float32)
    lax.fori_loop(0, (end - begin + UNROLL - 1) // UNROLL, place, held)

    base = first * size
    for out_ref in out_refs:
        depth = out_ref.shape[0]
        step = depth if depth <= 512 else 2 * size * frames // (4 if size % 4 == 0 else 2)

        def narrow(i, _, out_ref=out_ref, base=base, step=step):
            part = stage[pl.ds(base + i * (step // frames), step // frames)].reshape(step, LANE)
            out_ref[pl.ds(pl.multiple_of(i * step, step), step), :] = part.astype(jnp.bfloat16)
            return 0

        if step == depth:
            narrow(0, 0)
        else:
            lax.fori_loop(0, depth // step, narrow, 0)
        base += depth // frames


def join_kernel(picks, *refs):
    out_ref = refs[-1]
    depth = out_ref.shape[0] // len(picks)
    for i, (source, block) in enumerate(picks):
        out_ref[i * depth : (i + 1) * depth, :] = refs[source][block * depth : (block + 1) * depth, :]


def gram_kernel(picks, size, scalar_ref, *refs):
    x_refs, (out_ref, turn, grams, totals) = refs[:-4], refs[-4:]
    frames = out_ref.shape[0]
    local = frames // len(picks)
    last = size // 2 - 1
    tm_index, pixels = scalar_ref[1], scalar_ref[2]
    lane = lax.broadcasted_iota(jnp.int32, (1, LANE), 1)
    grams[...] = jnp.zeros(grams.shape, jnp.float32)
    totals[...] = jnp.zeros(totals.shape, jnp.float32)

    def several(step, _):
        exact, high, low = [], [], []
        total = totals[...]
        for k in range(QUAD):
            j = QUAD * step + k
            row = pl.multiple_of(jnp.minimum(j, last) * 2 * local, 2 * local)
            both = [
                x_refs[ref][pl.ds(block * size * local + row, 2 * local), :].astype(jnp.float32)
                for ref, block, _ in picks
            ]
            for i in range(2):
                used = lane + (2 * j + i) * LANE < pixels
                x = jnp.concatenate([part[i * local : (i + 1) * local] for part in both], axis=0)
                x = jnp.where(used, x, 0.0)
                mean = jnp.where(used, jnp.sum(x, axis=0, keepdims=True) / frames, 1.0)
                scale = 1.0 / mean
                total = total + x * scale
                y = x * (scale * scale)
                top = y.astype(jnp.bfloat16)
                exact.append(x.astype(jnp.bfloat16))
                high.append(top)
                low.append((y - top.astype(jnp.float32)).astype(jnp.bfloat16))
        totals[...] = total
        left = jnp.concatenate(exact, axis=1)
        right = jnp.concatenate(
            [jnp.concatenate(high, axis=1), jnp.concatenate(low, axis=1)], axis=0
        )
        grams[...] += lax.dot_general(left, right, NT, preferred_element_type=jnp.float32)
        return 0

    pairs = (pixels + 2 * LANE - 1) // (2 * LANE)
    lax.fori_loop(0, (pairs + QUAD - 1) // QUAD, several, 0)
    def in_order(value):
        for j, (_, _, apart) in enumerate(picks):
            at = pl.multiple_of((tm_index ^ apart) * local, local)
            turn[pl.ds(at, local), :] = value[j * local : (j + 1) * local]
        return turn[...]

    gram = in_order(grams[:, :frames] + grams[:, frames:])
    gram = in_order(gram.T)
    total = in_order(totals[...])
    first = jnp.sum(total, axis=1, keepdims=True)
    second = jnp.sum(total.T, axis=0, keepdims=True)
    out_ref[...] = pixels.astype(jnp.float32) * gram / (first * second)


def on_device_routed(frames, block_cycle, block_valid, cycle_owner):
    tm_count = lax.axis_size("tm")
    local_frames, half, _ = frames.shape
    frame_count = tm_count * local_frames
    ends = group_ends()
    list_rows = -(-(block_cycle.shape[0] + UNROLL) // (8 * LANE)) * 8
    vmem = pl.BlockSpec(memory_space=pltpu.VMEM)
    smem = pl.BlockSpec(memory_space=pltpu.SMEM)
    params = pltpu.CompilerParams(vmem_limit_bytes=VMEM_LIMIT)

    def widen(part, *given):
        return pl.pallas_call(
            functools.partial(widen_kernel, part),
            out_shape=jax.ShapeDtypeStruct((2 * half, local_frames, LANE), jnp.float32),
            in_specs=[vmem] * len(given),
            out_specs=vmem,
            input_output_aliases={1: 0} if part else {},
            compiler_params=params,
            name="widen",
        )(*given)

    far = lax.ppermute(frames, "tile", [(0, 1), (1, 0)])
    *lists, scalars = pl.pallas_call(
        plan_kernel,
        out_shape=(
            *[jax.ShapeDtypeStruct((list_rows, LANE), jnp.int32)] * 4,
            jax.ShapeDtypeStruct((3 + len(ends),), jnp.int32),
        ),
        in_specs=[pl.BlockSpec(memory_space=pltpu.HBM)] * 3,
        out_specs=(vmem,) * 4 + (smem,),
        scratch_shapes=[
            pltpu.SMEM(cycle_owner.shape, jnp.int32),
            pltpu.VMEM(block_cycle.shape, jnp.int32),
            pltpu.VMEM(block_valid.shape, jnp.int32),
            pltpu.SemaphoreType.DMA((3,)),
        ],
        compiler_params=params,
        name="plan",
    )(cycle_owner, block_cycle, block_valid)
    pool = widen(1, far, widen(0, frames))

    def branch(size):
        depth = size * local_frames

        def run(lists, scalars, pool):
            def send(parcel, apart):
                pairs = [(i, i ^ apart) for i in range(tm_count)]
                return lax.ppermute(parcel, "tm", pairs)

            def join(picks, after, *parts):
                return pl.pallas_call(
                    functools.partial(join_kernel, picks),
                    out_shape=jax.ShapeDtypeStruct((len(picks) * depth, LANE), jnp.bfloat16),
                    in_specs=[vmem] * len(parts) + [pl.BlockSpec(memory_space=pl.ANY)] * len(after),
                    out_specs=vmem,
                    compiler_params=params,
                    name="join",
                )(*parts, *after)

            packed, got, picks = {}, [], []
            after = scalars
            for group, parcels in enumerate(PARCELS):
                parts = pl.pallas_call(
                    functools.partial(pack_kernel, group, ends[group], size),
                    out_shape=[
                        jax.ShapeDtypeStruct((len(each) * depth, LANE), jnp.bfloat16)
                        for each in parcels
                    ],
                    in_specs=[smem] * 5 + [vmem, pl.BlockSpec(memory_space=pl.ANY)],
                    out_specs=[vmem] * len(parcels),
                    scratch_shapes=[
                        pltpu.VMEM((tm_count * size + 2, local_frames, LANE), jnp.float32)
                    ],
                    compiler_params=params,
                    name="pack",
                )(*lists, scalars, pool, after)
                for part, (apart, *_) in zip(parts, parcels):
                    if apart >= 8:
                        picks.append((len(got), 0, apart))
                        got.append(send(part, apart))
                    else:
                        packed[apart] = part
                after = got[1]
            along_x = send(packed[1], 1)
            picks_y = ((0, 0), (2, 2), (1, 0), (2, 3))
            parcel = join(picks_y, (got[0], got[2]), packed[2], packed[6], along_x)
            along_y = send(parcel, 2)
            picks_z = ((0, 0), (1, 1), (2, 2), (2, 3))
            parcel = join(picks_z, (got[3], got[4]), packed[4], along_x, along_y)
            along_z = send(parcel, 4)
            for part, sources in (
                (packed[0], (0,)),
                (along_x, (1,)),
                (along_y, (2, 3)),
                (along_z, (4, 5, 6, 7)),
            ):
                picks += [(len(got), block, apart) for block, apart in enumerate(sources)]
                got.append(part)
            return pl.pallas_call(
                functools.partial(gram_kernel, tuple(picks), size),
                out_shape=jax.ShapeDtypeStruct((frame_count, frame_count), jnp.float32),
                in_specs=[smem] + [vmem] * len(got),
                out_specs=vmem,
                scratch_shapes=[
                    pltpu.VMEM((frame_count, LANE), jnp.float32),
                    pltpu.VMEM((frame_count, 2 * frame_count), jnp.float32),
                    pltpu.VMEM((frame_count, LANE), jnp.float32),
                ],
                compiler_params=params,
                name="gram",
            )(scalars, *got)

        return run

    return lax.switch(
        scalars[0],
        [branch(size) for size in LADDER],
        [each.reshape(-1) for each in lists],
        scalars,
        pool,
    )


def normalize(pixel_intensity, valid_count, lanes):
    lane_index = jnp.arange(lanes, dtype=jnp.int32)
    valid_mask = lane_index[None, :] < valid_count[:, None]
    pixel_mean = jnp.sum(pixel_intensity, axis=0) / pixel_intensity.shape[0]
    guarded_average = jnp.where(valid_mask, pixel_mean, jnp.float32(1.0))
    return jnp.where(valid_mask[None], pixel_intensity / guarded_average[None], jnp.float32(0.0))


def on_device_summed(frames, block_cycle, block_valid, cycle_owner):
    tm_count = lax.axis_size("tm")
    tile_count = lax.axis_size("tile")
    tm_index = lax.axis_index("tm")
    tile_index = lax.axis_index("tile")
    local_frames = frames.shape[0]
    half = frames.shape[1]
    lanes = frames.shape[2]
    cycle_count = cycle_owner.shape[0]
    frame_count = local_frames * tm_count
    cycle_range = jnp.arange(cycle_count, dtype=jnp.int32)
    member_all = (block_cycle[None, :] == cycle_owner[:, None]).astype(jnp.float32)
    pixel_total = jnp.dot(
        member_all, block_valid.astype(jnp.float32), precision=lax.Precision.HIGHEST
    )
    row_count = cycle_count * frame_count // (tm_count * tile_count)
    block_local = half // tm_count
    reshaped = frames.reshape(local_frames, tm_count, block_local, lanes)
    arrived = lax.all_to_all(reshaped, "tm", split_axis=1, concat_axis=0, tiled=True)
    pixel_intensity = arrived.reshape(frame_count, block_local, lanes).astype(jnp.float32)
    offset = (tile_index * tm_count + tm_index) * block_local
    cycle_ids = lax.dynamic_slice_in_dim(block_cycle, offset, block_local, 0)
    valid_count = lax.dynamic_slice_in_dim(block_valid, offset, block_local, 0)
    members = (cycle_ids[None, :] == cycle_owner[:, None]).astype(jnp.float32)
    normalized_frames = normalize(pixel_intensity, valid_count, lanes)
    gram_matrices = jnp.einsum(
        "rnk,jnk->nrj", normalized_frames, normalized_frames, precision=lax.Precision.HIGHEST
    )
    partial_value = jnp.dot(
        members,
        gram_matrices.reshape(block_local, frame_count * frame_count),
        precision=lax.Precision.HIGHEST,
    )
    partial_value = partial_value.reshape(cycle_count * frame_count, frame_count)
    frame_sums = jnp.dot(
        members, jnp.sum(normalized_frames, axis=2).T, precision=lax.Precision.HIGHEST
    )
    owned = lax.psum_scatter(partial_value, ("tm", "tile"), scatter_dimension=0, tiled=True)
    frame_total = lax.psum(frame_sums, ("tm", "tile"))
    row_start = (tm_index * tile_count + tile_index) * row_count
    row_global = row_start + jnp.arange(row_count, dtype=jnp.int32)
    slot_index = row_global // frame_count
    frame_time_index = row_global % frame_count
    select = (slot_index[:, None] == cycle_range[None, :]).astype(jnp.float32)
    row_sums = jnp.dot(select, frame_total, precision=lax.Precision.HIGHEST)
    row_pixels = jnp.dot(select, pixel_total, precision=lax.Precision.HIGHEST)
    time_pick = (
        jnp.arange(frame_count, dtype=jnp.int32)[None, :] == frame_time_index[:, None]
    ).astype(jnp.float32)
    first_sums = jnp.sum(row_sums * time_pick, axis=1)
    return row_pixels[:, None] * owned / (first_sums[:, None] * row_sums)


def solution(mesh):
    in_specs = (P("tm", ("series", "tile"), None), P("series"), P("series"), P())
    out_specs = P(("series", "tm", "tile"), None)

    def on_device(frames, block_cycle, block_valid, cycle_owner):
        routed = (
            mesh.shape["tile"] == 2
            and mesh.shape["tm"] * 2 == cycle_owner.shape[0]
            and frames.shape[0] == 8
            and mesh.shape["tm"] * 8 == LANE
            and block_cycle.shape[0] <= 4096
        )
        body = on_device_routed if routed else on_device_summed
        return body(frames, block_cycle, block_valid, cycle_owner)

    return jax.shard_map(
        on_device, mesh=mesh, in_specs=in_specs, out_specs=out_specs, check_vma=False
    )
```

```python
import functools

import jax
import jax.numpy as jnp
from jax import lax
from jax.experimental import pallas as pl
from jax.experimental.pallas import tpu as pltpu
from jax.sharding import PartitionSpec as P

LANE = 128
UNROLL = 32
FIRST = 5
QUAD = 4
STEP = 128
VMEM_LIMIT = 24 * 1024 * 1024
LADDER = (32, 38, 40, 42, 44, 46, 56, 144)
NT = (((1,), (1,)), ((), ()))


def exchange_order(count):
    side = count // 2
    across = [count - 1 - i for i in range(side)]
    beside = [side - 1 - i for i in range(side)]
    order = across[:3] + beside[:1] + across[3:4]
    for far, near in zip(across[4:], beside[1:]):
        order += [near, far]
    return order + [apart for apart in beside if apart not in order]


def group_ends(count):
    return (0, FIRST, count)


def plan_kernel(
    owner_in, cycle_in, valid_in, word_ref, scalar_ref, owner_ref, cycle_ref, valid_ref, arrived
):
    tm_index, tile_index = lax.axis_index("tm"), lax.axis_index("tile")
    fetches = [
        pltpu.make_async_copy(source, target, arrived.at[i])
        for i, (source, target) in enumerate(
            ((owner_in, owner_ref), (cycle_in, cycle_ref), (valid_in, valid_ref))
        )
    ]
    for fetch in fetches:
        fetch.start()
    for fetch in fetches:
        fetch.wait()
    chunks = cycle_ref.shape[0] // LANE
    slots = owner_ref.shape[0]
    half = cycle_ref.shape[0] // 2
    list_rows = word_ref.shape[0]
    slot = lax.broadcasted_iota(jnp.int32, (slots, LANE), 0)
    mine = (slot % 2 == tile_index).astype(jnp.float32)
    owner = jnp.zeros((slots, LANE), jnp.int32)
    for s in range(slots):
        owner = jnp.where(slot == s, owner_ref[s], owner)

    member, weighted = [], []
    for k in range(chunks):
        cut = slice(k * LANE, (k + 1) * LANE)
        hit = (cycle_ref[cut].reshape(1, LANE) == owner).astype(jnp.float32)
        member.append(hit)
        weighted.append(hit * valid_ref[cut].reshape(1, LANE).astype(jnp.float32))
    stacked = jnp.concatenate(member + weighted, axis=0).astype(jnp.bfloat16)
    before = lax.broadcasted_iota(jnp.int32, (LANE, 2 * LANE), 0)
    column = lax.broadcasted_iota(jnp.int32, (LANE, 2 * LANE), 1)
    prefix = ((before < column) | (column >= LANE)).astype(jnp.float32).astype(jnp.bfloat16)
    sums = jnp.dot(stacked, prefix, preferred_element_type=jnp.float32)

    count = jnp.zeros((slots, LANE), jnp.float32)
    pixels = jnp.zeros((slots, LANE), jnp.float32)
    rank, start = [], []
    for k in range(chunks):
        low = slice(k * slots, (k + 1) * slots)
        high = slice((chunks + k) * slots, (chunks + k + 1) * slots)
        rank.append(count + sums[low, :LANE])
        start.append(pixels + sums[high, :LANE])
        count = count + sums[low, LANE:]
        pixels = pixels + sums[high, LANE:]

    rows = (jnp.max(pixels).astype(jnp.int32) + LANE - 1) // LANE
    rung = jnp.int32(0)
    size = jnp.int32(LADDER[0])
    for smaller, larger in zip(LADDER[:-1], LADDER[1:]):
        rung = rung + (rows > smaller).astype(jnp.int32)
        size = jnp.where(rows > smaller, larger, size)

    def turn_of(index):
        apart = (index // 2) ^ tm_index
        turn = jnp.zeros_like(apart)
        for place, each in enumerate(exchange_order(slots // 2)):
            turn = jnp.where(apart == each, place, turn)
        return turn

    row = turn_of(lax.broadcasted_iota(jnp.int32, (slots, slots), 0))
    index = lax.broadcasted_iota(jnp.int32, (slots, slots), 1)
    earlier = ((turn_of(index) < row) & (index % 2 == tile_index)).astype(jnp.float32)
    turn = turn_of(slot)
    base = jnp.dot(
        earlier, count, precision=lax.Precision.HIGHEST, preferred_element_type=jnp.float32
    )
    begin = (turn * size * LANE).astype(jnp.float32)

    list_row = lax.broadcasted_iota(jnp.int32, (list_rows, LANE), 0)
    list_col = lax.broadcasted_iota(jnp.int32, (LANE, LANE), 0)
    lane = lax.broadcasted_iota(jnp.int32, (1, LANE), 1)
    lists = jnp.zeros((4 * list_rows, LANE), jnp.float32)
    for k in range(chunks):
        own = member[k] * mine
        place = jnp.sum(own * (rank[k] + base), axis=0, keepdims=True).astype(jnp.int32)
        at = jnp.sum(own * (start[k] + begin), axis=0, keepdims=True).astype(jnp.int32)
        used = jnp.sum(own, axis=0, keepdims=True) > 0
        block = k * LANE + lane
        far = (block >= half) != (tile_index == 1)
        block = jnp.where(block >= half, block - half, block) + jnp.where(far, half, 0)
        pixel_count = jnp.sum(own * weighted[k], axis=0, keepdims=True).astype(jnp.int32)
        wraps = at % LANE + pixel_count >= LANE
        word = at * 4096 + block + jnp.where(wraps, jnp.int32(-(2**31)), 0)
        at_row = list_row == jnp.where(used, place // LANE, -1)
        at_col = (list_col == place % LANE).astype(jnp.float32).astype(jnp.bfloat16)
        spread = jnp.concatenate(
            [
                jnp.where(at_row, ((word >> (8 * part)) & 255).astype(jnp.float32), 0.0)
                for part in range(4)
            ],
            axis=0,
        ).astype(jnp.bfloat16)
        lists = lists + lax.dot_general(spread, at_col, NT, preferred_element_type=jnp.float32)
    lists = lists.astype(jnp.int32)
    words = jnp.zeros((list_rows, LANE), jnp.int32)
    for part in range(4):
        words = words + (lists[part * list_rows : (part + 1) * list_rows] << (8 * part))
    index = LANE * lax.broadcasted_iota(jnp.int32, (list_rows, LANE), 0)
    index = index + lax.broadcasted_iota(jnp.int32, (list_rows, LANE), 1)
    total = jnp.sum(count[:, :1] * mine[:, :1]).astype(jnp.int32)
    word_ref[...] = jnp.where(index < total, words, (slots // 2 * size) << 19)

    own_slot = 2 * tm_index + tile_index
    scalar_ref[0] = rung
    scalar_ref[1] = tm_index
    scalar_ref[2] = jnp.sum(jnp.where(slot == own_slot, pixels, 0.0)[:, :1]).astype(jnp.int32)
    for group, end in enumerate(group_ends(slots // 2)):
        ahead = jnp.where(turn < end, count * mine, 0.0)
        scalar_ref[3 + group] = jnp.sum(ahead[:, :1]).astype(jnp.int32)


def widen_kernel(part, in_ref, *rest):
    out_ref = rest[-1]
    half = in_ref.shape[1]

    def widen(i, _):
        begin = pl.multiple_of(i * STEP, STEP)
        rows = in_ref[:, pl.ds(begin, STEP), :].astype(jnp.float32)
        out_ref[pl.ds(part * half + begin, STEP)] = jnp.transpose(rows, (1, 0, 2))
        return 0

    lax.fori_loop(0, half // STEP, widen, 0)


def pack_kernel(group, first, word_ref, scalar_ref, pool_ref, after_ref, *rest):
    out_refs, stage = rest[:-1], rest[-1]
    depth = out_refs[0].shape[0]
    frames = pool_ref.shape[1]
    lane = lax.broadcasted_iota(jnp.int32, (frames, LANE), 1)
    begin, end = scalar_ref[3 + group], scalar_ref[4 + group]

    def place(i, held):
        at = begin + i * UNROLL
        turned = []
        for j in range(UNROLL):
            word = word_ref[at + j]
            turned.append(pltpu.roll(pool_ref[word & 4095], (word >> 12) & (LANE - 1), 1))
        for j in range(UNROLL):
            word = word_ref[at + j]
            shift = (word >> 12) & (LANE - 1)
            row = pl.multiple_of((word >> 16) & 0x7FF8, frames)
            stage[pl.ds(row, frames), :] = jnp.where(lane >= shift, turned[j], held)
            stage[pl.ds(row + frames, frames), :] = turned[j]
            held = jnp.where(lane >= jnp.where(word < 0, 0, shift), turned[j], held)
        return held

    held = jnp.zeros((frames, LANE), jnp.float32)
    lax.fori_loop(0, (end - begin + UNROLL - 1) // UNROLL, place, held)

    step = depth if depth <= 512 else LANE
    for d, out_ref in enumerate(out_refs):
        base = (first + d) * depth

        def narrow(i, _, out_ref=out_ref, base=base):
            row = pl.multiple_of(i * step, step)
            out_ref[pl.ds(row, step), :] = stage[pl.ds(base + row, step), :].astype(jnp.bfloat16)
            return 0

        if step == depth:
            narrow(0, 0)
        else:
            lax.fori_loop(0, depth // step, narrow, 0)


def gram_kernel(scalar_ref, *refs):
    x_refs, (out_ref, turn, grams, totals) = refs[:-4], refs[-4:]
    sources = len(x_refs)
    frames = out_ref.shape[0]
    local = frames // sources
    last = x_refs[0].shape[0] // (2 * local) - 1
    tm_index, pixels = scalar_ref[1], scalar_ref[2]
    lane = lax.broadcasted_iota(jnp.int32, (1, LANE), 1)
    grams[...] = jnp.zeros(grams.shape, jnp.float32)
    totals[...] = jnp.zeros(totals.shape, jnp.float32)

    def several(step, _):
        exact, high, low = [], [], []
        total = totals[...]
        for k in range(QUAD):
            j = QUAD * step + k
            rows = pl.ds(pl.multiple_of(jnp.minimum(j, last) * 2 * local, 2 * local), 2 * local)
            both = [ref[rows, :].astype(jnp.float32) for ref in x_refs]
            for i in range(2):
                used = lane + (2 * j + i) * LANE < pixels
                x = jnp.concatenate([part[i * local : (i + 1) * local] for part in both], axis=0)
                x = jnp.where(used, x, 0.0)
                mean = jnp.where(used, jnp.sum(x, axis=0, keepdims=True) / frames, 1.0)
                scale = 1.0 / mean
                total = total + x * scale
                y = x * (scale * scale)
                top = y.astype(jnp.bfloat16)
                exact.append(x.astype(jnp.bfloat16))
                high.append(top)
                low.append((y - top.astype(jnp.float32)).astype(jnp.bfloat16))
        totals[...] = total
        left = jnp.concatenate(exact, axis=1)
        right = jnp.concatenate(
            [jnp.concatenate(high, axis=1), jnp.concatenate(low, axis=1)], axis=0
        )
        grams[...] += lax.dot_general(left, right, NT, preferred_element_type=jnp.float32)
        return 0

    pairs = (pixels + 2 * LANE - 1) // (2 * LANE)
    lax.fori_loop(0, (pairs + QUAD - 1) // QUAD, several, 0)
    order = exchange_order(sources)

    def in_order(value):
        for j in range(sources):
            at = pl.multiple_of((tm_index ^ order[j]) * local, local)
            turn[pl.ds(at, local), :] = value[j * local : (j + 1) * local]
        return turn[...]

    gram = in_order(grams[:, :frames] + grams[:, frames:])
    gram = in_order(gram.T)
    total = in_order(totals[...])
    first = jnp.sum(total, axis=1, keepdims=True)
    second = jnp.sum(total.T, axis=0, keepdims=True)
    out_ref[...] = pixels.astype(jnp.float32) * gram / (first * second)


def on_device_routed(frames, block_cycle, block_valid, cycle_owner):
    tm_count = lax.axis_size("tm")
    local_frames, half, _ = frames.shape
    frame_count = tm_count * local_frames
    ends = group_ends(tm_count)
    order = exchange_order(tm_count)
    list_rows = -(-(block_cycle.shape[0] + UNROLL) // (8 * LANE)) * 8
    vmem = pl.BlockSpec(memory_space=pltpu.VMEM)
    smem = pl.BlockSpec(memory_space=pltpu.SMEM)
    params = pltpu.CompilerParams(vmem_limit_bytes=VMEM_LIMIT)

    def widen(*given):
        return pl.pallas_call(
            functools.partial(widen_kernel, len(given) - 1),
            out_shape=jax.ShapeDtypeStruct((2 * half, local_frames, LANE), jnp.float32),
            in_specs=[vmem] * len(given),
            out_specs=vmem,
            input_output_aliases={1: 0} if len(given) > 1 else {},
            compiler_params=params,
            name="widen",
        )(*given)

    far = lax.ppermute(frames, "tile", [(0, 1), (1, 0)])
    words, scalars = pl.pallas_call(
        plan_kernel,
        out_shape=(
            jax.ShapeDtypeStruct((list_rows, LANE), jnp.int32),
            jax.ShapeDtypeStruct((3 + len(ends),), jnp.int32),
        ),
        in_specs=[pl.BlockSpec(memory_space=pltpu.HBM)] * 3,
        out_specs=(vmem, smem),
        scratch_shapes=[
            pltpu.SMEM(cycle_owner.shape, jnp.int32),
            pltpu.VMEM(block_cycle.shape, jnp.int32),
            pltpu.VMEM(block_valid.shape, jnp.int32),
            pltpu.SemaphoreType.DMA((3,)),
        ],
        compiler_params=params,
        name="plan",
    )(cycle_owner, block_cycle, block_valid)
    pool = widen(far, widen(frames))

    def branch(size):
        depth = size * local_frames

        def run(words, scalars, pool):
            got = []
            after = scalars
            for group, (first, end) in enumerate(zip(ends[:-1], ends[1:])):
                members = end - first
                send = pl.pallas_call(
                    functools.partial(pack_kernel, group, first),
                    out_shape=(jax.ShapeDtypeStruct((depth, LANE), jnp.bfloat16),) * members,
                    in_specs=[smem, smem, vmem, pl.BlockSpec(memory_space=pl.ANY)],
                    out_specs=(vmem,) * members,
                    scratch_shapes=[
                        pltpu.VMEM(((tm_count * size + 2) * local_frames, LANE), jnp.float32)
                    ],
                    compiler_params=params,
                    cost_estimate=pl.CostEstimate(
                        flops=2_000_000, bytes_accessed=16_000_000, transcendentals=0
                    ),
                    name="pack",
                )(words, scalars, pool, after)
                for part, apart in zip(send, order[first:end]):
                    pairs = [(i, i ^ apart) for i in range(tm_count)]
                    got.append(lax.ppermute(part, "tm", pairs) if apart else part)
                after = got[first]
            return pl.pallas_call(
                gram_kernel,
                out_shape=jax.ShapeDtypeStruct((frame_count, frame_count), jnp.float32),
                in_specs=[smem] + [vmem] * tm_count,
                out_specs=vmem,
                scratch_shapes=[
                    pltpu.VMEM((frame_count, LANE), jnp.float32),
                    pltpu.VMEM((frame_count, 2 * frame_count), jnp.float32),
                    pltpu.VMEM((frame_count, LANE), jnp.float32),
                ],
                compiler_params=params,
                name="gram",
            )(scalars, *got)

        return run

    return lax.switch(
        scalars[0],
        [branch(size) for size in LADDER],
        words.reshape(-1),
        scalars,
        pool,
    )


def normalize(pixel_intensity, valid_count, lanes):
    lane_index = jnp.arange(lanes, dtype=jnp.int32)
    valid_mask = lane_index[None, :] < valid_count[:, None]
    pixel_mean = jnp.sum(pixel_intensity, axis=0) / pixel_intensity.shape[0]
    guarded_average = jnp.where(valid_mask, pixel_mean, jnp.float32(1.0))
    return jnp.where(valid_mask[None], pixel_intensity / guarded_average[None], jnp.float32(0.0))


def on_device_summed(frames, block_cycle, block_valid, cycle_owner):
    tm_count = lax.axis_size("tm")
    tile_count = lax.axis_size("tile")
    tm_index = lax.axis_index("tm")
    tile_index = lax.axis_index("tile")
    local_frames = frames.shape[0]
    half = frames.shape[1]
    lanes = frames.shape[2]
    cycle_count = cycle_owner.shape[0]
    frame_count = local_frames * tm_count
    cycle_range = jnp.arange(cycle_count, dtype=jnp.int32)
    member_all = (block_cycle[None, :] == cycle_owner[:, None]).astype(jnp.float32)
    pixel_total = jnp.dot(
        member_all, block_valid.astype(jnp.float32), precision=lax.Precision.HIGHEST
    )
    row_count = cycle_count * frame_count // (tm_count * tile_count)
    block_local = half // tm_count
    reshaped = frames.reshape(local_frames, tm_count, block_local, lanes)
    arrived = lax.all_to_all(reshaped, "tm", split_axis=1, concat_axis=0, tiled=True)
    pixel_intensity = arrived.reshape(frame_count, block_local, lanes).astype(jnp.float32)
    offset = (tile_index * tm_count + tm_index) * block_local
    cycle_ids = lax.dynamic_slice_in_dim(block_cycle, offset, block_local, 0)
    valid_count = lax.dynamic_slice_in_dim(block_valid, offset, block_local, 0)
    members = (cycle_ids[None, :] == cycle_owner[:, None]).astype(jnp.float32)
    normalized_frames = normalize(pixel_intensity, valid_count, lanes)
    gram_matrices = jnp.einsum(
        "rnk,jnk->nrj", normalized_frames, normalized_frames, precision=lax.Precision.HIGHEST
    )
    partial_value = jnp.dot(
        members,
        gram_matrices.reshape(block_local, frame_count * frame_count),
        precision=lax.Precision.HIGHEST,
    )
    partial_value = partial_value.reshape(cycle_count * frame_count, frame_count)
    frame_sums = jnp.dot(
        members, jnp.sum(normalized_frames, axis=2).T, precision=lax.Precision.HIGHEST
    )
    owned = lax.psum_scatter(partial_value, ("tm", "tile"), scatter_dimension=0, tiled=True)
    frame_total = lax.psum(frame_sums, ("tm", "tile"))
    row_start = (tm_index * tile_count + tile_index) * row_count
    row_global = row_start + jnp.arange(row_count, dtype=jnp.int32)
    slot_index = row_global // frame_count
    frame_time_index = row_global % frame_count
    select = (slot_index[:, None] == cycle_range[None, :]).astype(jnp.float32)
    row_sums = jnp.dot(select, frame_total, precision=lax.Precision.HIGHEST)
    row_pixels = jnp.dot(select, pixel_total, precision=lax.Precision.HIGHEST)
    time_pick = (
        jnp.arange(frame_count, dtype=jnp.int32)[None, :] == frame_time_index[:, None]
    ).astype(jnp.float32)
    first_sums = jnp.sum(row_sums * time_pick, axis=1)
    return row_pixels[:, None] * owned / (first_sums[:, None] * row_sums)


def solution(mesh):
    in_specs = (P("tm", ("series", "tile"), None), P("series"), P("series"), P())
    out_specs = P(("series", "tm", "tile"), None)

    def on_device(frames, block_cycle, block_valid, cycle_owner):
        routed = (
            mesh.shape["tile"] == 2
            and mesh.shape["tm"] * 2 == cycle_owner.shape[0]
            and frames.shape[0] == 8
            and mesh.shape["tm"] * 8 == LANE
            and block_cycle.shape[0] <= 4096
        )
        body = on_device_routed if routed else on_device_summed
        return body(frames, block_cycle, block_valid, cycle_owner)

    return jax.shard_map(
        on_device, mesh=mesh, in_specs=in_specs, out_specs=out_specs, check_vma=False
    )
```

```python
import functools

import jax
import jax.numpy as jnp
from jax import lax
from jax.experimental import pallas as pl
from jax.experimental.pallas import tpu as pltpu
from jax.sharding import PartitionSpec as P

LANE = 128
UNROLL = 32
FIRST = 5
QUAD = 4
STEP = 384
VMEM_LIMIT = 24 * 1024 * 1024
LADDER = (32, 38, 40, 42, 44, 46, 56, 144)
NT = (((1,), (1,)), ((), ()))


def exchange_order(count):
    side = count // 2
    across = [count - 1 - i for i in range(side)]
    beside = [side - 1 - i for i in range(side)]
    order = across[:3] + beside[:1] + across[3:4]
    for far, near in zip(across[4:], beside[1:]):
        order += [near, far]
    return order + [apart for apart in beside if apart not in order]


def group_ends(count):
    return (0, FIRST, count)


def plan_kernel(
    owner_in, cycle_in, valid_in, word_ref, scalar_ref, owner_ref, cycle_ref, valid_ref, arrived
):
    tm_index, tile_index = lax.axis_index("tm"), lax.axis_index("tile")
    fetches = [
        pltpu.make_async_copy(source, target, arrived.at[i])
        for i, (source, target) in enumerate(
            ((owner_in, owner_ref), (cycle_in, cycle_ref), (valid_in, valid_ref))
        )
    ]
    for fetch in fetches:
        fetch.start()
    for fetch in fetches:
        fetch.wait()
    chunks = cycle_ref.shape[0] // LANE
    slots = owner_ref.shape[0]
    half = cycle_ref.shape[0] // 2
    list_rows = word_ref.shape[0]
    slot = lax.broadcasted_iota(jnp.int32, (slots, LANE), 0)
    mine = (slot % 2 == tile_index).astype(jnp.float32)
    owner = jnp.zeros((slots, LANE), jnp.int32)
    for s in range(slots):
        owner = jnp.where(slot == s, owner_ref[s], owner)

    member, weighted = [], []
    for k in range(chunks):
        cut = slice(k * LANE, (k + 1) * LANE)
        hit = (cycle_ref[cut].reshape(1, LANE) == owner).astype(jnp.float32)
        member.append(hit)
        weighted.append(hit * valid_ref[cut].reshape(1, LANE).astype(jnp.float32))
    stacked = jnp.concatenate(member + weighted, axis=0).astype(jnp.bfloat16)
    before = lax.broadcasted_iota(jnp.int32, (LANE, 2 * LANE), 0)
    column = lax.broadcasted_iota(jnp.int32, (LANE, 2 * LANE), 1)
    prefix = ((before < column) | (column >= LANE)).astype(jnp.float32).astype(jnp.bfloat16)
    sums = jnp.dot(stacked, prefix, preferred_element_type=jnp.float32)

    count = jnp.zeros((slots, LANE), jnp.float32)
    pixels = jnp.zeros((slots, LANE), jnp.float32)
    rank, start = [], []
    for k in range(chunks):
        low = slice(k * slots, (k + 1) * slots)
        high = slice((chunks + k) * slots, (chunks + k + 1) * slots)
        rank.append(count + sums[low, :LANE])
        start.append(pixels + sums[high, :LANE])
        count = count + sums[low, LANE:]
        pixels = pixels + sums[high, LANE:]

    rows = (jnp.max(pixels).astype(jnp.int32) + LANE - 1) // LANE
    rung = jnp.int32(0)
    size = jnp.int32(LADDER[0])
    for smaller, larger in zip(LADDER[:-1], LADDER[1:]):
        rung = rung + (rows > smaller).astype(jnp.int32)
        size = jnp.where(rows > smaller, larger, size)

    def turn_of(index):
        apart = (index // 2) ^ tm_index
        turn = jnp.zeros_like(apart)
        for place, each in enumerate(exchange_order(slots // 2)):
            turn = jnp.where(apart == each, place, turn)
        return turn

    row = turn_of(lax.broadcasted_iota(jnp.int32, (slots, slots), 0))
    index = lax.broadcasted_iota(jnp.int32, (slots, slots), 1)
    earlier = ((turn_of(index) < row) & (index % 2 == tile_index)).astype(jnp.float32)
    turn = turn_of(slot)
    base = jnp.dot(
        earlier, count, precision=lax.Precision.HIGHEST, preferred_element_type=jnp.float32
    )
    begin = (turn * size * LANE).astype(jnp.float32)

    list_row = lax.broadcasted_iota(jnp.int32, (list_rows, LANE), 0)
    list_col = lax.broadcasted_iota(jnp.int32, (LANE, LANE), 0)
    lane = lax.broadcasted_iota(jnp.int32, (1, LANE), 1)
    lists = jnp.zeros((4 * list_rows, LANE), jnp.float32)
    for k in range(chunks):
        own = member[k] * mine
        place = jnp.sum(own * (rank[k] + base), axis=0, keepdims=True).astype(jnp.int32)
        at = jnp.sum(own * (start[k] + begin), axis=0, keepdims=True).astype(jnp.int32)
        used = jnp.sum(own, axis=0, keepdims=True) > 0
        block = k * LANE + lane
        far = (block >= half) != (tile_index == 1)
        block = jnp.where(block >= half, block - half, block) + jnp.where(far, half, 0)
        pixel_count = jnp.sum(own * weighted[k], axis=0, keepdims=True).astype(jnp.int32)
        wraps = at % LANE + pixel_count >= LANE
        word = at * 4096 + block + jnp.where(wraps, jnp.int32(-(2**31)), 0)
        at_row = list_row == jnp.where(used, place // LANE, -1)
        at_col = (list_col == place % LANE).astype(jnp.float32).astype(jnp.bfloat16)
        spread = jnp.concatenate(
            [
                jnp.where(at_row, ((word >> (8 * part)) & 255).astype(jnp.float32), 0.0)
                for part in range(4)
            ],
            axis=0,
        ).astype(jnp.bfloat16)
        lists = lists + lax.dot_general(spread, at_col, NT, preferred_element_type=jnp.float32)
    lists = lists.astype(jnp.int32)
    words = jnp.zeros((list_rows, LANE), jnp.int32)
    for part in range(4):
        words = words + (lists[part * list_rows : (part + 1) * list_rows] << (8 * part))
    index = LANE * lax.broadcasted_iota(jnp.int32, (list_rows, LANE), 0)
    index = index + lax.broadcasted_iota(jnp.int32, (list_rows, LANE), 1)
    total = jnp.sum(count[:, :1] * mine[:, :1]).astype(jnp.int32)
    word_ref[...] = jnp.where(index < total, words, (slots // 2 * size) << 19)

    own_slot = 2 * tm_index + tile_index
    scalar_ref[0] = rung
    scalar_ref[1] = tm_index
    scalar_ref[2] = jnp.sum(jnp.where(slot == own_slot, pixels, 0.0)[:, :1]).astype(jnp.int32)
    for group, end in enumerate(group_ends(slots // 2)):
        ahead = jnp.where(turn < end, count * mine, 0.0)
        scalar_ref[3 + group] = jnp.sum(ahead[:, :1]).astype(jnp.int32)


def widen_kernel(part, in_ref, *rest):
    out_ref = rest[-1]
    frames, half, _ = in_ref.shape
    for f in range(frames):

        def widen(i, _, f=f):
            begin = pl.multiple_of(i * STEP, STEP)
            rows = in_ref[f, pl.ds(begin, STEP), :].astype(jnp.float32)
            out_ref[pl.ds(f * (2 * half + 1) + part * half + begin, STEP), :] = rows
            return 0

        lax.fori_loop(0, half // STEP, widen, 0)


def pack_kernel(group, first, word_ref, scalar_ref, pool_ref, after_ref, *rest):
    out_refs, stage = rest[:-1], rest[-1]
    depth = out_refs[0].shape[0]
    frames = 8
    stride = pool_ref.shape[0] // frames
    lane = lax.broadcasted_iota(jnp.int32, (frames, LANE), 1)
    begin, end = scalar_ref[3 + group], scalar_ref[4 + group]

    def place(i, held):
        at = begin + i * UNROLL
        turned = []
        for j in range(UNROLL):
            word = word_ref[at + j]
            turned.append(pltpu.roll(pool_ref[pl.ds(word & 4095, frames, stride=stride), :], (word >> 12) & (LANE - 1), 1))
        for j in range(UNROLL):
            word = word_ref[at + j]
            shift = (word >> 12) & (LANE - 1)
            row = pl.multiple_of((word >> 16) & 0x7FF8, frames)
            stage[pl.ds(row, frames), :] = jnp.where(lane >= shift, turned[j], held)
            stage[pl.ds(row + frames, frames), :] = turned[j]
            held = jnp.where(lane >= jnp.where(word < 0, 0, shift), turned[j], held)
        return held

    held = jnp.zeros((frames, LANE), jnp.float32)
    lax.fori_loop(0, (end - begin + UNROLL - 1) // UNROLL, place, held)

    step = depth if depth <= 512 else LANE
    for d, out_ref in enumerate(out_refs):
        base = (first + d) * depth

        def narrow(i, _, out_ref=out_ref, base=base):
            row = pl.multiple_of(i * step, step)
            out_ref[pl.ds(row, step), :] = stage[pl.ds(base + row, step), :].astype(jnp.bfloat16)
            return 0

        if step == depth:
            narrow(0, 0)
        else:
            lax.fori_loop(0, depth // step, narrow, 0)


def gram_kernel(scalar_ref, *refs):
    x_refs, (out_ref, turn, grams, totals) = refs[:-4], refs[-4:]
    sources = len(x_refs)
    frames = out_ref.shape[0]
    local = frames // sources
    last = x_refs[0].shape[0] // (2 * local) - 1
    tm_index, pixels = scalar_ref[1], scalar_ref[2]
    lane = lax.broadcasted_iota(jnp.int32, (1, LANE), 1)
    grams[...] = jnp.zeros(grams.shape, jnp.float32)
    totals[...] = jnp.zeros(totals.shape, jnp.float32)

    def several(step, _):
        exact, high, low = [], [], []
        total = totals[...]
        for k in range(QUAD):
            j = QUAD * step + k
            rows = pl.ds(pl.multiple_of(jnp.minimum(j, last) * 2 * local, 2 * local), 2 * local)
            both = [ref[rows, :].astype(jnp.float32) for ref in x_refs]
            for i in range(2):
                used = lane + (2 * j + i) * LANE < pixels
                x = jnp.concatenate([part[i * local : (i + 1) * local] for part in both], axis=0)
                x = jnp.where(used, x, 0.0)
                mean = jnp.where(used, jnp.sum(x, axis=0, keepdims=True) / frames, 1.0)
                scale = 1.0 / mean
                total = total + x * scale
                y = x * (scale * scale)
                top = y.astype(jnp.bfloat16)
                exact.append(x.astype(jnp.bfloat16))
                high.append(top)
                low.append((y - top.astype(jnp.float32)).astype(jnp.bfloat16))
        totals[...] = total
        left = jnp.concatenate(exact, axis=1)
        right = jnp.concatenate(
            [jnp.concatenate(high, axis=1), jnp.concatenate(low, axis=1)], axis=0
        )
        grams[...] += lax.dot_general(left, right, NT, preferred_element_type=jnp.float32)
        return 0

    pairs = (pixels + 2 * LANE - 1) // (2 * LANE)
    lax.fori_loop(0, (pairs + QUAD - 1) // QUAD, several, 0)
    order = exchange_order(sources)

    def in_order(value):
        for j in range(sources):
            at = pl.multiple_of((tm_index ^ order[j]) * local, local)
            turn[pl.ds(at, local), :] = value[j * local : (j + 1) * local]
        return turn[...]

    gram = in_order(grams[:, :frames] + grams[:, frames:])
    gram = in_order(gram.T)
    total = in_order(totals[...])
    first = jnp.sum(total, axis=1, keepdims=True)
    second = jnp.sum(total.T, axis=0, keepdims=True)
    out_ref[...] = pixels.astype(jnp.float32) * gram / (first * second)


def on_device_routed(frames, block_cycle, block_valid, cycle_owner):
    tm_count = lax.axis_size("tm")
    local_frames, half, _ = frames.shape
    frame_count = tm_count * local_frames
    ends = group_ends(tm_count)
    order = exchange_order(tm_count)
    list_rows = -(-(block_cycle.shape[0] + UNROLL) // (8 * LANE)) * 8
    vmem = pl.BlockSpec(memory_space=pltpu.VMEM)
    smem = pl.BlockSpec(memory_space=pltpu.SMEM)
    params = pltpu.CompilerParams(vmem_limit_bytes=VMEM_LIMIT)

    def widen(*given):
        return pl.pallas_call(
            functools.partial(widen_kernel, len(given) - 1),
            out_shape=jax.ShapeDtypeStruct((local_frames * (2 * half + 1), LANE), jnp.float32),
            in_specs=[vmem] * len(given),
            out_specs=vmem,
            input_output_aliases={1: 0} if len(given) > 1 else {},
            compiler_params=params,
            name="widen",
        )(*given)

    far = lax.ppermute(frames, "tile", [(0, 1), (1, 0)])
    words, scalars = pl.pallas_call(
        plan_kernel,
        out_shape=(
            jax.ShapeDtypeStruct((list_rows, LANE), jnp.int32),
            jax.ShapeDtypeStruct((3 + len(ends),), jnp.int32),
        ),
        in_specs=[pl.BlockSpec(memory_space=pltpu.HBM)] * 3,
        out_specs=(vmem, smem),
        scratch_shapes=[
            pltpu.SMEM(cycle_owner.shape, jnp.int32),
            pltpu.VMEM(block_cycle.shape, jnp.int32),
            pltpu.VMEM(block_valid.shape, jnp.int32),
            pltpu.SemaphoreType.DMA((3,)),
        ],
        compiler_params=params,
        name="plan",
    )(cycle_owner, block_cycle, block_valid)
    pool = widen(far, widen(frames))

    def branch(size):
        depth = size * local_frames

        def run(words, scalars, pool):
            got = []
            after = scalars
            for group, (first, end) in enumerate(zip(ends[:-1], ends[1:])):
                members = end - first
                send = pl.pallas_call(
                    functools.partial(pack_kernel, group, first),
                    out_shape=(jax.ShapeDtypeStruct((depth, LANE), jnp.bfloat16),) * members,
                    in_specs=[smem, smem, vmem, pl.BlockSpec(memory_space=pl.ANY)],
                    out_specs=(vmem,) * members,
                    scratch_shapes=[
                        pltpu.VMEM(((tm_count * size + 2) * local_frames, LANE), jnp.float32)
                    ],
                    compiler_params=params,
                    cost_estimate=pl.CostEstimate(
                        flops=2_000_000, bytes_accessed=16_000_000, transcendentals=0
                    ),
                    name="pack",
                )(words, scalars, pool, after)
                for part, apart in zip(send, order[first:end]):
                    pairs = [(i, i ^ apart) for i in range(tm_count)]
                    got.append(lax.ppermute(part, "tm", pairs) if apart else part)
                after = got[first]
            return pl.pallas_call(
                gram_kernel,
                out_shape=jax.ShapeDtypeStruct((frame_count, frame_count), jnp.float32),
                in_specs=[smem] + [vmem] * tm_count,
                out_specs=vmem,
                scratch_shapes=[
                    pltpu.VMEM((frame_count, LANE), jnp.float32),
                    pltpu.VMEM((frame_count, 2 * frame_count), jnp.float32),
                    pltpu.VMEM((frame_count, LANE), jnp.float32),
                ],
                compiler_params=params,
                name="gram",
            )(scalars, *got)

        return run

    return lax.switch(
        scalars[0],
        [branch(size) for size in LADDER],
        words.reshape(-1),
        scalars,
        pool,
    )


def normalize(pixel_intensity, valid_count, lanes):
    lane_index = jnp.arange(lanes, dtype=jnp.int32)
    valid_mask = lane_index[None, :] < valid_count[:, None]
    pixel_mean = jnp.sum(pixel_intensity, axis=0) / pixel_intensity.shape[0]
    guarded_average = jnp.where(valid_mask, pixel_mean, jnp.float32(1.0))
    return jnp.where(valid_mask[None], pixel_intensity / guarded_average[None], jnp.float32(0.0))


def on_device_summed(frames, block_cycle, block_valid, cycle_owner):
    tm_count = lax.axis_size("tm")
    tile_count = lax.axis_size("tile")
    tm_index = lax.axis_index("tm")
    tile_index = lax.axis_index("tile")
    local_frames = frames.shape[0]
    half = frames.shape[1]
    lanes = frames.shape[2]
    cycle_count = cycle_owner.shape[0]
    frame_count = local_frames * tm_count
    cycle_range = jnp.arange(cycle_count, dtype=jnp.int32)
    member_all = (block_cycle[None, :] == cycle_owner[:, None]).astype(jnp.float32)
    pixel_total = jnp.dot(
        member_all, block_valid.astype(jnp.float32), precision=lax.Precision.HIGHEST
    )
    row_count = cycle_count * frame_count // (tm_count * tile_count)
    block_local = half // tm_count
    reshaped = frames.reshape(local_frames, tm_count, block_local, lanes)
    arrived = lax.all_to_all(reshaped, "tm", split_axis=1, concat_axis=0, tiled=True)
    pixel_intensity = arrived.reshape(frame_count, block_local, lanes).astype(jnp.float32)
    offset = (tile_index * tm_count + tm_index) * block_local
    cycle_ids = lax.dynamic_slice_in_dim(block_cycle, offset, block_local, 0)
    valid_count = lax.dynamic_slice_in_dim(block_valid, offset, block_local, 0)
    members = (cycle_ids[None, :] == cycle_owner[:, None]).astype(jnp.float32)
    normalized_frames = normalize(pixel_intensity, valid_count, lanes)
    gram_matrices = jnp.einsum(
        "rnk,jnk->nrj", normalized_frames, normalized_frames, precision=lax.Precision.HIGHEST
    )
    partial_value = jnp.dot(
        members,
        gram_matrices.reshape(block_local, frame_count * frame_count),
        precision=lax.Precision.HIGHEST,
    )
    partial_value = partial_value.reshape(cycle_count * frame_count, frame_count)
    frame_sums = jnp.dot(
        members, jnp.sum(normalized_frames, axis=2).T, precision=lax.Precision.HIGHEST
    )
    owned = lax.psum_scatter(partial_value, ("tm", "tile"), scatter_dimension=0, tiled=True)
    frame_total = lax.psum(frame_sums, ("tm", "tile"))
    row_start = (tm_index * tile_count + tile_index) * row_count
    row_global = row_start + jnp.arange(row_count, dtype=jnp.int32)
    slot_index = row_global // frame_count
    frame_time_index = row_global % frame_count
    select = (slot_index[:, None] == cycle_range[None, :]).astype(jnp.float32)
    row_sums = jnp.dot(select, frame_total, precision=lax.Precision.HIGHEST)
    row_pixels = jnp.dot(select, pixel_total, precision=lax.Precision.HIGHEST)
    time_pick = (
        jnp.arange(frame_count, dtype=jnp.int32)[None, :] == frame_time_index[:, None]
    ).astype(jnp.float32)
    first_sums = jnp.sum(row_sums * time_pick, axis=1)
    return row_pixels[:, None] * owned / (first_sums[:, None] * row_sums)


def solution(mesh):
    in_specs = (P("tm", ("series", "tile"), None), P("series"), P("series"), P())
    out_specs = P(("series", "tm", "tile"), None)

    def on_device(frames, block_cycle, block_valid, cycle_owner):
        routed = (
            mesh.shape["tile"] == 2
            and mesh.shape["tm"] * 2 == cycle_owner.shape[0]
            and frames.shape[0] == 8
            and mesh.shape["tm"] * 8 == LANE
            and block_cycle.shape[0] <= 4096
        )
        body = on_device_routed if routed else on_device_summed
        return body(frames, block_cycle, block_valid, cycle_owner)

    return jax.shard_map(
        on_device, mesh=mesh, in_specs=in_specs, out_specs=out_specs, check_vma=False
    )
```

```python
import functools

import jax
import jax.numpy as jnp
from jax import lax
from jax.experimental import pallas as pl
from jax.experimental.pallas import tpu as pltpu
from jax.sharding import PartitionSpec as P

LANE = 128
UNROLL = 32
FIRST = 4
QUAD = 4
STEP = 384
VMEM_LIMIT = 24 * 1024 * 1024
LADDER = (32, 38, 40, 42, 44, 46, 56, 144)
NT = (((1,), (1,)), ((), ()))


def exchange_order(count):
    side = count // 2
    across = [count - 1 - i for i in range(side)]
    beside = [side - 1 - i for i in range(side)]
    order = across[:3] + beside[:1] + across[3:4]
    for far, near in zip(across[4:], beside[1:]):
        order += [near, far]
    return order + [apart for apart in beside if apart not in order]


def group_ends(count):
    return (0, FIRST, count)


def plan_kernel(
    owner_in, cycle_in, valid_in, word_ref, scalar_ref, owner_ref, cycle_ref, valid_ref, arrived
):
    tm_index, tile_index = lax.axis_index("tm"), lax.axis_index("tile")
    fetches = [
        pltpu.make_async_copy(source, target, arrived.at[i])
        for i, (source, target) in enumerate(
            ((owner_in, owner_ref), (cycle_in, cycle_ref), (valid_in, valid_ref))
        )
    ]
    for fetch in fetches:
        fetch.start()
    for fetch in fetches:
        fetch.wait()
    chunks = cycle_ref.shape[0] // LANE
    slots = owner_ref.shape[0]
    half = cycle_ref.shape[0] // 2
    list_rows = word_ref.shape[0]
    slot = lax.broadcasted_iota(jnp.int32, (slots, LANE), 0)
    mine = (slot % 2 == tile_index).astype(jnp.float32)
    owner = jnp.zeros((slots, LANE), jnp.int32)
    for s in range(slots):
        owner = jnp.where(slot == s, owner_ref[s], owner)

    member, weighted = [], []
    for k in range(chunks):
        cut = slice(k * LANE, (k + 1) * LANE)
        hit = (cycle_ref[cut].reshape(1, LANE) == owner).astype(jnp.float32)
        member.append(hit)
        weighted.append(hit * valid_ref[cut].reshape(1, LANE).astype(jnp.float32))
    stacked = jnp.concatenate(member + weighted, axis=0).astype(jnp.bfloat16)
    before = lax.broadcasted_iota(jnp.int32, (LANE, 2 * LANE), 0)
    column = lax.broadcasted_iota(jnp.int32, (LANE, 2 * LANE), 1)
    prefix = ((before < column) | (column >= LANE)).astype(jnp.float32).astype(jnp.bfloat16)
    sums = jnp.dot(stacked, prefix, preferred_element_type=jnp.float32)

    count = jnp.zeros((slots, LANE), jnp.float32)
    pixels = jnp.zeros((slots, LANE), jnp.float32)
    rank, start = [], []
    for k in range(chunks):
        low = slice(k * slots, (k + 1) * slots)
        high = slice((chunks + k) * slots, (chunks + k + 1) * slots)
        rank.append(count + sums[low, :LANE])
        start.append(pixels + sums[high, :LANE])
        count = count + sums[low, LANE:]
        pixels = pixels + sums[high, LANE:]

    rows = (jnp.max(pixels).astype(jnp.int32) + LANE - 1) // LANE
    rung = jnp.int32(0)
    size = jnp.int32(LADDER[0])
    for smaller, larger in zip(LADDER[:-1], LADDER[1:]):
        rung = rung + (rows > smaller).astype(jnp.int32)
        size = jnp.where(rows > smaller, larger, size)

    def turn_of(index):
        apart = (index // 2) ^ tm_index
        turn = jnp.zeros_like(apart)
        for place, each in enumerate(exchange_order(slots // 2)):
            turn = jnp.where(apart == each, place, turn)
        return turn

    row = turn_of(lax.broadcasted_iota(jnp.int32, (slots, slots), 0))
    index = lax.broadcasted_iota(jnp.int32, (slots, slots), 1)
    earlier = ((turn_of(index) < row) & (index % 2 == tile_index)).astype(jnp.float32)
    turn = turn_of(slot)
    base = jnp.dot(
        earlier, count, precision=lax.Precision.HIGHEST, preferred_element_type=jnp.float32
    )
    begin = (turn * size * LANE).astype(jnp.float32)

    list_row = lax.broadcasted_iota(jnp.int32, (list_rows, LANE), 0)
    list_col = lax.broadcasted_iota(jnp.int32, (LANE, LANE), 0)
    lane = lax.broadcasted_iota(jnp.int32, (1, LANE), 1)
    lists = jnp.zeros((4 * list_rows, LANE), jnp.float32)
    for k in range(chunks):
        own = member[k] * mine
        place = jnp.sum(own * (rank[k] + base), axis=0, keepdims=True).astype(jnp.int32)
        at = jnp.sum(own * (start[k] + begin), axis=0, keepdims=True).astype(jnp.int32)
        used = jnp.sum(own, axis=0, keepdims=True) > 0
        block = k * LANE + lane
        far = (block >= half) != (tile_index == 1)
        block = jnp.where(block >= half, block - half, block) + jnp.where(far, half, 0)
        pixel_count = jnp.sum(own * weighted[k], axis=0, keepdims=True).astype(jnp.int32)
        wraps = at % LANE + pixel_count >= LANE
        word = at * 4096 + block + jnp.where(wraps, jnp.int32(-(2**31)), 0)
        at_row = list_row == jnp.where(used, place // LANE, -1)
        at_col = (list_col == place % LANE).astype(jnp.float32).astype(jnp.bfloat16)
        spread = jnp.concatenate(
            [
                jnp.where(at_row, ((word >> (8 * part)) & 255).astype(jnp.float32), 0.0)
                for part in range(4)
            ],
            axis=0,
        ).astype(jnp.bfloat16)
        lists = lists + lax.dot_general(spread, at_col, NT, preferred_element_type=jnp.float32)
    lists = lists.astype(jnp.int32)
    words = jnp.zeros((list_rows, LANE), jnp.int32)
    for part in range(4):
        words = words + (lists[part * list_rows : (part + 1) * list_rows] << (8 * part))
    index = LANE * lax.broadcasted_iota(jnp.int32, (list_rows, LANE), 0)
    index = index + lax.broadcasted_iota(jnp.int32, (list_rows, LANE), 1)
    total = jnp.sum(count[:, :1] * mine[:, :1]).astype(jnp.int32)
    word_ref[...] = jnp.where(index < total, words, (slots // 2 * size) << 19)

    own_slot = 2 * tm_index + tile_index
    scalar_ref[0] = rung
    scalar_ref[1] = tm_index
    scalar_ref[2] = jnp.sum(jnp.where(slot == own_slot, pixels, 0.0)[:, :1]).astype(jnp.int32)
    for group, end in enumerate(group_ends(slots // 2)):
        ahead = jnp.where(turn < end, count * mine, 0.0)
        scalar_ref[3 + group] = jnp.sum(ahead[:, :1]).astype(jnp.int32)


def widen_kernel(part, in_ref, *rest):
    out_ref = rest[-1]
    frames, half, _ = in_ref.shape
    for f in range(frames):

        def widen(i, _, f=f):
            begin = pl.multiple_of(i * STEP, STEP)
            rows = in_ref[f, pl.ds(begin, STEP), :].astype(jnp.float32)
            out_ref[pl.ds(f * (2 * half + 1) + part * half + begin, STEP), :] = rows
            return 0

        lax.fori_loop(0, half // STEP, widen, 0)


def pack_kernel(group, first, word_ref, scalar_ref, pool_ref, after_ref, *rest):
    out_refs, stage = rest[:-1], rest[-1]
    depth = out_refs[0].shape[0]
    frames = 8
    stride = pool_ref.shape[0] // frames
    lane = lax.broadcasted_iota(jnp.int32, (frames, LANE), 1)
    begin, end = scalar_ref[3 + group], scalar_ref[4 + group]

    def place(i, held):
        at = begin + i * UNROLL
        turned = []
        for j in range(UNROLL):
            word = word_ref[at + j]
            turned.append(pltpu.roll(pool_ref[pl.ds(word & 4095, frames, stride=stride), :], (word >> 12) & (LANE - 1), 1))
        for j in range(UNROLL):
            word = word_ref[at + j]
            shift = (word >> 12) & (LANE - 1)
            row = pl.multiple_of((word >> 16) & 0x7FF8, frames)
            stage[pl.ds(row, frames), :] = jnp.where(lane >= shift, turned[j], held)
            stage[pl.ds(row + frames, frames), :] = turned[j]
            held = jnp.where(lane >= jnp.where(word < 0, 0, shift), turned[j], held)
        return held

    held = jnp.zeros((frames, LANE), jnp.float32)
    lax.fori_loop(0, (end - begin + UNROLL - 1) // UNROLL, place, held)

    step = depth if depth <= 512 else LANE
    for d, out_ref in enumerate(out_refs):
        base = (first + d) * depth

        def narrow(i, _, out_ref=out_ref, base=base):
            row = pl.multiple_of(i * step, step)
            out_ref[pl.ds(row, step), :] = stage[pl.ds(base + row, step), :].astype(jnp.bfloat16)
            return 0

        if step == depth:
            narrow(0, 0)
        else:
            lax.fori_loop(0, depth // step, narrow, 0)


def gram_kernel(scalar_ref, *refs):
    x_refs, (out_ref, turn, grams, totals) = refs[:-4], refs[-4:]
    sources = len(x_refs)
    frames = out_ref.shape[0]
    local = frames // sources
    last = x_refs[0].shape[0] // (2 * local) - 1
    tm_index, pixels = scalar_ref[1], scalar_ref[2]
    lane = lax.broadcasted_iota(jnp.int32, (1, LANE), 1)
    grams[...] = jnp.zeros(grams.shape, jnp.float32)
    totals[...] = jnp.zeros(totals.shape, jnp.float32)

    def several(step, _):
        exact, high, low = [], [], []
        total = totals[...]
        for k in range(QUAD):
            j = QUAD * step + k
            rows = pl.ds(pl.multiple_of(jnp.minimum(j, last) * 2 * local, 2 * local), 2 * local)
            both = [ref[rows, :].astype(jnp.float32) for ref in x_refs]
            for i in range(2):
                used = lane + (2 * j + i) * LANE < pixels
                x = jnp.concatenate([part[i * local : (i + 1) * local] for part in both], axis=0)
                x = jnp.where(used, x, 0.0)
                mean = jnp.where(used, jnp.sum(x, axis=0, keepdims=True) / frames, 1.0)
                scale = 1.0 / mean
                total = total + x * scale
                y = x * (scale * scale)
                top = y.astype(jnp.bfloat16)
                exact.append(x.astype(jnp.bfloat16))
                high.append(top)
                low.append((y - top.astype(jnp.float32)).astype(jnp.bfloat16))
        totals[...] = total
        left = jnp.concatenate(exact, axis=1)
        right = jnp.concatenate(
            [jnp.concatenate(high, axis=1), jnp.concatenate(low, axis=1)], axis=0
        )
        grams[...] += lax.dot_general(left, right, NT, preferred_element_type=jnp.float32)
        return 0

    pairs = (pixels + 2 * LANE - 1) // (2 * LANE)
    lax.fori_loop(0, (pairs + QUAD - 1) // QUAD, several, 0)
    order = exchange_order(sources)

    def in_order(value):
        for j in range(sources):
            at = pl.multiple_of((tm_index ^ order[j]) * local, local)
            turn[pl.ds(at, local), :] = value[j * local : (j + 1) * local]
        return turn[...]

    gram = in_order(grams[:, :frames] + grams[:, frames:])
    gram = in_order(gram.T)
    total = in_order(totals[...])
    first = jnp.sum(total, axis=1, keepdims=True)
    second = jnp.sum(total.T, axis=0, keepdims=True)
    out_ref[...] = pixels.astype(jnp.float32) * gram / (first * second)


def on_device_routed(frames, block_cycle, block_valid, cycle_owner):
    tm_count = lax.axis_size("tm")
    local_frames, half, _ = frames.shape
    frame_count = tm_count * local_frames
    ends = group_ends(tm_count)
    order = exchange_order(tm_count)
    list_rows = -(-(block_cycle.shape[0] + UNROLL) // (8 * LANE)) * 8
    vmem = pl.BlockSpec(memory_space=pltpu.VMEM)
    smem = pl.BlockSpec(memory_space=pltpu.SMEM)
    params = pltpu.CompilerParams(vmem_limit_bytes=VMEM_LIMIT)

    def widen(*given):
        return pl.pallas_call(
            functools.partial(widen_kernel, len(given) - 1),
            out_shape=jax.ShapeDtypeStruct((local_frames * (2 * half + 1), LANE), jnp.float32),
            in_specs=[vmem] * len(given),
            out_specs=vmem,
            input_output_aliases={1: 0} if len(given) > 1 else {},
            compiler_params=params,
            name="widen",
        )(*given)

    far = lax.ppermute(frames, "tile", [(0, 1), (1, 0)])
    words, scalars = pl.pallas_call(
        plan_kernel,
        out_shape=(
            jax.ShapeDtypeStruct((list_rows, LANE), jnp.int32),
            jax.ShapeDtypeStruct((3 + len(ends),), jnp.int32),
        ),
        in_specs=[pl.BlockSpec(memory_space=pltpu.HBM)] * 3,
        out_specs=(vmem, smem),
        scratch_shapes=[
            pltpu.SMEM(cycle_owner.shape, jnp.int32),
            pltpu.VMEM(block_cycle.shape, jnp.int32),
            pltpu.VMEM(block_valid.shape, jnp.int32),
            pltpu.SemaphoreType.DMA((3,)),
        ],
        compiler_params=params,
        name="plan",
    )(cycle_owner, block_cycle, block_valid)
    pool = widen(far, widen(frames))

    def branch(size):
        depth = size * local_frames

        def run(words, scalars, pool):
            got = []
            after = scalars
            for group, (first, end) in enumerate(zip(ends[:-1], ends[1:])):
                members = end - first
                send = pl.pallas_call(
                    functools.partial(pack_kernel, group, first),
                    out_shape=(jax.ShapeDtypeStruct((depth, LANE), jnp.bfloat16),) * members,
                    in_specs=[smem, smem, vmem, pl.BlockSpec(memory_space=pl.ANY)],
                    out_specs=(vmem,) * members,
                    scratch_shapes=[
                        pltpu.VMEM(((tm_count * size + 2) * local_frames, LANE), jnp.float32)
                    ],
                    compiler_params=params,
                    cost_estimate=pl.CostEstimate(
                        flops=2_000_000, bytes_accessed=16_000_000, transcendentals=0
                    ),
                    name="pack",
                )(words, scalars, pool, after)
                for part, apart in zip(send, order[first:end]):
                    pairs = [(i, i ^ apart) for i in range(tm_count)]
                    got.append(lax.ppermute(part, "tm", pairs) if apart else part)
                after = got[first]
            return pl.pallas_call(
                gram_kernel,
                out_shape=jax.ShapeDtypeStruct((frame_count, frame_count), jnp.float32),
                in_specs=[smem] + [vmem] * tm_count,
                out_specs=vmem,
                scratch_shapes=[
                    pltpu.VMEM((frame_count, LANE), jnp.float32),
                    pltpu.VMEM((frame_count, 2 * frame_count), jnp.float32),
                    pltpu.VMEM((frame_count, LANE), jnp.float32),
                ],
                compiler_params=params,
                name="gram",
            )(scalars, *got)

        return run

    return lax.switch(
        scalars[0],
        [branch(size) for size in LADDER],
        words.reshape(-1),
        scalars,
        pool,
    )


def normalize(pixel_intensity, valid_count, lanes):
    lane_index = jnp.arange(lanes, dtype=jnp.int32)
    valid_mask = lane_index[None, :] < valid_count[:, None]
    pixel_mean = jnp.sum(pixel_intensity, axis=0) / pixel_intensity.shape[0]
    guarded_average = jnp.where(valid_mask, pixel_mean, jnp.float32(1.0))
    return jnp.where(valid_mask[None], pixel_intensity / guarded_average[None], jnp.float32(0.0))


def on_device_summed(frames, block_cycle, block_valid, cycle_owner):
    tm_count = lax.axis_size("tm")
    tile_count = lax.axis_size("tile")
    tm_index = lax.axis_index("tm")
    tile_index = lax.axis_index("tile")
    local_frames = frames.shape[0]
    half = frames.shape[1]
    lanes = frames.shape[2]
    cycle_count = cycle_owner.shape[0]
    frame_count = local_frames * tm_count
    cycle_range = jnp.arange(cycle_count, dtype=jnp.int32)
    member_all = (block_cycle[None, :] == cycle_owner[:, None]).astype(jnp.float32)
    pixel_total = jnp.dot(
        member_all, block_valid.astype(jnp.float32), precision=lax.Precision.HIGHEST
    )
    row_count = cycle_count * frame_count // (tm_count * tile_count)
    block_local = half // tm_count
    reshaped = frames.reshape(local_frames, tm_count, block_local, lanes)
    arrived = lax.all_to_all(reshaped, "tm", split_axis=1, concat_axis=0, tiled=True)
    pixel_intensity = arrived.reshape(frame_count, block_local, lanes).astype(jnp.float32)
    offset = (tile_index * tm_count + tm_index) * block_local
    cycle_ids = lax.dynamic_slice_in_dim(block_cycle, offset, block_local, 0)
    valid_count = lax.dynamic_slice_in_dim(block_valid, offset, block_local, 0)
    members = (cycle_ids[None, :] == cycle_owner[:, None]).astype(jnp.float32)
    normalized_frames = normalize(pixel_intensity, valid_count, lanes)
    gram_matrices = jnp.einsum(
        "rnk,jnk->nrj", normalized_frames, normalized_frames, precision=lax.Precision.HIGHEST
    )
    partial_value = jnp.dot(
        members,
        gram_matrices.reshape(block_local, frame_count * frame_count),
        precision=lax.Precision.HIGHEST,
    )
    partial_value = partial_value.reshape(cycle_count * frame_count, frame_count)
    frame_sums = jnp.dot(
        members, jnp.sum(normalized_frames, axis=2).T, precision=lax.Precision.HIGHEST
    )
    owned = lax.psum_scatter(partial_value, ("tm", "tile"), scatter_dimension=0, tiled=True)
    frame_total = lax.psum(frame_sums, ("tm", "tile"))
    row_start = (tm_index * tile_count + tile_index) * row_count
    row_global = row_start + jnp.arange(row_count, dtype=jnp.int32)
    slot_index = row_global // frame_count
    frame_time_index = row_global % frame_count
    select = (slot_index[:, None] == cycle_range[None, :]).astype(jnp.float32)
    row_sums = jnp.dot(select, frame_total, precision=lax.Precision.HIGHEST)
    row_pixels = jnp.dot(select, pixel_total, precision=lax.Precision.HIGHEST)
    time_pick = (
        jnp.arange(frame_count, dtype=jnp.int32)[None, :] == frame_time_index[:, None]
    ).astype(jnp.float32)
    first_sums = jnp.sum(row_sums * time_pick, axis=1)
    return row_pixels[:, None] * owned / (first_sums[:, None] * row_sums)


def solution(mesh):
    in_specs = (P("tm", ("series", "tile"), None), P("series"), P("series"), P())
    out_specs = P(("series", "tm", "tile"), None)

    def on_device(frames, block_cycle, block_valid, cycle_owner):
        routed = (
            mesh.shape["tile"] == 2
            and mesh.shape["tm"] * 2 == cycle_owner.shape[0]
            and frames.shape[0] == 8
            and mesh.shape["tm"] * 8 == LANE
            and block_cycle.shape[0] <= 4096
        )
        body = on_device_routed if routed else on_device_summed
        return body(frames, block_cycle, block_valid, cycle_owner)

    return jax.shard_map(
        on_device, mesh=mesh, in_specs=in_specs, out_specs=out_specs, check_vma=False
    )
```
